32 devices in a mesh: batch: 16 (over z, y, core), blk: 2 (over x).
Axes of the slice: x: 2, y: 2, z: 4, core: 2. Of those that a mesh axis runs over, the one named last changes fastest.
Arguments:
- frames: bfloat16 [16, 1024, 768], P('batch', 'blk'), may hold values from -6 to 6
- cotangent: bfloat16 [16, 1024, 768], P('batch', 'blk'), may hold values from -6 to 6
- query_weight: bfloat16 [768, 768], replicated, may hold values from -0.21875 to 0.21875
- key_weight: bfloat16 [768, 768], replicated, may hold values from -0.21875 to 0.21875
- value_weight: bfloat16 [768, 768], replicated, may hold values from -0.21875 to 0.21875
- output_weight: bfloat16 [768, 768], replicated, may hold values from -0.875 to 0.875
- up_weight: bfloat16 [768, 3072], replicated, may hold values from -0.21875 to 0.21875
- down_weight: bfloat16 [3072, 768], replicated, may hold values from -0.109375 to 0.109375
- attn_gain: float32 [768], replicated, may hold values from 0.25 to 1.75
- attn_shift: float32 [768], replicated, may hold values from -1.5 to 1.5
- query_bias: float32 [768], replicated, may hold values from -2.5 to 2.5
- value_bias: float32 [768], replicated, may hold values from -2.5 to 2.5
- output_bias: float32 [768], replicated, may hold values from -2.5 to 2.5
- ffn_gain: float32 [768], replicated, may hold values from 0.25 to 1.75
- ffn_shift: float32 [768], replicated, may hold values from -1.5 to 1.5
- up_bias: float32 [3072], replicated, may hold values from -2.5 to 2.5
- down_bias: float32 [768], replicated, may hold values from -2.5 to 2.5
- rel_table: float32 [320, 12], replicated, may hold values from -5 to 5
- utt_lengths: int32 [16, 8], P('batch'), may hold values from 1 to 1000, 1024 in all within a row
- frame_mask: int32 [16, 1024], P('batch', 'blk'), may hold values 0 or 1
- rel_bucket: int32 [2047], replicated, may hold values from 0 to 319, as said below
Outputs:
- mixed_out: bfloat16 [16, 1024, 768], P('batch', 'blk')
- frames_grad: float32 [16, 1024, 768], P('batch', 'blk')
- query_weight_grad: float32 [768, 768], replicated
- key_weight_grad: float32 [768, 768], replicated
- value_weight_grad: float32 [768, 768], replicated
- output_weight_grad: float32 [768, 768], replicated
- up_weight_grad: float32 [768, 3072], replicated
- down_weight_grad: float32 [3072, 768], replicated
- attn_gain_grad: float32 [768], replicated
- attn_shift_grad: float32 [768], replicated
- query_bias_grad: float32 [768], replicated
- value_bias_grad: float32 [768], replicated
- output_bias_grad: float32 [768], replicated
- ffn_gain_grad: float32 [768], replicated
- ffn_shift_grad: float32 [768], replicated
- up_bias_grad: float32 [3072], replicated
- down_bias_grad: float32 [768], replicated
- rel_table_grad: float32 [320, 12], replicated
The draws below stay inside these ranges and needn't reach their ends.
Inputs may be any that keep to these rules, and one draw needn't show every extreme that they name: `utt_lengths`: the 8 lengths of each row add up to 1024, and each row has one utterance of exactly 1000 frames. rel_bucket[r + 1023] is the bucket of relative position r (query minus key); it never falls as r rises, equals 160 at r = 0 and reaches 0 and 319.
All inputs are finite; a program needn't handle non-finite values. No bound on the sum of `frame_mask` on one device may be relied on, other than what follows from the above.
Results may differ from the reference program's by a relative error of at most 0.013.
Values may be sent and summed in bfloat16 or wider, within the bound.
No kernel may reach another device: no remote copies, remote signals or barrier semaphores. Data moves between devices by JAX's collectives and lax.ppermute only.
A program may use at most 256 MiB of HBM per device.

```python
import math
import jax
import jax.numpy as jnp
import numpy as np
from jax import lax

D = 768
H = 12
HD = 64
FF = 3072
NB = 320
SEQ = 1024
UTTS = 8
ROWS = 16
MOST = 1000


def draw_rel_bucket(key, part):
    key = jax.random.fold_in(key, 11)
    strides = jax.random.randint(key, (2 * SEQ - 2,), 1, 3, dtype=jnp.int32)
    rising = jnp.concatenate([jnp.zeros((1,), jnp.int32), jnp.cumsum(strides).astype(jnp.int32)])
    centred = rising - rising[SEQ - 1] + NB // 2
    return jnp.clip(centred, 0, NB - 1).astype(jnp.int32)


def set_ends(drawn, own_key, low, top_value):
    longest = drawn.shape.index(max(drawn.shape))
    spots = []
    for shift in (0, 1):
        where = [jax.random.randint(jax.random.fold_in(own_key, axis), (), 0, length) for axis, length in enumerate(drawn.shape)]
        where[longest] = (where[longest] + shift) % drawn.shape[longest]
        spots.append(tuple(where))
    return drawn.at[spots[0]].set(low).at[spots[1]].set(top_value)


def steps_of(key, extent, split, smallest, top_value):
    level, own = 1.0, jax.random.fold_in(key, 6)
    for dim, blocks in split:
        heights = jnp.exp(jax.random.uniform(jax.random.fold_in(own, dim), (blocks,), jnp.float32, smallest / len(split), top_value / len(split)))
        level = level * jnp.repeat(heights, extent[dim] // blocks).reshape([-1 if axis == dim else 1 for axis in range(len(extent))])
    return level


def split_up(amount, total, most, slope):
    loads = [(1 << 20) // math.isqrt(grade ** slope) + 1 for grade in range(2, amount + 1)]
    rest, given = total - most - (amount - 1), [1] * (amount - 1)
    while rest > 0:
        candidates = [i for i in range(amount - 1) if given[i] < most]
        pool, budget = sum([loads[i] for i in candidates]), rest
        for i in candidates:
            addition = min(most - given[i], max(1, budget * loads[i] // pool), rest)
            given[i] = given[i] + addition
            rest = rest - addition
    return np.array([most] + given)


def ragged_sizes(own_key, amount, total, most, skew):
    if amount == 2:
        one = jax.random.randint(own_key, (), max(1, total - most), min(most, total - 1) + 1)
        return jnp.stack([one, total - one])
    lengths = jnp.asarray(split_up(amount, total, most, skew), jnp.int32)
    couples = (amount - 1) // 2
    source_of, receiver = lengths[1:1 + 2 * couples:2], lengths[2:2 + 2 * couples:2]
    slack = jnp.minimum(source_of - 1, most - receiver)
    shifted = jax.random.randint(jax.random.fold_in(own_key, 1), (couples,), 0, 1 << 20) % (slack + 1)
    lengths = lengths.at[1:1 + 2 * couples:2].set(source_of - shifted).at[2:2 + 2 * couples:2].set(receiver + shifted)
    return lengths[jax.random.permutation(jax.random.fold_in(own_key, 2), amount)]


def normal_values(own_key, shape, scale, most, shards=(), kind=jnp.bfloat16):
    level = steps_of(own_key, shape, shards, -0.22, 0.18) if shards else 1.0
    values = jax.random.normal(own_key, shape, jnp.float32) * scale * level
    return jnp.minimum(jnp.maximum(values, -most), most).astype(kind)


def setup_inputs(seed: int = 0) -> dict:
    key_list = jax.random.split(jax.random.key(seed), 22)
    frames = normal_values(key_list[0], (ROWS, SEQ, D), 1.0, 6.0, ((0, 16), (1, 2)))
    cotangent = normal_values(key_list[1], (ROWS, SEQ, D), 1.0, 6.0, ((0, 16), (1, 2)))
    query_weight = normal_values(key_list[2], (D, D), D ** -0.5, 0.21875)
    key_weight = normal_values(key_list[3], (D, D), D ** -0.5, 0.21875)
    value_weight = normal_values(key_list[4], (D, D), D ** -0.5, 0.21875)
    output_weight = normal_values(key_list[5], (D, D), (D // 16) ** -0.5, 0.875)
    up_weight = normal_values(key_list[6], (D, FF), D ** -0.5, 0.21875)
    down_weight = normal_values(key_list[7], (FF, D), FF ** -0.5, 0.109375)
    attn_gain = jnp.clip(1.0 + 0.15 * jax.random.normal(key_list[8], (D,), jnp.float32), 0.25, 1.75)
    attn_shift = normal_values(key_list[9], (D,), 0.3, 1.5, (), jnp.float32)
    query_bias = normal_values(key_list[10], (D,), 0.5, 2.5, (), jnp.float32)
    value_bias = normal_values(key_list[11], (D,), 0.5, 2.5, (), jnp.float32)
    output_bias = normal_values(key_list[12], (D,), 0.5, 2.5, (), jnp.float32)
    ffn_gain = jnp.clip(1.0 + 0.15 * jax.random.normal(key_list[13], (D,), jnp.float32), 0.25, 1.75)
    ffn_shift = normal_values(key_list[14], (D,), 0.3, 1.5, (), jnp.float32)
    up_bias = normal_values(key_list[15], (FF,), 0.5, 2.5, (), jnp.float32)
    down_bias = normal_values(key_list[16], (D,), 0.5, 2.5, (), jnp.float32)
    rel_table = normal_values(key_list[17], (NB, H), 1.0, 5.0, (), jnp.float32)
    utt_lengths = jax.vmap(lambda own: ragged_sizes(own, UTTS, SEQ, MOST, 2))(jax.random.split(key_list[18], ROWS)).reshape((ROWS, UTTS)).astype(jnp.int32)
    frame_mask = set_ends((jax.random.randint(key_list[19], (ROWS, SEQ), 0, 8) < 7).astype(jnp.int32), jax.random.fold_in(key_list[19], 1), 0, 1)
    rel_bucket = draw_rel_bucket(jax.random.fold_in(key_list[21], 71), 0)
    return dict(frames=frames, cotangent=cotangent, query_weight=query_weight, key_weight=key_weight, value_weight=value_weight, output_weight=output_weight, up_weight=up_weight, down_weight=down_weight, attn_gain=attn_gain, attn_shift=attn_shift, query_bias=query_bias, value_bias=value_bias, output_bias=output_bias, ffn_gain=ffn_gain, ffn_shift=ffn_shift, up_bias=up_bias, down_bias=down_bias, rel_table=rel_table, utt_lengths=utt_lengths, frame_mask=frame_mask, rel_bucket=rel_bucket)


HIGHEST_PRECISION = lax.Precision.HIGHEST
EPSILON = 1e-05
MASKED_SCORE = -1e+30

@jax.custom_vjp
def low(v):
    return lax.optimization_barrier(v.astype(jnp.bfloat16)).astype(jnp.float32)

@jax.custom_vjp
def low_back(v):
    return v

def low_keep(v):
    return (low(v), None)

def low_pass(kept, grad):
    return (grad,)

def back_keep(v):
    return (v, None)

def back_low(kept, grad):
    return (low(grad),)
low.defvjp(low_keep, low_pass)
low_back.defvjp(back_keep, back_low)

def layer_norm(values, gain_vec, shift_vec):
    centre = values - lax.optimization_barrier(jnp.mean(values, axis=-1, keepdims=True))
    spread = lax.optimization_barrier(jnp.mean(centre * centre, axis=-1, keepdims=True))
    return centre * lax.rsqrt(spread + EPSILON) * gain_vec + shift_vec

def matmul(left, right):
    return jnp.dot(left, right, precision=HIGHEST_PRECISION)

def add_pair(first_term, second_term):
    return first_term + second_term

def encoder_layer(param_set, frames_f, allowed, pair_bucket):
    query_weight, key_weight, value_weight, output_weight, up_weight, down_weight, attn_gain, attn_shift, query_bias, value_bias, output_bias, ffn_gain, ffn_shift, up_bias, down_bias, rel_table = param_set
    group_rows, length, model_width = frames_f.shape
    normed = low(layer_norm(frames_f, attn_gain, attn_shift))
    query_heads = low(low_back((matmul(normed, query_weight) + query_bias) * 0.125)).reshape(group_rows, length, H, HD)
    key_heads = low(low_back(matmul(normed, key_weight))).reshape(group_rows, length, H, HD)
    value_heads = low(low_back(matmul(normed, value_weight) + value_bias)).reshape(group_rows, length, H, HD)
    bias_pairs = jnp.take(rel_table, pair_bucket, axis=0)
    scores = jnp.einsum('gihd,gjhd->ghij', query_heads, key_heads, precision=HIGHEST_PRECISION)
    scores = low_back(scores + jnp.transpose(bias_pairs, (2, 0, 1))[None])
    scores = jnp.where(allowed[:, None], scores, MASKED_SCORE)
    attn_probs = jax.nn.softmax(scores, axis=-1)
    attended = jnp.einsum('ghij,gjhd->gihd', attn_probs, value_heads, precision=HIGHEST_PRECISION)
    context = low(low_back(attended)).reshape(group_rows, length, model_width)
    branch = low_back(matmul(context, output_weight) + output_bias)
    residual = frames_f + branch
    hidden = low(layer_norm(residual, ffn_gain, ffn_shift))
    pre_act = low_back(matmul(hidden, up_weight) + up_bias)
    gelu_out = low(jax.nn.gelu(pre_act, approximate=False))
    return residual + low_back(matmul(gelu_out, down_weight) + down_bias)

def reference(frames, cotangent, query_weight, key_weight, value_weight, output_weight, up_weight, down_weight, attn_gain, attn_shift, query_bias, value_bias, output_bias, ffn_gain, ffn_shift, up_bias, down_bias, rel_table, utt_lengths, frame_mask, rel_bucket):
    row_count = frames.shape[0]
    positions = jnp.arange(SEQ, dtype=jnp.int32)
    utt_ends = jnp.cumsum(utt_lengths, axis=1).astype(jnp.int32)
    segment = lax.optimization_barrier(jnp.sum((utt_ends[:, None, :] <= positions[None, :, None]).astype(jnp.int32), axis=-1))
    pair_bucket = rel_bucket[(positions[:, None] - positions[None, :] + SEQ - 1).astype(jnp.int32)]
    on_diagonal = positions[:, None] == positions[None, :]
    params = tuple((weight.astype(jnp.float32) for weight in (query_weight, key_weight, value_weight, output_weight, up_weight, down_weight, attn_gain, attn_shift, query_bias, value_bias, output_bias, ffn_gain, ffn_shift, up_bias, down_bias, rel_table)))
    group_rows = 2 if row_count % 2 == 0 else 1
    slab_count = row_count // group_rows

    def regroup(array):
        return array.reshape((slab_count, group_rows) + array.shape[1:])

    def one_group(totals, slab):
        frames_g, cot_g, segment_g, mask_g = slab
        allowed = (segment_g[:, :, None] == segment_g[:, None, :]) & ((mask_g[:, None, :] == 1) | on_diagonal[None])

        def layer_run(param_set, frames_in):
            return encoder_layer(param_set, frames_in, allowed, pair_bucket)
        output, pullback = jax.vjp(layer_run, params, frames_g.astype(jnp.float32))
        param_grads, frames_grad = pullback(cot_g.astype(jnp.float32))
        totals = jax.tree.map(add_pair, totals, param_grads)
        return (totals, (output.astype(jnp.bfloat16), frames_grad))
    zeros_init = jax.tree.map(jnp.zeros_like, params)
    totals, outputs = lax.scan(one_group, zeros_init, (regroup(frames), regroup(cotangent), regroup(segment), regroup(frame_mask)))
    mixed_out = outputs[0].reshape(frames.shape)
    frames_grad = outputs[1].reshape(frames.shape)
    grad_query, grad_key, grad_value, grad_output, grad_up, grad_down, grad_attn_gain, grad_attn_shift, grad_query_bias, grad_value_bias, grad_output_bias, grad_ffn_gain, grad_ffn_shift, grad_up_bias, grad_down_bias, grad_table = totals
    return (mixed_out, frames_grad, grad_query, grad_key, grad_value, grad_output, grad_up, grad_down, grad_attn_gain, grad_attn_shift, grad_query_bias, grad_value_bias, grad_output_bias, grad_ffn_gain, grad_ffn_shift, grad_up_bias, grad_down_bias, grad_table)
```

```python
import functools

import jax
import jax.numpy as jnp
from jax import lax
from jax.experimental import pallas as pl
from jax.experimental.pallas import tpu as pltpu
from jax.sharding import PartitionSpec as P

HD = 64
LANES = 128
EPSILON = 1e-05
MASKED = -1e30
BF16 = jnp.bfloat16
F32 = jnp.float32
VMEM_LIMIT = 56 * 1024 * 1024
HIGHEST = lax.Precision.HIGHEST


def dot_nn(a, b):
    return lax.dot_general(a, b, (((1,), (0,)), ((), ())), preferred_element_type=F32)


def dot_nt(a, b):
    return lax.dot_general(a, b, (((1,), (1,)), ((), ())), preferred_element_type=F32)


def dot_tn(a, b):
    return lax.dot_general(a, b, (((0,), (0,)), ((), ())), preferred_element_type=F32)


def normalise(values):
    centre = values - jnp.mean(values, axis=-1, keepdims=True)
    scale = lax.rsqrt(jnp.mean(centre * centre, axis=-1, keepdims=True) + EPSILON)
    return centre * scale, scale


def column_sum(values):
    return jnp.sum(values, axis=0, keepdims=True)


def call(kernel, out_shape, flops, nbytes, transcendentals=0, **kw):
    return pl.pallas_call(
        kernel,
        out_shape=out_shape,
        compiler_params=pltpu.CompilerParams(vmem_limit_bytes=VMEM_LIMIT),
        cost_estimate=pl.CostEstimate(
            flops=flops, bytes_accessed=nbytes, transcendentals=transcendentals
        ),
        **kw,
    )


def shaped(shape, dtype):
    return jax.ShapeDtypeStruct(shape, dtype)


def project_kernel(with_query, *refs):
    if with_query:
        x_ref, g_ref, s_ref, wq_ref, wk_ref, wv_ref, bq_ref, bv_ref = refs[:8]
        n_ref, q_ref, k_ref, v_ref, norm = refs[8:]
    else:
        x_ref, g_ref, s_ref, wk_ref, wv_ref, bv_ref = refs[:6]
        n_ref, k_ref, v_ref, norm = refs[6:]

    @pl.when(pl.program_id(0) == 0)
    def _():
        y, _ = normalise(x_ref[...].astype(F32))
        norm[...] = (y * g_ref[...] + s_ref[...]).astype(BF16)
        n_ref[...] = norm[...]

    x = norm[...]
    if with_query:
        q_ref[...] = ((dot_nn(x, wq_ref[...]) + bq_ref[...]) * 0.125).astype(BF16)
    k_ref[...] = dot_nn(x, wk_ref[...]).astype(BF16)
    v_ref[...] = (dot_nn(x, wv_ref[...]) + bv_ref[...]).astype(BF16)


def project(x, gain, shift, weights, biases):
    rows, width = x.shape
    cols = 256
    with_query = len(weights) == 3
    whole = pl.BlockSpec((rows, width), lambda j: (0, 0))
    vec = pl.BlockSpec((1, width), lambda j: (0, 0))
    part = pl.BlockSpec((width, cols), lambda j: (0, j))
    bias = pl.BlockSpec((1, cols), lambda j: (0, j))
    out = pl.BlockSpec((rows, cols), lambda j: (0, j))
    count = len(weights)
    return call(
        functools.partial(project_kernel, with_query),
        [shaped((rows, width), BF16)] * (count + 1),
        2 * rows * width * width * count,
        2 * width * (rows * (count + 2) + width * count),
        grid=(width // cols,),
        in_specs=[whole, vec, vec] + [part] * count + [bias] * len(biases),
        out_specs=[whole] + [out] * count,
        scratch_shapes=[pltpu.VMEM((rows, width), BF16)],
    )(x, gain, shift, *weights, *biases)


def attend_kernel(own, last, chunk, *refs):
    refs = list(refs)
    q_ref, k_ref, v_ref, qf_ref, kf_ref, w_ref = refs[:6]
    refs = refs[6:]
    if not own:
        o_in, m_in, l_in = refs[:3]
        refs = refs[3:]
    if last:
        p_ref, m_ref, at_ref, cx_ref, lse_ref, t_ref = refs
    elif own:
        p_ref, m_ref, o_ref, l_ref, t_ref = refs
    else:
        p_ref, m_ref, o_ref, l_ref, run_ref, t_ref = refs
    length = q_ref.shape[1]
    nb = length // LANES
    q = q_ref[0]
    k = k_ref[0]
    v = v_ref[0]
    lane = lax.broadcasted_iota(jnp.int32, (length, LANES), 1)
    low = lane < HD
    k_wide = jnp.concatenate([k, kf_ref[0]], axis=1)
    v_wide = jnp.concatenate([v, jnp.ones((length, LANES), BF16)], axis=1)
    eye = lax.broadcasted_iota(jnp.int32, (LANES, LANES), 0) == lax.broadcasted_iota(
        jnp.int32, (LANES, LANES), 1
    )
    zero = jnp.zeros((), BF16)
    heads = []
    for h in range(2):
        for a in range(2 * nb - 1):
            x = w_ref[0, h : h + 1, 2 * length - 256 - 128 * a : 2 * length - 128 * a]
            t = pltpu.roll(jnp.broadcast_to(x, (LANES, 256)), 0, 1, stride=1, stride_axis=0)
            t_ref[128 * a : 128 * a + 128, :] = t[:, LANES:]
        q_head = jnp.where(low if h == 0 else ~low, q, zero)
        q_wide = jnp.concatenate([q_head, qf_ref[0]], axis=1)
        sums = []
        for c in range(0, length, chunk):
            s = dot_nt(q_wide[c : c + chunk], k_wide)
            tiles = []
            for j in range(nb):
                u = c - 128 * j + 128 * (nb - 1)
                tile = s[:, 128 * j : 128 * j + 128] + t_ref[u : u + chunk, :]
                if own and c <= 128 * j < c + chunk:
                    r = 128 * j - c
                    here = slice(128 * j, 128 * j + 128)
                    plain = dot_nt(q_head[here], k[here]) + t_ref[128 * (nb - 1) : 128 * nb, :]
                    fixed = jnp.where(eye, plain, tile[r : r + 128])
                    around = [tile[:r], fixed, tile[r + 128 :]]
                    tile = jnp.concatenate([x for x in around if x.shape[0]], axis=0)
                tiles.append(tile)
            top = jnp.max(functools.reduce(jnp.maximum, tiles), axis=1, keepdims=True)
            p = jnp.concatenate([jnp.exp(tile - top).astype(BF16) for tile in tiles], axis=1)
            p_ref[0, h, c : c + chunk, :] = p
            o = dot_nn(p, v_wide)
            sums.append((o[:, :LANES], o[:, LANES:], jnp.broadcast_to(top, (chunk, LANES))))
        heads.append([jnp.concatenate(part, axis=0) for part in zip(*sums)])
    o, l, m = [jnp.where(low, first, second) for first, second in zip(*heads)]
    m_ref[0] = m
    if not own:
        m_old = m_in[0]
        m_new = jnp.maximum(m_old, m)
        old, new = jnp.exp(m_old - m_new), jnp.exp(m - m_new)
        o = o_in[0] * old + o * new
        l = l_in[0] * old + l * new
        m = m_new
    if last:
        attended = o / l
        at_ref[0] = attended
        cx_ref[0] = attended.astype(BF16)
        lse_ref[0] = m + jnp.log(l)
    else:
        o_ref[0] = o
        l_ref[0] = l
        if not own:
            run_ref[0] = m


def attend(q, k, v, qf, kf, window, state, last, chunk=256):
    rows, length, width = q.shape
    pairs, nb = width // LANES, length // LANES
    own = state is None
    blk = pl.BlockSpec((1, length, LANES), lambda p, r: (r, 0, p))
    feat = pl.BlockSpec((1, length, LANES), lambda p, r: (r, 0, 0))
    probs = pl.BlockSpec((1, 2, length, length), lambda p, r: (r, p, 0, 0))
    arrays = [q, k, v, qf, kf, window] + ([] if own else list(state))
    specs = [blk] * 3 + [feat] * 2 + [pl.BlockSpec((1, 2, 2 * length), lambda p, r: (p, 0, 0))]
    specs += [] if own else [blk] * 3
    kinds = [F32, F32, BF16, F32] if last else [F32] * (3 if own else 4)
    pair_count = rows * 2 * pairs * length * length
    return call(
        functools.partial(attend_kernel, own, last, min(chunk, length)),
        [shaped((rows, 2 * pairs, length, length), BF16)]
        + [shaped((rows, length, width), kind) for kind in kinds],
        8 * pair_count * HD,
        2 * pair_count,
        pair_count,
        grid=(pairs, rows),
        in_specs=specs,
        out_specs=[probs] + [blk] * len(kinds),
        scratch_shapes=[pltpu.VMEM(((2 * nb - 1) * LANES, LANES), F32)],
    )(*arrays)


def attend_back_kernel(first, *refs):
    refs = list(refs)
    p_ref, q_ref, k_ref, v_ref, dc_ref, at_ref, lse_ref, m_ref, ones_ref = refs[:9]
    refs = refs[9:]
    if not first:
        dq_in = refs.pop(0)
    dq_ref, dk_ref, dv_ref, w_ref, ds_ref = refs
    length = q_ref.shape[1]
    nb = length // LANES
    q, k, v = q_ref[0], k_ref[0], v_ref[0]
    lane = lax.broadcasted_iota(jnp.int32, (length, LANES), 1)
    lane8 = lax.broadcasted_iota(jnp.int32, (8, LANES), 1)
    low = lane < HD
    in_head = lane & (HD - 1)
    zero = jnp.zeros((), BF16)
    factor = jnp.exp(m_ref[0] - lse_ref[0])
    scaled = dc_ref[0] * factor
    do = scaled.astype(BF16)
    product = scaled * at_ref[0]
    product_hi = product.astype(BF16)
    product_lo = (product - product_hi.astype(F32)).astype(BF16)
    row_dot = dot_nn(product_hi, ones_ref[...]) + dot_nn(product_lo, ones_ref[...])
    dot_hi = row_dot.astype(BF16)
    dot_lo = (row_dot - dot_hi.astype(F32)).astype(BF16)
    feat = jnp.where(in_head == 0, dot_hi, jnp.where(in_head == 1, dot_lo, zero))
    v_wide = jnp.concatenate([v, jnp.where(in_head < 2, -1.0, 0.0).astype(BF16)], axis=1)
    row = pl.program_id(1)
    parts = []
    for h in range(2):
        mine = low if h == 0 else ~low
        do_wide = jnp.concatenate([jnp.where(mine, do, zero), jnp.where(mine, feat, zero)], axis=1)
        p = p_ref[0, h]
        ds = (p.astype(F32) * dot_nt(do_wide, v_wide)).astype(BF16)
        ds_ref[...] = ds
        parts.append((dot_nn(ds, k), dot_tn(ds, q), dot_tn(p, do)))
        tops, lows = [], []
        for a in range(2 * nb - 1):
            total = None
            for j in range(nb):
                i0 = 128 * (a - (nb - 1) + j)
                if 0 <= i0 < length:
                    x = ds_ref[i0 : i0 + 128, 128 * j : 128 * j + 128].astype(F32)
                    total = x if total is None else total + x
            whole, top = total[:8], total[:8]
            for g in range(1, 16):
                x = pltpu.roll(total[8 * g : 8 * g + 8], 128 - 8 * g, 1)
                whole = whole + x
                top = top + jnp.where(lane8 < 128 - 8 * g, x, 0.0)
            tops.append(top)
            lows.append(whole - top)
        pieces = []
        for g in range(2 * nb):
            a = 2 * nb - 1 - g
            if a == 2 * nb - 1:
                pieces.append(lows[a - 1])
            elif a == 0:
                pieces.append(tops[a])
            else:
                pieces.append(tops[a] + lows[a - 1])
        z = jnp.concatenate(pieces, axis=1)
        sub = lax.broadcasted_iota(jnp.int32, z.shape, 0)
        for bit in (1, 2, 4):
            z = jnp.where((sub & bit) != 0, pltpu.roll(z, 2 * length - bit, 1), z)
        diagonal = column_sum(z)

        @pl.when(row == 0)
        def _():
            w_ref[0, h : h + 1, :] = diagonal

        @pl.when(row != 0)
        def _():
            w_ref[0, h : h + 1, :] += diagonal

    dq, dk, dv = [jnp.where(low, one, two) for one, two in zip(*parts)]
    if not first:
        dq = dq + dq_in[0]
    dq_ref[0] = dq.astype(dq_ref.dtype)
    dk_ref[0] = dk.astype(BF16)
    dv_ref[0] = dv.astype(BF16)


def attend_back(p, q, k, v, dctx, attended, lse, m, ones, dq, last):
    rows, length, width = q.shape
    pairs = width // LANES
    first = dq is None
    blk = pl.BlockSpec((1, length, LANES), lambda p, r: (r, 0, p))
    probs = pl.BlockSpec((1, 2, length, length), lambda p, r: (r, p, 0, 0))
    window = pl.BlockSpec((1, 2, 2 * length), lambda p, r: (p, 0, 0))
    arrays = [p, q, k, v, dctx, attended, lse, m, ones] + ([] if first else [dq])
    specs = [probs] + [blk] * 7 + [pl.BlockSpec((LANES, LANES), lambda p, r: (0, 0))]
    specs += [] if first else [blk]
    pair_count = rows * 2 * pairs * length * length
    kinds = [BF16 if last else F32, BF16, BF16]
    return call(
        functools.partial(attend_back_kernel, first),
        [shaped((rows, length, width), kind) for kind in kinds]
        + [shaped((pairs, 2, 2 * length), F32)],
        16 * pair_count * HD,
        2 * pair_count,
        grid=(pairs, rows),
        in_specs=specs,
        out_specs=[blk] * 3 + [window],
        scratch_shapes=[pltpu.VMEM((length, length), BF16)],
    )(*arrays)


def ffn_step(j, core, hid, cot, up_ref, down_ref, bias_ref, down_acc, hid_acc, grads_ref, bias_grad):
    up = up_ref[...]
    down = down_ref[...]
    pre = dot_nn(hid, up) + bias_ref[0]
    cdf = 0.5 + 0.5 * lax.erf(pre * 0.7071067811865476)
    slope = cdf + pre * (0.3989422804014327 * jnp.exp(-0.5 * pre * pre))
    act = (pre * cdf).astype(BF16)
    pre_grad = (dot_nt(cot, down) * slope).astype(BF16)
    down_acc[...] += dot_nn(act, down)
    hid_acc[...] += dot_nt(pre_grad, up)
    grads_ref[core, 0] = dot_tn(hid, pre_grad).astype(BF16)
    grads_ref[1 - core, 0] = dot_tn(act, cot).astype(BF16)
    bias_grad[0] = column_sum(pre_grad.astype(F32))


def ffn_head_kernel(
    core_ref, ctx_ref, x_ref, cot_ref, wo_ref, bo_ref, g_ref, s_ref, up_ref, down_ref, bias_ref,
    res_ref, hid_ref, down_acc, hid_acc, grads_ref, bias_grad,
):
    j = pl.program_id(0)

    @pl.when(j == 0)
    def _():
        res = x_ref[...].astype(F32) + (dot_nn(ctx_ref[...], wo_ref[...]) + bo_ref[...])
        res_ref[...] = res
        y, _ = normalise(res)
        hid_ref[...] = (y * g_ref[...] + s_ref[...]).astype(BF16)
        down_acc[...] = jnp.zeros_like(down_acc)
        hid_acc[...] = jnp.zeros_like(hid_acc)

    ffn_step(
        j, core_ref[0], hid_ref[...], cot_ref[...], up_ref, down_ref, bias_ref,
        down_acc, hid_acc, grads_ref, bias_grad,
    )


def ffn_tail_kernel(
    core_ref, ctx_ref, cot_ref, wo_ref, g_ref, bd_ref, res_ref, hid_ref, down_in, hid_in,
    up_ref, down_ref, bias_ref,
    mixed_ref, dres_ref, dctx_ref, dwo_ref, vec_ref, grads_ref, bias_grad, down_acc, hid_acc,
):
    j = pl.program_id(0)

    @pl.when(j == 0)
    def _():
        down_acc[...] = down_in[...]
        hid_acc[...] = hid_in[...]

    ffn_step(
        j, core_ref[0], hid_ref[...], cot_ref[...], up_ref, down_ref, bias_ref,
        down_acc, hid_acc, grads_ref, bias_grad,
    )

    @pl.when(j == pl.num_programs(0) - 1)
    def _():
        res = res_ref[...]
        cot = cot_ref[...].astype(F32)
        mixed_ref[...] = (res + (down_acc[...] + bd_ref[...])).astype(BF16)
        y, scale = normalise(res)
        dh = hid_acc[...]
        a = dh * g_ref[...]
        dres = cot + scale * (
            a - jnp.mean(a, axis=-1, keepdims=True) - y * jnp.mean(a * y, axis=-1, keepdims=True)
        )
        dres_ref[...] = dres
        branch = dres.astype(BF16)
        dctx_ref[...] = dot_nt(branch, wo_ref[...])
        dwo_ref[...] = dot_tn(ctx_ref[...], branch).astype(BF16)
        vec_ref[0:1] = column_sum(dh * y)
        vec_ref[1:2] = column_sum(dh)
        vec_ref[2:3] = column_sum(branch.astype(F32))
        vec_ref[3:4] = column_sum(cot)


def ffn_specs(rows, width, start):
    whole = pl.BlockSpec((rows, width), lambda j: (0, 0), pipeline_mode=pl.Buffered(1))
    square = pl.BlockSpec((width, width), lambda j: (0, 0), pipeline_mode=pl.Buffered(1))
    vec = pl.BlockSpec((1, width), lambda j: (0, 0))
    up = pl.BlockSpec((width, width), lambda j: (0, j + start))
    down = pl.BlockSpec((width, width), lambda j: (j + start, 0))
    bias = pl.BlockSpec((1, 1, width), lambda j: (j + start, 0, 0))
    grads = pl.BlockSpec((2, 1, width, width), lambda j: (0, j, 0, 0))
    bias_grad = pl.BlockSpec((1, 1, width), lambda j: (j, 0, 0))
    return whole, square, vec, up, down, bias, grads, bias_grad


SMEM = pl.BlockSpec(memory_space=pltpu.SMEM)


def ffn_head(core, ctx, x, cot, wo, bo, gain, shift, up, down, bias, steps):
    rows, width = x.shape
    whole, square, vec, up_s, down_s, bias_s, grads, bias_grad = ffn_specs(rows, width, 0)
    return call(
        ffn_head_kernel,
        [
            shaped((rows, width), F32),
            shaped((rows, width), BF16),
            shaped((rows, width), F32),
            shaped((rows, width), F32),
            shaped((2, steps, width, width), BF16),
            shaped((steps, 1, width), F32),
        ],
        2 * rows * width * width * (6 * steps + 1),
        8 * steps * width * width + 18 * rows * width,
        grid=(steps,),
        in_specs=[SMEM, whole, whole, whole, square, vec, vec, vec, up_s, down_s, bias_s],
        out_specs=[whole, whole, whole, whole, grads, bias_grad],
    )(core, ctx, x, cot, wo, bo, gain, shift, up, down, bias)


def ffn_tail(core, ctx, cot, wo, gain, bd, res, hid, down_acc, hid_acc, up, down, bias, start, steps):
    rows, width = cot.shape
    whole, square, vec, up_s, down_s, bias_s, grads, bias_grad = ffn_specs(rows, width, start)
    vecs = pl.BlockSpec((8, width), lambda j: (0, 0))
    return call(
        ffn_tail_kernel,
        [
            shaped((rows, width), BF16),
            shaped((rows, width), F32),
            shaped((rows, width), F32),
            shaped((width, width), BF16),
            shaped((8, width), F32),
            shaped((2, steps, width, width), BF16),
            shaped((steps, 1, width), F32),
        ],
        2 * rows * width * width * (6 * steps + 2),
        8 * steps * width * width + 24 * rows * width,
        grid=(steps,),
        in_specs=[SMEM, whole, whole, square, vec, vec]
        + [whole] * 4
        + [up_s, down_s, bias_s],
        out_specs=[whole, whole, whole, square, vecs, grads, bias_grad],
        scratch_shapes=[pltpu.VMEM((rows, width), F32)] * 2,
    )(core, ctx, cot, wo, gain, bd, res, hid, down_acc, hid_acc, up, down, bias)


def peer_back_kernel(first, *refs):
    refs = list(refs)
    x_ref, n_ref, dk_ref, dv_ref, wk_ref, wv_ref = refs[:6]
    refs = refs[6:]
    if not first:
        wk_in, wv_in, vec_in = refs[:3]
        refs = refs[3:]
    ng_ref, gk_ref, gv_ref, vec_ref = refs
    dk, dv, norm = dk_ref[...], dv_ref[...], n_ref[...]
    ng = dot_nt(dk, wk_ref[...]) + dot_nt(dv, wv_ref[...])
    ng_ref[...] = ng.astype(BF16)
    gk, gv = dot_tn(norm, dk), dot_tn(norm, dv)
    y, _ = normalise(x_ref[...].astype(F32))
    vecs = [column_sum(ng * y), column_sum(ng), column_sum(dv.astype(F32))]
    if not first:
        gk, gv = gk + wk_in[...], gv + wv_in[...]
        vecs = [vec + vec_in[i : i + 1] for i, vec in enumerate(vecs)]
    gk_ref[...] = gk
    gv_ref[...] = gv
    for i, vec in enumerate(vecs):
        vec_ref[i : i + 1] = vec


def peer_back(x, norm, dk, dv, wk, wv, state):
    rows, width = x.shape
    first = state is None
    return call(
        functools.partial(peer_back_kernel, first),
        [
            shaped((rows, width), BF16),
            shaped((width, width), F32),
            shaped((width, width), F32),
            shaped((8, width), F32),
        ],
        8 * rows * width * width,
        10 * rows * width + 12 * width * width,
    )(x, norm, dk, dv, wk, wv, *([] if first else state))


def own_back_kernel(alone, *refs):
    refs = list(refs)
    core_ref, x_ref, n_ref, dq_ref, dk_ref, dv_ref, wq_ref, wk_ref, wv_ref, wo_ref = refs[:10]
    refs = refs[10:]
    if not alone:
        gk_in, gv_in, vec_in = refs[:3]
        refs = refs[3:]
    ng_ref, grads_ref, vec_ref = refs
    core = core_ref[0]
    dq, dk, dv, norm = dq_ref[...], dk_ref[...], dv_ref[...], n_ref[...]
    gk, gv = dot_tn(norm, dk), dot_tn(norm, dv)
    if not alone:
        gk, gv = gk + gk_in[...], gv + gv_in[...]
    grads_ref[core, 0] = (0.125 * dot_tn(norm, dq)).astype(BF16)
    grads_ref[core, 1] = gk.astype(BF16)
    grads_ref[1 - core, 0] = gv.astype(BF16)
    grads_ref[1 - core, 1] = wo_ref[...]
    ng = 0.125 * dot_nt(dq, wq_ref[...]) + dot_nt(dk, wk_ref[...]) + dot_nt(dv, wv_ref[...])
    ng_ref[...] = ng
    y, _ = normalise(x_ref[...].astype(F32))
    vecs = [column_sum(ng * y), column_sum(ng), column_sum(dv.astype(F32))]
    if not alone:
        vecs = [vec + vec_in[i : i + 1] for i, vec in enumerate(vecs)]
    vecs.append(0.125 * column_sum(dq.astype(F32)))
    for i, vec in enumerate(vecs):
        vec_ref[i : i + 1] = vec


def own_back(core, x, norm, dq, dk, dv, wq, wk, wv, dwo, state):
    rows, width = x.shape
    alone = state is None
    arrays = [core, x, norm, dq, dk, dv, wq, wk, wv, dwo] + ([] if alone else list(state))
    return call(
        functools.partial(own_back_kernel, alone),
        [
            shaped((rows, width), F32),
            shaped((2, 2, width, width), BF16),
            shaped((8, width), F32),
        ],
        12 * rows * width * width,
        14 * rows * width + 24 * width * width,
        in_specs=[SMEM] + [pl.BlockSpec(memory_space=pltpu.VMEM)] * (len(arrays) - 1),
    )(*arrays)


def frames_back_kernel(count, *refs):
    x_ref, g_ref, dres_ref, ng_ref = refs[:4]
    out_ref = refs[-1]
    y, scale = normalise(x_ref[...].astype(F32))
    ng = ng_ref[...]
    for other in refs[4 : 4 + count]:
        ng = ng + other[...].astype(F32)
    a = ng * g_ref[...]
    out_ref[...] = dres_ref[...] + scale * (
        a - jnp.mean(a, axis=-1, keepdims=True) - y * jnp.mean(a * y, axis=-1, keepdims=True)
    )


def frames_back(x, gain, dres, ng, others):
    rows, width = x.shape
    tile = 128
    blk = pl.BlockSpec((tile, width), lambda i: (i, 0))
    vec = pl.BlockSpec((1, width), lambda i: (0, 0))
    return call(
        functools.partial(frames_back_kernel, len(others)),
        shaped((rows, width), F32),
        30 * rows * width,
        14 * rows * width,
        grid=(rows // tile,),
        in_specs=[blk, vec, blk, blk] + [blk] * len(others),
        out_specs=blk,
    )(x, gain, dres, ng, *others)


def swap(x, bit):
    axis, k = bit
    size = lax.axis_size(axis)
    return lax.ppermute(x, axis, [(i, i ^ (1 << k)) for i in range(size)])


def bit_of(bit):
    axis, k = bit
    return (lax.axis_index(axis) >> k) & 1


def halve(x, bit):
    half = x.shape[-2] // 2
    mine = bit_of(bit) * half
    keep = lax.dynamic_slice_in_dim(x, mine, half, x.ndim - 2)
    send = lax.dynamic_slice_in_dim(x, half - mine, half, x.ndim - 2)
    return keep, send


def plus(a, b):
    return (a.astype(F32) + b.astype(F32)).astype(BF16)


def reduce_step(x, bit):
    keep, send = halve(x, bit)
    return plus(keep, swap(send, bit))


def gather_step(x, bit):
    other = swap(x, bit)
    first = bit_of(bit) == 0
    return jnp.concatenate([jnp.where(first, x, other), jnp.where(first, other, x)], axis=-2)


def mesh_bits():
    across = [("blk", k) for k in range(lax.axis_size("blk").bit_length() - 1)]
    batch = [("batch", k) for k in range(lax.axis_size("batch").bit_length() - 1)]
    return batch[0], across, batch[1:2], batch[2:]


def all_reduce(grads):
    core, across, along, rest = mesh_bits()
    held = plus(grads[0], swap(grads[1], core))
    one, two = held[0], held[1]
    for bit in across + along:
        one = reduce_step(one, bit)
    for bit in along + across:
        two = reduce_step(two, bit)
    both = jnp.stack([one, two])
    for bit in rest:
        both = reduce_step(both, bit)
    for bit in rest[::-1]:
        both = gather_step(both, bit)
    one, two = both[0], both[1]
    for bit in (across + along)[::-1]:
        one = gather_step(one, bit)
    for bit in (along + across)[::-1]:
        two = gather_step(two, bit)
    held = jnp.stack([one, two])
    other = swap(held, core)
    first = bit_of(core) == 0
    return jnp.where(first, held, other), jnp.where(first, other, held)


def all_reduce_small(x):
    core, across, along, rest = mesh_bits()
    for bit in [core] + across + along + rest:
        x = x + swap(x, bit)
    return x


def per_device(
    frames,
    cotangent,
    query_weight,
    key_weight,
    value_weight,
    output_weight,
    up_weight,
    down_weight,
    attn_gain,
    attn_shift,
    query_bias,
    value_bias,
    output_bias,
    ffn_gain,
    ffn_shift,
    up_bias,
    down_bias,
    rel_table,
    utt_lengths,
    frame_mask,
    rel_bucket,
):
    rows_n, length, width = frames.shape
    blocks = lax.axis_size("blk")
    seq = length * blocks
    me = lax.axis_index("blk")
    rows = rows_n * length
    units = up_weight.shape[1]
    steps = units // width
    heads = rel_table.shape[1]
    buckets = rel_table.shape[0]
    core = (lax.axis_index("batch") & 1).astype(jnp.int32).reshape(1)

    def from_peer(x, b):
        return lax.ppermute(x, "blk", [((i + b) % blocks, i) for i in range(blocks)])

    def to_peer(x, b):
        return lax.ppermute(x, "blk", [(i, (i + b) % blocks) for i in range(blocks)])

    flat_frames = frames.reshape(rows, width)
    x_blocks = [flat_frames] + [from_peer(flat_frames, b) for b in range(1, blocks)]
    masks = [frame_mask] + [from_peer(frame_mask, b) for b in range(1, blocks)]
    starts = [((me + b) % blocks) * length for b in range(blocks)]

    ends = jnp.cumsum(utt_lengths, axis=1)
    begins = ends - utt_lengths
    spare = LANES - utt_lengths.shape[1]

    def in_segment(start):
        pos = (start + jnp.arange(length, dtype=jnp.int32))[None, :, None]
        return (begins[:, None, :] <= pos) & (pos < ends[:, None, :])

    def widen(x):
        return jnp.pad(x.astype(BF16), ((0, 0), (0, 0), (0, spare)))

    query_feat = widen(in_segment(starts[0]))
    key_feats = [
        widen(jnp.where(in_segment(start) & (mask == 1)[..., None], 0.0, MASKED))
        for start, mask in zip(starts, masks)
    ]

    bucket_of = jnp.concatenate([jnp.full((1,), -1, jnp.int32), rel_bucket[::-1]])
    one_hot = (jnp.arange(buckets, dtype=jnp.int32)[:, None] == bucket_of[None, :]).astype(F32)
    bias_rel = jnp.dot(rel_table.T, one_hot, precision=HIGHEST)
    offsets = [seq - length + start - starts[0] for start in starts]
    windows = [
        lax.dynamic_slice_in_dim(bias_rel, offset, 2 * length, 1).reshape(
            heads // 2, 2, 2 * length
        )
        for offset in offsets
    ]

    gain = attn_gain.reshape(1, width)
    shift = attn_shift.reshape(1, width)
    q_bias = query_bias.reshape(1, width)
    v_bias = value_bias.reshape(1, width)
    ffn_g = ffn_gain.reshape(1, width)

    def split(x):
        return x.reshape(rows_n, length, width)

    def flat(x):
        return x.reshape(rows, width)

    norm, query, key, value = project(
        flat_frames, gain, shift, (query_weight, key_weight, value_weight), (q_bias, v_bias)
    )
    norms, keys, values = [norm], [key], [value]
    query = split(query)
    probs, tops = [], []
    state = None
    for b in range(blocks):
        last = b == blocks - 1
        if b:
            norm, key, value = project(
                x_blocks[b], gain, shift, (key_weight, value_weight), (v_bias,)
            )
            norms.append(norm)
            keys.append(key)
            values.append(value)
        p, m, *rest = attend(
            query, split(keys[b]), split(values[b]), query_feat, key_feats[b], windows[b], state, last
        )
        probs.append(p)
        tops.append(m)
        if last:
            attended, context, lse = rest
        else:
            o, l, *run = rest
            state = (o, run[0] if run else m, l)

    half = steps // 2
    context = flat(context)
    cot = cotangent.reshape(rows, width)
    bias3 = up_bias.reshape(steps, 1, width)
    res, hid, down_acc, hid_acc, grads_a, up_bias_a = ffn_head(
        core, context, flat_frames, cot, output_weight, output_bias.reshape(1, width), ffn_g,
        ffn_shift.reshape(1, width), up_weight, down_weight, bias3, half,
    )
    mixed, dres, dctx, dwo, vec_ffn, grads_b, up_bias_b = ffn_tail(
        core, context, cot, output_weight, ffn_g, down_bias.reshape(1, width), res, hid,
        down_acc, hid_acc, up_weight, down_weight, bias3, half, steps - half,
    )
    up_a, down_a = all_reduce(grads_a)
    up_b, down_b = all_reduce(grads_b)

    index = jnp.arange(LANES, dtype=jnp.int32) // HD
    ones = (index[:, None] == index[None, :]).astype(BF16)
    dq = None
    state = None
    sent = []
    rel_grad = jnp.zeros((heads, 2 * seq), F32)
    for b in list(range(1, blocks)) + [0]:
        dq, dk, dv, w = attend_back(
            probs[b], query, split(keys[b]), split(values[b]), split(dctx), attended, lse,
            tops[b], ones, dq, b == 0,
        )
        w = w.reshape(heads, 2 * length)
        present = lax.dynamic_slice_in_dim(rel_grad, offsets[b], 2 * length, 1)
        rel_grad = lax.dynamic_update_slice_in_dim(rel_grad, present + w, offsets[b], 1)
        if b:
            ng, *state = peer_back(
                x_blocks[b], norms[b], flat(dk), flat(dv), key_weight, value_weight, state
            )
            sent.append(to_peer(ng, b))
        else:
            ng, grads_c, vec_attn = own_back(
                core, flat_frames, norms[0], flat(dq), flat(dk), flat(dv), query_weight,
                key_weight, value_weight, dwo, state,
            )
    frames_grad = frames_back(flat_frames, gain, dres, ng, sent)
    query_key, value_output = all_reduce(grads_c)

    table_grad = jnp.dot(one_hot, rel_grad.T, precision=HIGHEST)
    small = jnp.concatenate(
        [vec_attn[:4], vec_ffn[:4], up_bias_a[:, 0], up_bias_b[:, 0]]
        + [table_grad.reshape(-1, width)]
    )
    total = all_reduce_small(small)
    table_total = total[8 + steps :].reshape(rel_table.shape)
    up_total = jnp.concatenate([up_a, up_b])
    return (
        mixed.reshape(frames.shape),
        frames_grad.reshape(frames.shape),
        query_key[0].astype(F32),
        query_key[1].astype(F32),
        value_output[0].astype(F32),
        value_output[1].astype(F32),
        jnp.concatenate([up_total[i] for i in range(steps)], axis=1).astype(F32),
        jnp.concatenate([down_a, down_b]).reshape(units, width).astype(F32),
        total[0],
        total[1],
        total[3],
        total[2],
        total[6],
        total[4],
        total[5],
        total[8 : 8 + steps].reshape(units),
        total[7],
        table_total,
    )


def solution(mesh):
    batch3 = P("batch", "blk", None)
    in_specs = (batch3, batch3) + (P(),) * 16 + (P("batch", None), P("batch", "blk"), P())
    out_specs = (batch3, batch3) + (P(),) * 16
    return jax.shard_map(
        per_device, mesh=mesh, in_specs=in_specs, out_specs=out_specs, check_vma=False
    )
```

```python
import functools

import jax
import jax.numpy as jnp
from jax import lax
from jax.experimental import pallas as pl
from jax.experimental.pallas import tpu as pltpu
from jax.sharding import PartitionSpec as P

HD = 64
LANES = 128
EPSILON = 1e-05
MASKED = -1e30
BF16 = jnp.bfloat16
F32 = jnp.float32
COST = 12
HIGHEST = lax.Precision.HIGHEST


def dot_nn(a, b):
    return lax.dot_general(a, b, (((1,), (0,)), ((), ())), preferred_element_type=F32)


def dot_nt(a, b):
    return lax.dot_general(a, b, (((1,), (1,)), ((), ())), preferred_element_type=F32)


def dot_tn(a, b):
    return lax.dot_general(a, b, (((0,), (0,)), ((), ())), preferred_element_type=F32)


def normalise(values):
    centre = values - jnp.mean(values, axis=-1, keepdims=True)
    scale = lax.rsqrt(jnp.mean(centre * centre, axis=-1, keepdims=True) + EPSILON)
    return centre * scale, scale


def column_sum(values):
    return jnp.sum(values, axis=0, keepdims=True)


def cost_of(time):
    return pl.CostEstimate(
        flops=int(time * COST * 1.1e9), bytes_accessed=int(time * COST * 3e6), transcendentals=0
    )


def call(kernel, out_shape, time, after=(), vmem=32, **kw):
    skip = len(after)

    def run(*refs):
        kernel(*refs[skip:])

    kw["in_specs"] = [pl.BlockSpec(memory_space=pl.ANY)] * skip + list(kw["in_specs"])
    program = pl.pallas_call(
        run,
        out_shape=out_shape,
        compiler_params=pltpu.CompilerParams(vmem_limit_bytes=vmem * 1024 * 1024),
        cost_estimate=cost_of(time),
        **kw,
    )
    return lambda *arrays: program(*after, *arrays)


SMEM = pl.BlockSpec(memory_space=pltpu.SMEM)
IN_VMEM = pl.BlockSpec(memory_space=pltpu.VMEM)


def shaped(shape, dtype):
    return jax.ShapeDtypeStruct(shape, dtype)


ATTN_GAIN, ATTN_SHIFT, Q_BIAS, V_BIAS, O_BIAS, FFN_GAIN, FFN_SHIFT, DOWN_BIAS = range(8)


def vector(ref, index):
    return ref[index : index + 1, :]


def store_pairs(ref, values):
    for p in range(values.shape[1] // LANES):
        ref[p] = values[:, p * LANES : (p + 1) * LANES].astype(ref.dtype)


def all_pairs(refs):
    return jnp.concatenate([ref[p] for ref in refs for p in range(ref.shape[0])], axis=1)


def project_kernel(own, where, *refs):
    refs = list(refs)
    info_ref, lengths_ref, x_ref, vec_ref, bias_ref, mask_ref, bucket_ref, table_ref = refs[:8]
    refs = refs[8:]
    if own:
        wq_ref, wk_ref, wv_ref, n_ref, kf_ref, win_ref, qf_ref, q_ref, k_ref, v_ref, norm = refs
    else:
        wk_ref, wv_ref, n_ref, kf_ref, win_ref, k_ref, v_ref, norm = refs
    rows_n, length, _ = kf_ref.shape

    @pl.when(pl.program_id(0) == 0)
    def _():
        y, _ = normalise(x_ref[...].astype(F32))
        norm[...] = (y * vector(vec_ref, ATTN_GAIN) + vector(vec_ref, ATTN_SHIFT)).astype(BF16)
        n_ref[...] = norm[...]
        count = lengths_ref.shape[1]
        lane_row = lax.broadcasted_iota(jnp.int32, (1, LANES), 1)
        lane = lax.broadcasted_iota(jnp.int32, (length, LANES), 1)
        pos = info_ref[2 * where] + lax.broadcasted_iota(jnp.int32, (length, LANES), 0)
        for r in range(rows_n):
            end = jnp.int32(0)
            begins = jnp.zeros((1, LANES), jnp.int32)
            ends = jnp.zeros((1, LANES), jnp.int32)
            for u in range(count):
                begin, end = end, end + lengths_ref[r, u]
                begins = jnp.where(lane_row == u, begin, begins)
                ends = jnp.where(lane_row == u, end, ends)
            inside = (pos >= begins) & (pos < ends)
            row = jnp.broadcast_to(mask_ref[r : r + 1, :].astype(F32), (LANES, length))
            seen = row.T > 0.5
            free = (lane >= count) | (inside & seen)
            kf_ref[r] = jnp.where(free, 0.0, MASKED).astype(BF16)
            if own:
                qf_ref[r] = jnp.where(inside, 1.0, 0.0).astype(BF16)
        buckets = table_ref.shape[1]
        at = pl.multiple_of(info_ref[2 * where + 1], LANES)
        window = bucket_ref[:, pl.ds(at, 2 * length)]
        one_hot = jnp.where(
            lax.broadcasted_iota(jnp.int32, (buckets, 2 * length), 0) == window, 1.0, 0.0
        ).astype(BF16)
        rest = table_ref[...]
        bias = None
        for _ in range(3):
            part = rest.astype(BF16)
            rest = rest - part.astype(F32)
            product = dot_nn(part, one_hot)
            bias = product if bias is None else bias + product
        for p in range(win_ref.shape[0]):
            win_ref[p] = bias[2 * p : 2 * p + 2]

    x = norm[...]
    if own:
        store_pairs(q_ref, (dot_nn(x, wq_ref[...]) + vector(bias_ref, Q_BIAS)) * 0.125)
    store_pairs(k_ref, dot_nn(x, wk_ref[...]))
    store_pairs(v_ref, dot_nn(x, wv_ref[...]) + vector(bias_ref, V_BIAS))


def project(info, lengths, x, vectors, mask, bucket, table, weights, where, after=()):
    rows, width = x.shape
    rows_n, length = mask.shape
    pairs = table.shape[0] // 2
    cols = 256
    own = len(weights) == 3
    whole = pl.BlockSpec((rows, width), lambda j: (0, 0))
    part = pl.BlockSpec((width, cols), lambda j: (0, j))
    out = pl.BlockSpec((cols // LANES, rows, LANES), lambda j: (j, 0, 0))
    feat = pl.BlockSpec((rows_n, length, LANES), lambda j: (0, 0, 0))

    def fixed(array):
        return pl.BlockSpec(array.shape, lambda j: (0,) * array.ndim)

    count = len(weights)
    features = shaped((rows_n, length, LANES), BF16)
    window = shaped((pairs, 2, 2 * length), F32)
    return call(
        functools.partial(project_kernel, own, where),
        [shaped((rows, width), BF16), features, window]
        + [features] * own
        + [shaped((pairs, rows, LANES), BF16)] * count,
        4.5,
        after=after,
        grid=(width // cols,),
        in_specs=[SMEM, SMEM, whole, fixed(vectors)]
        + [pl.BlockSpec((vectors.shape[0], cols), lambda j: (0, j))]
        + [fixed(mask), fixed(bucket), fixed(table)]
        + [part] * count,
        out_specs=[whole, feat, fixed(window)] + [feat] * own + [out] * count,
        scratch_shapes=[pltpu.VMEM((rows, width), BF16)],
    )(info, lengths, x, vectors, vectors, mask, bucket, table, *weights)


def rows_of_head(h):
    return slice(h * HD, (h + 1) * HD)


def attend_kernel(own, last, chunk, *refs):
    refs = list(refs)
    q_ref, k_ref, v_ref, qf_ref, kf_ref, w_ref = refs[:6]
    refs = refs[6:]
    if not own:
        o_in, stats_in = refs[:2]
        refs = refs[2:]
    p_ref, m_ref, o_ref, stats_ref = refs[:4]
    cx_ref = refs[4] if last else None
    t_refs = refs[-2:]
    length = q_ref.shape[0]
    nb = length // LANES
    q = q_ref[...]
    k = k_ref[...]
    lane = lax.broadcasted_iota(jnp.int32, (length, LANES), 1)
    k_wide = jnp.concatenate([k, kf_ref[...]], axis=1)
    v_flip = v_ref[...].T
    ones = jnp.ones((16, length), BF16)
    eye = lax.broadcasted_iota(jnp.int32, (LANES, LANES), 0) == lax.broadcasted_iota(
        jnp.int32, (LANES, LANES), 1
    )
    zero = jnp.zeros((), BF16)
    for h in range(2):
        t_ref = t_refs[h]
        for a in range(2 * nb - 1):
            x = w_ref[h : h + 1, 2 * length - 256 - 128 * a : 2 * length - 128 * a]
            t = pltpu.roll(jnp.broadcast_to(x, (LANES, 256)), 0, 1, stride=1, stride_axis=0)
            t_ref[128 * a : 128 * a + 128, :] = t[:, LANES:]
        q_head = jnp.where((lane < HD) == (h == 0), q, zero)
        q_wide = jnp.concatenate([q_head, qf_ref[...]], axis=1)
        v_head = jnp.concatenate([v_flip[rows_of_head(h)], ones], axis=0)
        sums, tops = [], []
        for c in range(0, length, chunk):
            s = dot_nt(k_wide, q_wide[c : c + chunk])
            weights = []
            for i in range(c // LANES, (c + chunk) // LANES):
                first = 128 * (nb - 1 - i)
                here = slice(128 * i, 128 * i + 128)
                tile = s[:, 128 * i - c : 128 * i - c + 128] + t_ref[first : first + length, :]
                if own:
                    plain = dot_nt(k[here], q_head[here]) + t_ref[128 * (nb - 1) : 128 * nb, :]
                    fixed = jnp.where(eye, plain, tile[here])
                    around = [tile[: 128 * i], fixed, tile[128 * i + 128 :]]
                    tile = jnp.concatenate([x for x in around if x.shape[0]], axis=0)
                top = jnp.max(tile, axis=0, keepdims=True)
                weight = jnp.exp(tile - top).astype(BF16)
                p_ref[h, :, here] = weight
                weights.append(weight)
                tops.append(top)
            sums.append(dot_nn(v_head, jnp.concatenate(weights, axis=1)))
        o = jnp.concatenate(sums, axis=1)
        m = jnp.concatenate(tops, axis=1)
        o, l = o[:HD], o[HD : HD + 1]
        m_ref[h : h + 1, :] = m
        if not own:
            m_old = stats_in[h : h + 1, :]
            m_new = jnp.maximum(m_old, m)
            old, new = jnp.exp(m_old - m_new), jnp.exp(m - m_new)
            o = o_in[rows_of_head(h), :] * old + o * new
            l = stats_in[2 + h : 3 + h, :] * old + l * new
            m = m_new
        if last:
            o = o / l
            m = m + jnp.log(l)
        o_ref[rows_of_head(h), :] = o
        stats_ref[h : h + 1, :] = m
        stats_ref[2 + h : 3 + h, :] = l
    if last:
        cx_ref[...] = o_ref[...].T.astype(BF16)


def attend(q, k, v, qf, kf, window, state, last, chunk=256):
    pairs, rows, length, _ = q.shape
    nb = length // LANES
    own = state is None

    def spec(*shape):
        return pl.BlockSpec((pl.squeezed, pl.squeezed, *shape), lambda p, r: (p, r) + (0,) * len(shape))

    blk, flip, stats = spec(length, LANES), spec(LANES, length), spec(8, length)
    feat = pl.BlockSpec((pl.squeezed, length, LANES), lambda p, r: (r, 0, 0))
    stats_shape = shaped((pairs, rows, 8, length), F32)
    outs = [
        shaped((pairs, rows, 2, length, length), BF16),
        stats_shape,
        shaped((pairs, rows, LANES, length), F32),
        stats_shape,
    ] + [shaped((pairs, rows, length, LANES), BF16)] * last
    return call(
        functools.partial(attend_kernel, own, last, min(chunk, length)),
        outs,
        12,
        grid=(pairs, rows),
        in_specs=[blk] * 3
        + [feat] * 2
        + [pl.BlockSpec((pl.squeezed, 2, 2 * length), lambda p, r: (p, 0, 0))]
        + ([] if own else [flip, stats]),
        out_specs=[spec(2, length, length), stats, flip, stats] + [blk] * last,
        scratch_shapes=[pltpu.VMEM(((2 * nb - 1) * LANES, LANES), F32)] * 2,
    )(q, k, v, qf, kf, window, *([] if own else state))


def diagonal_sums(ds_ref, nb, lane8):
    length = nb * LANES
    tops, lows = [], []
    for a in range(2 * nb - 1):
        total = None
        for j in range(nb):
            i0 = 128 * (a - (nb - 1) + j)
            if 0 <= i0 < length:
                x = ds_ref[i0 : i0 + 128, 128 * j : 128 * j + 128].astype(F32)
                total = x if total is None else total + x
        whole, top = total[:8], total[:8]
        for g in range(1, 16):
            x = pltpu.roll(total[8 * g : 8 * g + 8], 128 - 8 * g, 1)
            whole = whole + x
            top = top + jnp.where(lane8 < 128 - 8 * g, x, 0.0)
        tops.append(top)
        lows.append(whole - top)
    pieces = []
    for g in range(2 * nb):
        a = 2 * nb - 1 - g
        if a == 2 * nb - 1:
            pieces.append(lows[a - 1])
        elif a == 0:
            pieces.append(tops[a])
        else:
            pieces.append(tops[a] + lows[a - 1])
    z = jnp.concatenate(pieces, axis=1)
    sub = lax.broadcasted_iota(jnp.int32, z.shape, 0)
    for bit in (1, 2, 4):
        z = jnp.where((sub & bit) != 0, pltpu.roll(z, 2 * length - bit, 1), z)
    return column_sum(z)


def attend_back_kernel(first, last, *refs):
    refs = list(refs)
    p_ref, q_ref, k_ref, v_ref, dc_ref, dot_ref, lse_ref, m_ref = refs[:8]
    refs = refs[8:]
    dq_in = None if first else refs.pop(0)
    dq_ref, dk_ref, dv_ref, w_ref, ds_ref, dq_flip = refs
    length = q_ref.shape[0]
    nb = length // LANES
    q, k, v = q_ref[...], k_ref[...], v_ref[...]
    lane = lax.broadcasted_iota(jnp.int32, (length, LANES), 1)
    line = lax.broadcasted_iota(jnp.int32, (LANES, length), 0)
    lane8 = lax.broadcasted_iota(jnp.int32, (8, LANES), 1)
    low = lane < HD
    zero = jnp.zeros((), BF16)
    k_flip = k.T
    v_wide = jnp.concatenate([v, jnp.where(lane < 2, -1.0, 0.0).astype(BF16)], axis=1)
    scaled, dots = [], []
    for h in range(2):
        factor = jnp.exp(m_ref[h : h + 1, :] - lse_ref[h : h + 1, :])
        scaled.append((dc_ref[rows_of_head(h), :].astype(F32) * factor).astype(BF16))
        dots.append(dot_ref[h : h + 1, :] * factor)
    do_flip = jnp.concatenate(scaled, axis=0)
    do = do_flip.T
    row = pl.program_id(1)
    parts = []
    for h in range(2):
        dot_hi = dots[h].astype(BF16)
        dot_lo = (dots[h] - dot_hi.astype(F32)).astype(BF16)
        feat = jnp.where(line == 0, dot_hi, jnp.where(line == 1, dot_lo, zero))
        mine = jnp.where((line < HD) == (h == 0), do_flip, zero)
        p = p_ref[h]
        dp = dot_nn(v_wide, jnp.concatenate([mine, feat], axis=0))
        ds = (p.astype(F32) * dp).astype(BF16)
        ds_ref[h] = ds
        parts.append((dot_nn(ds, q), dot_nn(p, do)))
        dq = dot_nn(k_flip[rows_of_head(h)], ds)
        dq_flip[rows_of_head(h), :] = dq if first else dq + dq_in[rows_of_head(h), :]
        diagonal = diagonal_sums(ds_ref.at[h], nb, lane8)

        @pl.when(row == 0)
        def _():
            w_ref[h : h + 1, :] = diagonal

        @pl.when(row != 0)
        def _():
            w_ref[h : h + 1, :] += diagonal

    dk, dv = [jnp.where(low, one, two) for one, two in zip(*parts)]
    dq_ref[...] = dq_flip[...].T.astype(BF16) if last else dq_flip[...]
    dk_ref[...] = dk.astype(BF16)
    dv_ref[...] = dv.astype(BF16)


def attend_back(p, q, k, v, dctx, dots, lse, m, dq, last, start, count, after=()):
    _, rows, length, _ = q.shape
    first = dq is None

    def spec(*shape, start=start):
        return pl.BlockSpec(
            (pl.squeezed, pl.squeezed, *shape), lambda p, r: (p + start, r) + (0,) * len(shape)
        )

    blk, flip, stats = spec(length, LANES), spec(LANES, length), spec(8, length)
    out, out_flip = spec(length, LANES, start=0), spec(LANES, length, start=0)
    arrays = [p, q, k, v, dctx, dots, lse, m] + ([] if first else [dq])
    natural = shaped((count, rows, length, LANES), BF16)
    return call(
        functools.partial(attend_back_kernel, first, last),
        [
            natural if last else shaped((count, rows, LANES, length), F32),
            natural,
            natural,
            shaped((count, 2, 2 * length), F32),
        ],
        2.2 * count,
        after=after,
        grid=(count, rows),
        in_specs=[spec(2, length, length)]
        + [blk] * 3
        + [flip]
        + [stats] * 3
        + ([] if first else [out_flip]),
        out_specs=[out if last else out_flip, out, out]
        + [pl.BlockSpec((pl.squeezed, 2, 2 * length), lambda p, r: (p, 0, 0))],
        scratch_shapes=[
            pltpu.VMEM((2, length, length), BF16),
            pltpu.VMEM((LANES, length), F32),
        ],
    )(*arrays)


def ffn_kernel(head, *refs):
    core_ref, vec_ref, cot_ref, up_ref, down_ref, bias_ref, ctx_ref, wo_ref = refs[:8]
    refs = refs[8:]
    if head:
        x_ref, res_ref, hid_ref, down_acc, hid_acc, keep_ref, send_ref, bias_grad = refs
    else:
        hid_ref, down_in, hid_in, res_ref, at_ref = refs[:5]
        mixed_ref, dres_ref, dctx_ref, dots_ref, sums_ref = refs[5:10]
        keep_ref, send_ref, bias_grad, down_acc, hid_acc = refs[10:]
    j = pl.program_id(0)

    @pl.when(j == 0)
    def _():
        if head:
            res = x_ref[...].astype(F32) + (
                dot_nn(all_pairs([ctx_ref]), wo_ref[...]) + vector(vec_ref, O_BIAS)
            )
            res_ref[...] = res
            y, _ = normalise(res)
            hid_ref[...] = (y * vector(vec_ref, FFN_GAIN) + vector(vec_ref, FFN_SHIFT)).astype(BF16)
            down_acc[...] = jnp.zeros_like(down_acc)
            hid_acc[...] = jnp.zeros_like(hid_acc)
        else:
            down_acc[...] = down_in[...]
            hid_acc[...] = hid_in[...]

    hid, cot = hid_ref[...], cot_ref[...]
    up, down = up_ref[...], down_ref[...]
    pre = dot_nn(hid, up) + bias_ref[0]
    cdf = 0.5 + 0.5 * lax.erf(pre * 0.7071067811865476)
    slope = cdf + pre * (0.3989422804014327 * jnp.exp(-0.5 * pre * pre))
    act = (pre * cdf).astype(BF16)
    pre_grad = (dot_nt(cot, down) * slope).astype(BF16)
    down_acc[...] += dot_nn(act, down)
    hid_acc[...] += dot_nt(pre_grad, up)
    up_grad = dot_tn(hid, pre_grad).astype(BF16)
    down_grad = dot_tn(act, cot).astype(BF16)
    bias_grad[0] = column_sum(pre_grad.astype(F32))

    cb = up.shape[1] // LANES
    for core in range(2):

        @pl.when(core_ref[0] == core)
        def _():
            for c in range(cb):
                cols = slice(c * LANES, (c + 1) * LANES)
                (keep_ref, send_ref)[core][j * cb + c] = up_grad[:, cols]
                (send_ref, keep_ref)[core][j * cb + c] = down_grad[:, cols]

    if not head:

        @pl.when(j == pl.num_programs(0) - 1)
        def _():
            res = res_ref[...]
            cot = cot_ref[...].astype(F32)
            mixed_ref[...] = (res + (down_acc[...] + vector(vec_ref, DOWN_BIAS))).astype(BF16)
            y, scale = normalise(res)
            dh = hid_acc[...]
            a = dh * vector(vec_ref, FFN_GAIN)
            dres = cot + scale * (
                a
                - jnp.mean(a, axis=-1, keepdims=True)
                - y * jnp.mean(a * y, axis=-1, keepdims=True)
            )
            dres_ref[...] = dres
            branch = dres.astype(BF16)
            dots_ref[...] = jnp.zeros_like(dots_ref)
            for p in range(dctx_ref.shape[0]):
                part = dot_nt(wo_ref[p * LANES : (p + 1) * LANES, :], branch).astype(BF16)
                dctx_ref[p] = part
                product = part.astype(F32) * at_ref[p]
                for h in range(2):
                    dots_ref[p, h : h + 1, :] = column_sum(product[rows_of_head(h)])
            sums_ref[0:1] = column_sum(dh * y)
            sums_ref[1:2] = column_sum(dh)
            sums_ref[2:3] = column_sum(branch.astype(F32))
            sums_ref[3:4] = column_sum(cot)
            out_grad = dot_tn(all_pairs([ctx_ref]), branch).astype(BF16)
            first = 2 * cb
            for at in range(first, keep_ref.shape[0]):
                if at >= first + cb // 2:
                    keep_ref[at] = jnp.zeros(keep_ref.shape[1:], BF16)
                    send_ref[at] = jnp.zeros(keep_ref.shape[1:], BF16)
                    continue
                low, high = [
                    out_grad[:, c * LANES : (c + 1) * LANES]
                    for c in (at - first, at - first + cb // 2)
                ]
                for core in range(2):

                    @pl.when(core_ref[0] == core)
                    def _():
                        (keep_ref, send_ref)[core][at] = low
                        (send_ref, keep_ref)[core][at] = high


def ffn(core, vectors, cot, up, down, bias, ctx, wo, start, steps, head=None, tail=None, after=()):
    rows, width = cot.shape
    once = pl.Buffered(1)
    whole = pl.BlockSpec((rows, width), lambda j: (0, 0), pipeline_mode=once)
    square = pl.BlockSpec((width, width), lambda j: (0, 0), pipeline_mode=once)
    vecs = pl.BlockSpec((8, width), lambda j: (0, 0))
    cb = width // LANES

    def pairs(*shape):
        return pl.BlockSpec((cb, *shape), lambda j: (0, 0, 0), pipeline_mode=once)

    full, half = shaped((rows, width), F32), shaped((rows, width), BF16)
    if head is not None:
        count = steps * cb
        outs, out_specs = [full, half, full, full], [whole] * 4
    else:
        count = steps * cb + cb // 2
        count += count % 2
        outs = [
            half, full, shaped((cb, LANES, rows), BF16), shaped((cb, 8, rows), F32),
            shaped((8, width), F32),
        ]
        out_specs = [whole, whole, pairs(LANES, rows), pairs(8, rows), vecs]
    extra = list(head if head is not None else tail)
    grad_spec = pl.BlockSpec((count, width, LANES), lambda j: (0, 0, 0), pipeline_mode=once)
    return call(
        functools.partial(ffn_kernel, head is not None),
        outs + [shaped((count, width, LANES), BF16)] * 2 + [shaped((steps, 1, width), F32)],
        7 * steps,
        after=after,
        grid=(steps,),
        in_specs=[
            SMEM,
            vecs,
            whole,
            pl.BlockSpec((width, width), lambda j: (0, j + start)),
            pl.BlockSpec((width, width), lambda j: (j + start, 0)),
            pl.BlockSpec((1, 1, width), lambda j: (j + start, 0, 0)),
            pairs(rows, LANES),
            square,
        ]
        + ([whole] if head is not None else [whole] * 4 + [pairs(LANES, rows)]),
        out_specs=out_specs + [grad_spec] * 2 + [pl.BlockSpec((1, 1, width), lambda j: (j, 0, 0))],
        scratch_shapes=[] if head is not None else [pltpu.VMEM((rows, width), F32)] * 2,
    )(core, vectors, cot, up, down, bias, ctx, wo, *extra)


class Shared:
    def __init__(self, core_ref, keep_ref, send_ref):
        self.core_ref, self.refs, self.count = core_ref, (keep_ref, send_ref), 0

    def store(self, values):
        half = self.refs[0].shape[0]
        values = values.astype(BF16)
        for c in range(values.shape[1] // LANES):
            block = values[:, c * LANES : (c + 1) * LANES]
            owner, at = divmod(self.count, half)
            self.count += 1

            @pl.when(self.core_ref[0] == owner)
            def _():
                self.refs[0][at] = block

            @pl.when(self.core_ref[0] != owner)
            def _():
                self.refs[1][at] = block


def project_back_kernel(blocks, calls, *refs):
    refs = list(refs)

    def take(count):
        taken = refs[:count]
        del refs[:count]
        return taken

    core_ref, info_ref, bucket_ref, vec_ffn, *bias_grads = take(6)
    peer_sums = take(blocks - 1)
    n_refs, (x_ref,) = take(blocks), take(1)
    wq_ref, wk_ref, wv_ref = take(3)
    dq_refs = take(calls)
    dk_refs, dv_refs, w_refs = [[take(calls) for _ in range(blocks)] for _ in range(3)]
    (ng_ref,) = take(1)
    keep_ref, send_ref, small_ref = take(3)
    grads = Shared(core_ref, keep_ref, send_ref)
    dq = all_pairs(dq_refs)
    gk = gv = bias = None
    for b in range(blocks):
        dk, dv, norm = all_pairs(dk_refs[b]), all_pairs(dv_refs[b]), n_refs[b][...]
        if b == 0:
            ng = 0.125 * dot_nt(dq, wq_ref[...])
            ng = ng + dot_nt(dk, wk_ref[...]) + dot_nt(dv, wv_ref[...])
            grads.store(0.125 * dot_tn(norm, dq))
            ng_ref[...] = ng
            y, _ = normalise(x_ref[...].astype(F32))
            sums = [column_sum(ng * y), column_sum(ng)]
        k_part, v_part, b_part = dot_tn(norm, dk), dot_tn(norm, dv), column_sum(dv.astype(F32))
        gk = k_part if gk is None else gk + k_part
        gv = v_part if gv is None else gv + v_part
        bias = b_part if bias is None else bias + b_part
    for peer in peer_sums:
        sums = [mine + peer[i : i + 1] for i, mine in enumerate(sums)]
    grads.store(gk)
    grads.store(gv)
    small_ref[...] = jnp.zeros_like(small_ref)
    vectors = sums + [0.125 * column_sum(dq.astype(F32)), bias]
    vectors += [vec_ffn[i : i + 1] for i in range(4)]
    vectors += [ref[i] for ref in bias_grads for i in range(ref.shape[0])]
    at = 0
    for vec in vectors:
        for c in range(vec.shape[1] // LANES):
            small_ref[at : at + 1, :] = vec[:, c * LANES : (c + 1) * LANES]
            at += 1
    table = None
    span = w_refs[0][0].shape[2]
    for b in range(blocks):
        start = pl.multiple_of(info_ref[2 * b + 1], LANES)
        window = bucket_ref[:, pl.ds(start, span)]
        one_hot = jnp.where(
            lax.broadcasted_iota(jnp.int32, (TABLE_ROWS, span), 0) == window, 1.0, 0.0
        ).astype(BF16)
        w = jnp.concatenate([ref[p] for ref in w_refs[b] for p in range(ref.shape[0])], axis=0)
        w_hi = w.astype(BF16)
        w_lo = (w - w_hi.astype(F32)).astype(BF16)
        part = dot_nt(w_hi, one_hot) + dot_nt(w_lo, one_hot)
        table = part if table is None else table + part
    for c in range(TABLE_ROWS // LANES):
        small_ref[at : at + table.shape[0], :] = table[:, c * LANES : (c + 1) * LANES]
        at += table.shape[0]
    grads.store(small_ref[...])
    while grads.count < 2 * keep_ref.shape[0]:
        grads.store(jnp.zeros_like(small_ref))


TABLE_ROWS = 384


def project_back(core, info, bucket, vec_ffn, bias_grads, peer_sums, norms, x, weights, parts,
                 after=()):
    rows, width = norms[0].shape
    blocks = len(norms)
    whole = pl.BlockSpec(memory_space=pltpu.VMEM)
    arrays = [core, info, bucket, vec_ffn, *bias_grads, *peer_sums, *norms, x, *weights]
    arrays += [part[0].reshape(-1, rows, LANES) for part in parts[0]]
    for kind in (1, 2):
        arrays += [part[kind].reshape(-1, rows, LANES) for block in parts for part in block]
    arrays += [part[3] for block in parts for part in block]
    count = 3 * width // LANES + 1
    count += -count % 4
    ng, *grads = call(
        functools.partial(project_back_kernel, blocks, len(parts[0])),
        [shaped((rows, width), F32)] + [shaped((count // 2, width, LANES), BF16)] * 2,
        14,
        after=after,
        grid=(1,),
        in_specs=[SMEM, SMEM] + [whole] * (len(arrays) - 2),
        scratch_shapes=[pltpu.VMEM((width, LANES), F32)],
    )(*arrays)
    return ng, grads


def peer_back_kernel(calls, *refs):
    x_ref, wk_ref, wv_ref = refs[:3]
    dk_refs, dv_refs = refs[3 : 3 + calls], refs[3 + calls : 3 + 2 * calls]
    ng_ref, sums_ref = refs[3 + 2 * calls :]
    dk, dv = all_pairs(dk_refs), all_pairs(dv_refs)
    ng = dot_nt(dk, wk_ref[...]) + dot_nt(dv, wv_ref[...])
    ng_ref[...] = ng.astype(BF16)
    y, _ = normalise(x_ref[...].astype(F32))
    sums_ref[0:1] = column_sum(ng * y)
    sums_ref[1:2] = column_sum(ng)


def peer_back(x, weights, parts, after=()):
    rows, width = x.shape
    arrays = [x, *weights[1:]]
    for kind in (1, 2):
        arrays += [part[kind].reshape(-1, rows, LANES) for part in parts]
    return call(
        functools.partial(peer_back_kernel, len(parts)),
        [shaped((rows, width), BF16), shaped((8, width), F32)],
        4,
        after=after,
        grid=(1,),
        in_specs=[IN_VMEM] * len(arrays),
    )(*arrays)


def frames_back_kernel(count, *refs):
    x_ref, vec_ref, dres_ref, ng_ref = refs[:4]
    out_ref = refs[-1]
    y, scale = normalise(x_ref[...].astype(F32))
    ng = ng_ref[...]
    for other in refs[4 : 4 + count]:
        ng = ng + other[...].astype(F32)
    a = ng * vector(vec_ref, ATTN_GAIN)
    out_ref[...] = dres_ref[...] + scale * (
        a - jnp.mean(a, axis=-1, keepdims=True) - y * jnp.mean(a * y, axis=-1, keepdims=True)
    )


def frames_back(x, vectors, dres, ng, others, after=()):
    rows, width = x.shape
    tile = 128
    blk = pl.BlockSpec((tile, width), lambda i: (i, 0))
    vec = pl.BlockSpec((8, width), lambda i: (0, 0))
    return call(
        functools.partial(frames_back_kernel, len(others)),
        shaped((rows, width), F32),
        4,
        after=after,
        grid=(rows // tile,),
        in_specs=[blk, vec, blk, blk] + [blk] * len(others),
        out_specs=blk,
    )(x, vectors, dres, ng, *others)


def swap(x, bit):
    axis, mask = bit
    if isinstance(mask, int):
        mask = [(i, i ^ mask) for i in range(lax.axis_size(axis))]
    return lax.ppermute(x, axis, mask)


def side(bit):
    axis, mask = bit
    return ((lax.axis_index(axis) & mask) != 0).astype(jnp.int32)


CORE, ALONG, ACROSS = ("batch", 1), ("batch", 2), ("blk", 1)

def local(kernel, sides, arrays, shapes):
    return pl.pallas_call(
        kernel,
        out_shape=[shaped(shape, BF16) for shape in shapes],
        in_specs=[SMEM] + [IN_VMEM] * len(arrays),
        out_specs=[IN_VMEM] * len(shapes),
        compiler_params=pltpu.CompilerParams(vmem_limit_bytes=4 * 1024 * 1024),
        cost_estimate=cost_of(0.01),
    )(sides, *arrays)


def both_halves(size, at):
    return [pl.ds(pl.multiple_of(k * size, 16), size) for k in (1 - at, at)]


def add(a, b):
    return (a.astype(F32) + b.astype(F32)).astype(BF16)


def sum_over_devices(keep, send):
    n, rows, _ = keep.shape
    half = n // 2
    x, y = range(2)
    here = lax.axis_index("batch") // 4
    sides = jnp.stack([side(ACROSS), side(ALONG), here])
    (got,) = yield [(send, CORE)]

    def first(s, keep, got, send_a, keep_a, send_b, keep_b):
        for k, bit, outs in ((0, x, (send_a, keep_a)), (1, y, (send_b, keep_b))):
            block = slice(k * half, (k + 1) * half)
            for rows_at, out in zip(both_halves(rows // 2, s[bit]), outs):
                out[...] = add(keep[block, rows_at, :], got[block, rows_at, :])

    shape = (half, rows // 2, LANES)
    send_a, keep_a, send_b, keep_b = local(first, sides, [keep, got], [shape] * 4)
    got_a, got_b = yield [(send_a, ACROSS), (send_b, ALONG)]

    def second(s, keep_a, got_a, keep_b, got_b, *outs):
        for k, bit, keep, got in ((0, y, keep_a, got_a), (1, x, keep_b, got_b)):
            for rows_at, out in zip(both_halves(rows // 4, s[bit]), outs[2 * k : 2 * k + 2]):
                out[...] = add(keep[:, rows_at, :], got[:, rows_at, :])

    shape = (half, rows // 4, LANES)
    send_a, keep_a, send_b, keep_b = local(
        second, sides, [keep_a, got_a, keep_b, got_b], [shape] * 4
    )
    got_a, got_b = yield [(send_a, ALONG), (send_b, ACROSS)]

    quarter = rows // 16
    peers = [("batch", mask) for mask in (4, 8, 12)]

    def third(s, keep_a, got_a, keep_b, got_b, *outs):
        for k, keep, got in ((0, keep_a, got_a), (1, keep_b, got_b)):
            for distance, out in enumerate(outs):
                at = pl.ds(pl.multiple_of((s[2] ^ distance) * quarter, 16), quarter)
                out[k * half : (k + 1) * half] = add(keep[:, at, :], got[:, at, :])

    shape = (n, quarter, LANES)
    keep, *sends = local(third, sides, [keep_a, got_a, keep_b, got_b], [shape] * 4)
    gots = yield list(zip(sends, peers))

    def fourth(s, *refs):
        refs[-1][...] = functools.reduce(jnp.add, [x[...].astype(F32) for x in refs[:-1]]).astype(
            BF16
        )

    (held,) = local(fourth, sides, [keep, *gots], [shape])
    gots = yield [(held, peer) for peer in peers]

    def join_third(s, *refs):
        for distance, ref in enumerate(refs[:4]):
            at = pl.ds(pl.multiple_of((s[2] ^ distance) * quarter, 16), quarter)
            for k, out in enumerate(refs[4:]):
                out[:, at, :] = ref[k * half : (k + 1) * half]

    held_a, held_b = local(join_third, sides, [held, *gots], [(half, rows // 4, LANES)] * 2)
    got_a, got_b = yield [(held_a, ALONG), (held_b, ACROSS)]

    def join_second(s, held_a, got_a, held_b, got_b, *outs):
        for bit, held, got, out in ((y, held_a, got_a, outs[0]), (x, held_b, got_b, outs[1])):
            for rows_at, ref in zip(both_halves(rows // 4, s[bit]), (got, held)):
                out[:, rows_at, :] = ref[...]

    held_a, held_b = local(
        join_second, sides, [held_a, got_a, held_b, got_b], [(half, rows // 2, LANES)] * 2
    )
    got_a, got_b = yield [(held_a, ACROSS), (held_b, ALONG)]

    def join_first(s, held_a, got_a, held_b, got_b, out):
        for k, bit, held, got in ((0, x, held_a, got_a), (1, y, held_b, got_b)):
            for rows_at, ref in zip(both_halves(rows // 2, s[bit]), (got, held)):
                out[k * half : (k + 1) * half, rows_at, :] = ref[...]

    (held,) = local(join_first, sides, [held_a, got_a, held_b, got_b], [(n, rows, LANES)])
    (got,) = yield [(held, CORE)]
    return held, got


def sum_plainly(keep, send):
    low = side(CORE) == 0
    first, second = [
        lax.psum(jnp.where(low, *pair), ("batch", "blk")) for pair in ((keep, send), (send, keep))
    ]
    yield [(first[:1, :8], CORE)]
    return jnp.where(low, first, second), jnp.where(low, second, first)


def send_back(x, b):
    blocks = lax.axis_size("blk")
    (got,) = yield [(x, ("blk", [(i, (i + b) % blocks) for i in range(blocks)]))]
    return got


def summed(keep, send):
    fits = lax.axis_size("blk") == 2 and lax.axis_size("batch") == 16
    return (sum_over_devices if fits else sum_plainly)(keep, send)


class Flow:
    def __init__(self, steps):
        self.steps = steps
        self.result = None
        self.pending = next(steps)

    def arrays(self):
        return [array for array, _ in self.pending]

    def send(self):
        self.got = [swap(array, bit) for array, bit in self.pending]

    def land(self, after):
        if after:
            *self.got, _ = lax.optimization_barrier([*self.got, *after])
        try:
            self.pending = self.steps.send(self.got)
        except StopIteration as end:
            self.pending, self.result = [], end.value


class Flows:
    def __init__(self):
        self.open = []

    def add(self, steps):
        flow = Flow(steps)
        self.open.append(flow)
        return flow

    def during(self, kernel):
        after = [array for flow in self.open for array in flow.arrays()]
        for flow in self.open:
            flow.send()
        result = kernel(after)
        self.land(jax.tree.leaves(result)[-1:])
        return result

    def land(self, after):
        for flow in self.open:
            flow.land(after)
        self.open = [flow for flow in self.open if flow.pending]

    def step(self):
        for flow in self.open:
            flow.send()
        came = lax.optimization_barrier([flow.got for flow in self.open])
        for flow, got in zip(self.open, came):
            flow.got = got
        self.land([])


def place_kernel(plan, tile, core_ref, *refs):
    ins = refs[: 2 * (1 + max(step[0] for step in plan))]
    outs = refs[len(ins) :]
    rows = pl.ds(pl.multiple_of(pl.program_id(0) * tile, 16), tile)
    for core in range(2):

        @pl.when(core_ref[0] == core)
        def _():
            for source, half, column, out, slot, at in plan:
                x = ins[2 * source + (half ^ core)][column, rows, :].astype(F32)
                cols = slice(at * LANES, (at + 1) * LANES)
                if slot is None:
                    outs[out][:, cols] = x
                else:
                    outs[out][slot, :, cols] = x


def place(core, flows, plan, out_shapes, after=()):
    halves = [half for flow in flows for half in flow.result]
    tile = 96
    out_specs = []
    for shape in out_shapes:
        if len(shape) == 2:
            out_specs.append(pl.BlockSpec((tile, shape[1]), lambda i: (i, 0)))
        else:
            out_specs.append(pl.BlockSpec((shape[0], tile, shape[2]), lambda i: (0, i, 0)))
    return call(
        functools.partial(place_kernel, plan, tile),
        [shaped(shape, F32) for shape in out_shapes],
        7,
        after=after,
        grid=(halves[0].shape[1] // tile,),
        in_specs=[SMEM] + [IN_VMEM] * len(halves),
        out_specs=out_specs,
    )(core, *halves)


def per_device(
    frames,
    cotangent,
    query_weight,
    key_weight,
    value_weight,
    output_weight,
    up_weight,
    down_weight,
    attn_gain,
    attn_shift,
    query_bias,
    value_bias,
    output_bias,
    ffn_gain,
    ffn_shift,
    up_bias,
    down_bias,
    rel_table,
    utt_lengths,
    frame_mask,
    rel_bucket,
):
    rows_n, length, width = frames.shape
    blocks = lax.axis_size("blk")
    seq = length * blocks
    me = lax.axis_index("blk")
    rows = rows_n * length
    units = up_weight.shape[1]
    steps = units // width
    heads = rel_table.shape[1]
    buckets = rel_table.shape[0]
    core = side(CORE).reshape(1)
    weights = (query_weight, key_weight, value_weight)

    def from_peer(x, b):
        return lax.ppermute(x, "blk", [((i + b) % blocks, i) for i in range(blocks)])

    def split(x):
        return x.reshape(x.shape[0], rows_n, length, x.shape[2])

    def split_flip(x):
        return jnp.swapaxes(x.reshape(*x.shape[:2], rows_n, length), 1, 2)

    def join_flip(x):
        return jnp.swapaxes(x, 1, 2).reshape(x.shape[0], x.shape[2], rows)

    def flat(x):
        return x.reshape(rows, x.shape[-1])

    flat_frames = flat(frames)
    x_blocks = [flat_frames] + [from_peer(flat_frames, b) for b in range(1, blocks)]
    masks = [frame_mask] + [from_peer(frame_mask, b) for b in range(1, blocks)]
    starts = [((me + b) % blocks) * length for b in range(blocks)]
    info = jnp.stack(
        [x for start in starts for x in (start, seq - length + starts[0] - start)]
    ).astype(jnp.int32)
    bucket = jnp.concatenate([jnp.full((1,), -1, jnp.int32), rel_bucket]).reshape(1, -1)
    vectors = jnp.stack(
        [
            attn_gain, attn_shift, query_bias, value_bias, output_bias, ffn_gain, ffn_shift,
            down_bias,
        ]
    )

    norms, keys, values, probs, tops = [], [], [], [], []
    state = None
    for b in range(blocks):
        last = b == blocks - 1
        norm, key_feat, window, *rest = project(
            info, utt_lengths, x_blocks[b], vectors, masks[b], bucket, rel_table.T,
            weights[1:] if b else weights, b,
        )
        if b == 0:
            query_feat, query, key, value = rest
            query = split(query)
        else:
            key, value = rest
        norms.append(norm)
        keys.append(split(key))
        values.append(split(value))
        p, m, out, stats, *context = attend(
            query, keys[b], values[b], query_feat, key_feat, window, state, last
        )
        probs.append(p)
        tops.append(m)
        state = (out, stats)

    attended, lse = state
    context = context[0].reshape(heads // 2, rows, LANES)
    cot = flat(cotangent)
    flows = Flows()
    dense = (
        core, vectors, cot, up_weight, down_weight, up_bias.reshape(steps, 1, width), context,
        output_weight,
    )
    half = steps // 2
    res, hid, *carry, keep, send, bias_one = ffn(*dense, 0, half, head=(flat_frames,))
    sums = [flows.add(summed(keep, send))]
    mixed, dres, dctx, dots, vec_ffn, keep, send, bias_two = flows.during(
        lambda after: ffn(
            *dense, half, steps - half, tail=(hid, *carry, res, join_flip(attended)), after=after
        )
    )
    sums.append(flows.add(summed(keep, send)))

    dctx, dots = split_flip(dctx), split_flip(dots)
    pairs = heads // 2
    half_pairs = pairs // 2
    parts = [[] for _ in range(blocks)]
    peer_sums, sent = [], []
    dqs = [None, None]
    for b in [*range(1, blocks), 0]:
        for i in range(2):

            def run(after):
                return attend_back(
                    probs[b], query, keys[b], values[b], dctx, dots, lse, tops[b], dqs[i], b == 0, i * half_pairs, (half_pairs, pairs - half_pairs)[i], after=after,
                )

            parts[b].append(flows.during(run))
            dqs[i] = parts[b][-1][0]
        if b:
            ng, peer_sum = peer_back(x_blocks[b], weights, parts[b])
            peer_sums.append(peer_sum)
            sent.append(flows.add(send_back(ng, b)))
    own_ng, shared = flows.during(
        lambda after: project_back(
            core, info, bucket, vec_ffn, (bias_one, bias_two), peer_sums, norms, flat_frames,
            weights, parts, after=after + [flow.result for flow in sent if flow.result is not None],
        )
    )
    last_sum = flows.add(summed(*shared))

    cb = width // LANES
    plan = []
    for chunk in range(steps):
        which, first = divmod(chunk, half)
        for c in range(cb):
            column = first * cb + c
            plan.append((which, 0, column, 0, None, chunk * cb + c))
            plan.append((which, 1, column, 1, chunk, c))
    for c in range(cb):
        plan.append((1, c // (cb // 2), 2 * cb + c % (cb // 2), 2, None, c))
    shapes = [(width, units), (steps, width, width), (width, width)]

    def place_dense(after):
        return place(core, sums, plan, shapes, after=after)

    def place_frames(after):
        return frames_back(
            flat_frames, vectors, dres, own_ng, [flow.result for flow in sent], after=after
        )

    tasks = [place_frames, place_dense]
    done = []
    while flows.open:
        if tasks and (tasks[0] is place_frames or all(flow.result is not None for flow in sums)):
            done.append(flows.during(tasks.pop(0)))
        else:
            flows.step()
    done += [task([]) for task in tasks]
    frames_grad, (up_total, down_total, output_total) = done
    last_half = last_sum.result[0].shape[0]
    plan = [
        (0, n // last_half, n % last_half, n // cb, None, n % cb) for n in range(3 * cb + 1)
    ]
    query_total, key_total, value_total, small = place(
        core, [last_sum], plan, [(width, width)] * 3 + [(width, LANES)]
    )
    flat_small = small[: (8 + steps) * cb].reshape(-1, width)
    table_rows = small[(8 + steps) * cb : (8 + steps) * cb + heads * TABLE_ROWS // LANES]
    table_total = jnp.concatenate(
        [table_rows[i : i + heads] for i in range(0, table_rows.shape[0], heads)], axis=1
    )[:, :buckets].T
    return (
        mixed.reshape(frames.shape),
        frames_grad.reshape(frames.shape),
        query_total,
        key_total,
        value_total,
        output_total,
        up_total,
        down_total.reshape(units, width),
        flat_small[0],
        flat_small[1],
        flat_small[2],
        flat_small[3],
        flat_small[6],
        flat_small[4],
        flat_small[5],
        flat_small[8:].reshape(units),
        flat_small[7],
        table_total,
    )


def solution(mesh):
    batch3 = P("batch", "blk", None)
    in_specs = (batch3, batch3) + (P(),) * 16 + (P("batch", None), P("batch", "blk"), P())
    out_specs = (batch3, batch3) + (P(),) * 16
    return jax.shard_map(
        per_device, mesh=mesh, in_specs=in_specs, out_specs=out_specs, check_vma=False
    )
```

```python
import functools

import jax
import jax.numpy as jnp
from jax import lax
from jax.experimental import pallas as pl
from jax.experimental.pallas import tpu as pltpu
from jax.sharding import PartitionSpec as P

HD = 64
LANES = 128
EPSILON = 1e-05
MASKED = -1e30
BF16 = jnp.bfloat16
F32 = jnp.float32
COST = 1
SHORT, LONG = 0.05, 1000
HIGHEST = lax.Precision.HIGHEST


def dot_nn(a, b):
    return lax.dot_general(a, b, (((1,), (0,)), ((), ())), preferred_element_type=F32)


def dot_nt(a, b):
    return lax.dot_general(a, b, (((1,), (1,)), ((), ())), preferred_element_type=F32)


def dot_tn(a, b):
    return lax.dot_general(a, b, (((0,), (0,)), ((), ())), preferred_element_type=F32)


def normalise(values):
    centre = values - jnp.mean(values, axis=-1, keepdims=True)
    scale = lax.rsqrt(jnp.mean(centre * centre, axis=-1, keepdims=True) + EPSILON)
    return centre * scale, scale


def column_sum(values):
    return jnp.sum(values, axis=0, keepdims=True)


def cost_of(time):
    return pl.CostEstimate(
        flops=int(time * COST * 1.1e9), bytes_accessed=int(time * COST * 3e6), transcendentals=0
    )


def call(kernel, out_shape, time, after=(), vmem=32, **kw):
    skip = len(after)

    def run(*refs):
        kernel(*refs[skip:])

    kw["in_specs"] = [pl.BlockSpec(memory_space=pl.ANY)] * skip + list(kw["in_specs"])
    program = pl.pallas_call(
        run,
        out_shape=out_shape,
        compiler_params=pltpu.CompilerParams(vmem_limit_bytes=vmem * 1024 * 1024),
        cost_estimate=cost_of(time),
        **kw,
    )
    return lambda *arrays: program(*after, *arrays)


SMEM = pl.BlockSpec(memory_space=pltpu.SMEM)
IN_VMEM = pl.BlockSpec(memory_space=pltpu.VMEM)


def shaped(shape, dtype):
    return jax.ShapeDtypeStruct(shape, dtype)


def row(ref):
    return ref[...].reshape(1, ref.shape[0])


def store_pairs(ref, values):
    for p in range(values.shape[1] // LANES):
        ref[p] = values[:, p * LANES : (p + 1) * LANES].astype(ref.dtype)


def all_pairs(refs):
    return jnp.concatenate([ref[p] for ref in refs for p in range(ref.shape[0])], axis=1)


def project_kernel(own, where, *refs):
    refs = list(refs)
    info_ref, lengths_ref, x_ref, gain_ref, shift_ref, mask_ref, bucket_ref, table_ref = refs[:8]
    refs = refs[8:]
    if own:
        bq_ref = refs.pop(0)
    bv_ref = refs.pop(0)
    if own:
        wq_ref, wk_ref, wv_ref, n_ref, kf_ref, win_ref, qf_ref, q_ref, k_ref, v_ref, norm = refs
    else:
        wk_ref, wv_ref, n_ref, kf_ref, win_ref, k_ref, v_ref, norm = refs
    rows_n, length, _ = kf_ref.shape

    @pl.when(pl.program_id(0) == 0)
    def _():
        y, _ = normalise(x_ref[...].astype(F32))
        norm[...] = (y * row(gain_ref) + row(shift_ref)).astype(BF16)
        n_ref[...] = norm[...]
        count = lengths_ref.shape[1]
        lane_row = lax.broadcasted_iota(jnp.int32, (1, LANES), 1)
        lane = lax.broadcasted_iota(jnp.int32, (length, LANES), 1)
        pos = info_ref[2 * where] + lax.broadcasted_iota(jnp.int32, (length, LANES), 0)
        for r in range(rows_n):
            end = jnp.int32(0)
            begins = jnp.zeros((1, LANES), jnp.int32)
            ends = jnp.zeros((1, LANES), jnp.int32)
            for u in range(count):
                begin, end = end, end + lengths_ref[r, u]
                begins = jnp.where(lane_row == u, begin, begins)
                ends = jnp.where(lane_row == u, end, ends)
            inside = (pos >= begins) & (pos < ends)
            seen = jnp.broadcast_to(mask_ref[r : r + 1, :].astype(F32), (LANES, length)).T > 0.5
            free = (lane >= count) | (inside & seen)
            kf_ref[r] = jnp.where(free, 0.0, MASKED).astype(BF16)
            if own:
                qf_ref[r] = jnp.where(inside, 1.0, 0.0).astype(BF16)
        buckets = table_ref.shape[1]
        at = pl.multiple_of(info_ref[2 * where + 1], LANES)
        window = bucket_ref[:, pl.ds(at, 2 * length)]
        one_hot = jnp.where(
            lax.broadcasted_iota(jnp.int32, (buckets, 2 * length), 0) == window, 1.0, 0.0
        ).astype(BF16)
        rest = table_ref[...]
        bias = None
        for _ in range(3):
            part = rest.astype(BF16)
            rest = rest - part.astype(F32)
            product = dot_nn(part, one_hot)
            bias = product if bias is None else bias + product
        for p in range(win_ref.shape[0]):
            win_ref[p] = bias[2 * p : 2 * p + 2]

    x = norm[...]
    if own:
        store_pairs(q_ref, (dot_nn(x, wq_ref[...]) + row(bq_ref)) * 0.125)
    store_pairs(k_ref, dot_nn(x, wk_ref[...]))
    store_pairs(v_ref, dot_nn(x, wv_ref[...]) + row(bv_ref))


def project(info, lengths, x, norm, mask, bucket, table, weights, biases, where, after=()):
    rows, width = x.shape
    rows_n, length = mask.shape
    pairs = table.shape[0] // 2
    cols = 256
    own = len(weights) == 3
    whole = pl.BlockSpec((rows, width), lambda j: (0, 0))
    part = pl.BlockSpec((width, cols), lambda j: (0, j))
    out = pl.BlockSpec((cols // LANES, rows, LANES), lambda j: (j, 0, 0))
    feat = pl.BlockSpec((rows_n, length, LANES), lambda j: (0, 0, 0))

    def fixed(array):
        return pl.BlockSpec(array.shape, lambda j: (0,) * array.ndim)

    count = len(weights)
    features = shaped((rows_n, length, LANES), BF16)
    window = shaped((pairs, 2, 2 * length), F32)
    return call(
        functools.partial(project_kernel, own, where),
        [shaped((rows, width), BF16), features, window]
        + [features] * own
        + [shaped((pairs, rows, LANES), BF16)] * count,
        5,
        after=after,
        vmem=56,
        grid=(width // cols,),
        in_specs=[SMEM, SMEM, whole, fixed(norm[0]), fixed(norm[1])]
        + [fixed(mask), fixed(bucket), fixed(table)]
        + [pl.BlockSpec((cols,), lambda j: (j,))] * len(biases)
        + [part] * count,
        out_specs=[whole, feat, fixed(window)] + [feat] * own + [out] * count,
        scratch_shapes=[pltpu.VMEM((rows, width), BF16)],
    )(info, lengths, x, *norm, mask, bucket, table, *biases, *weights)


def rows_of_head(h):
    return slice(h * HD, (h + 1) * HD)


def attend_kernel(own, last, chunk, *refs):
    refs = list(refs)
    q_ref, k_ref, v_ref, qf_ref, kf_ref, w_ref = refs[:6]
    refs = refs[6:]
    if not own:
        o_in, stats_in = refs[:2]
        refs = refs[2:]
    p_ref, m_ref, o_ref, stats_ref = refs[:4]
    cx_ref = refs[4] if last else None
    t_refs = refs[-2:]
    length = q_ref.shape[0]
    nb = length // LANES
    q = q_ref[...]
    k = k_ref[...]
    lane = lax.broadcasted_iota(jnp.int32, (length, LANES), 1)
    k_wide = jnp.concatenate([k, kf_ref[...]], axis=1)
    v_flip = v_ref[...].T
    ones = jnp.ones((16, length), BF16)
    eye = lax.broadcasted_iota(jnp.int32, (LANES, LANES), 0) == lax.broadcasted_iota(
        jnp.int32, (LANES, LANES), 1
    )
    zero = jnp.zeros((), BF16)
    for h in range(2):
        t_ref = t_refs[h]
        for a in range(2 * nb - 1):
            x = w_ref[h : h + 1, 2 * length - 256 - 128 * a : 2 * length - 128 * a]
            t = pltpu.roll(jnp.broadcast_to(x, (LANES, 256)), 0, 1, stride=1, stride_axis=0)
            t_ref[128 * a : 128 * a + 128, :] = t[:, LANES:]
        q_head = jnp.where((lane < HD) == (h == 0), q, zero)
        q_wide = jnp.concatenate([q_head, qf_ref[...]], axis=1)
        v_head = jnp.concatenate([v_flip[rows_of_head(h)], ones], axis=0)
        sums, tops = [], []
        for c in range(0, length, chunk):
            s = dot_nt(k_wide, q_wide[c : c + chunk])
            weights = []
            for i in range(c // LANES, (c + chunk) // LANES):
                first = 128 * (nb - 1 - i)
                here = slice(128 * i, 128 * i + 128)
                tile = s[:, 128 * i - c : 128 * i - c + 128] + t_ref[first : first + length, :]
                if own:
                    plain = dot_nt(k[here], q_head[here]) + t_ref[128 * (nb - 1) : 128 * nb, :]
                    fixed = jnp.where(eye, plain, tile[here])
                    around = [tile[: 128 * i], fixed, tile[128 * i + 128 :]]
                    tile = jnp.concatenate([x for x in around if x.shape[0]], axis=0)
                top = jnp.max(tile, axis=0, keepdims=True)
                weight = jnp.exp(tile - top).astype(BF16)
                p_ref[h, :, here] = weight
                weights.append(weight)
                tops.append(top)
            sums.append(dot_nn(v_head, jnp.concatenate(weights, axis=1)))
        o = jnp.concatenate(sums, axis=1)
        m = jnp.concatenate(tops, axis=1)
        o, l = o[:HD], o[HD : HD + 1]
        m_ref[h : h + 1, :] = m
        if not own:
            m_old = stats_in[h : h + 1, :]
            m_new = jnp.maximum(m_old, m)
            old, new = jnp.exp(m_old - m_new), jnp.exp(m - m_new)
            o = o_in[rows_of_head(h), :] * old + o * new
            l = stats_in[2 + h : 3 + h, :] * old + l * new
            m = m_new
        if last:
            o = o / l
            m = m + jnp.log(l)
        o_ref[rows_of_head(h), :] = o
        stats_ref[h : h + 1, :] = m
        stats_ref[2 + h : 3 + h, :] = l
    if last:
        cx_ref[...] = o_ref[...].T.astype(BF16)


def attend(q, k, v, qf, kf, window, state, last, chunk=256):
    pairs, rows, length, _ = q.shape
    nb = length // LANES
    own = state is None

    def spec(*shape):
        return pl.BlockSpec((pl.squeezed, pl.squeezed, *shape), lambda p, r: (p, r) + (0,) * len(shape))

    blk, flip, stats = spec(length, LANES), spec(LANES, length), spec(8, length)
    feat = pl.BlockSpec((pl.squeezed, length, LANES), lambda p, r: (r, 0, 0))
    stats_shape = shaped((pairs, rows, 8, length), F32)
    outs = [
        shaped((pairs, rows, 2, length, length), BF16),
        stats_shape,
        shaped((pairs, rows, LANES, length), F32),
        stats_shape,
    ] + [shaped((pairs, rows, length, LANES), BF16)] * last
    return call(
        functools.partial(attend_kernel, own, last, min(chunk, length)),
        outs,
        12,
        vmem=56,
        grid=(pairs, rows),
        in_specs=[blk] * 3
        + [feat] * 2
        + [pl.BlockSpec((pl.squeezed, 2, 2 * length), lambda p, r: (p, 0, 0))]
        + ([] if own else [flip, stats]),
        out_specs=[spec(2, length, length), stats, flip, stats] + [blk] * last,
        scratch_shapes=[pltpu.VMEM(((2 * nb - 1) * LANES, LANES), F32)] * 2,
    )(q, k, v, qf, kf, window, *([] if own else state))


def diagonal_sums(ds_ref, nb, lane8):
    length = nb * LANES
    tops, lows = [], []
    for a in range(2 * nb - 1):
        total = None
        for j in range(nb):
            i0 = 128 * (a - (nb - 1) + j)
            if 0 <= i0 < length:
                x = ds_ref[i0 : i0 + 128, 128 * j : 128 * j + 128].astype(F32)
                total = x if total is None else total + x
        whole, top = total[:8], total[:8]
        for g in range(1, 16):
            x = pltpu.roll(total[8 * g : 8 * g + 8], 128 - 8 * g, 1)
            whole = whole + x
            top = top + jnp.where(lane8 < 128 - 8 * g, x, 0.0)
        tops.append(top)
        lows.append(whole - top)
    pieces = []
    for g in range(2 * nb):
        a = 2 * nb - 1 - g
        if a == 2 * nb - 1:
            pieces.append(lows[a - 1])
        elif a == 0:
            pieces.append(tops[a])
        else:
            pieces.append(tops[a] + lows[a - 1])
    z = jnp.concatenate(pieces, axis=1)
    sub = lax.broadcasted_iota(jnp.int32, z.shape, 0)
    for bit in (1, 2, 4):
        z = jnp.where((sub & bit) != 0, pltpu.roll(z, 2 * length - bit, 1), z)
    return column_sum(z)


def attend_back_kernel(first, last, *refs):
    refs = list(refs)
    p_ref, q_ref, k_ref, v_ref, dc_ref, dot_ref, lse_ref, m_ref = refs[:8]
    refs = refs[8:]
    dq_in = None if first else refs.pop(0)
    dq_ref, dk_ref, dv_ref, w_ref, ds_ref, dq_flip = refs
    length = q_ref.shape[0]
    nb = length // LANES
    q, k, v = q_ref[...], k_ref[...], v_ref[...]
    lane = lax.broadcasted_iota(jnp.int32, (length, LANES), 1)
    line = lax.broadcasted_iota(jnp.int32, (LANES, length), 0)
    lane8 = lax.broadcasted_iota(jnp.int32, (8, LANES), 1)
    low = lane < HD
    zero = jnp.zeros((), BF16)
    k_flip = k.T
    v_wide = jnp.concatenate([v, jnp.where(lane < 2, -1.0, 0.0).astype(BF16)], axis=1)
    scaled, dots = [], []
    for h in range(2):
        factor = jnp.exp(m_ref[h : h + 1, :] - lse_ref[h : h + 1, :])
        scaled.append((dc_ref[rows_of_head(h), :].astype(F32) * factor).astype(BF16))
        dots.append(dot_ref[h : h + 1, :] * factor)
    do_flip = jnp.concatenate(scaled, axis=0)
    do = do_flip.T
    row = pl.program_id(1)
    parts = []
    for h in range(2):
        dot_hi = dots[h].astype(BF16)
        dot_lo = (dots[h] - dot_hi.astype(F32)).astype(BF16)
        feat = jnp.where(line == 0, dot_hi, jnp.where(line == 1, dot_lo, zero))
        mine = jnp.where((line < HD) == (h == 0), do_flip, zero)
        p = p_ref[h]
        dp = dot_nn(v_wide, jnp.concatenate([mine, feat], axis=0))
        ds = (p.astype(F32) * dp).astype(BF16)
        ds_ref[h] = ds
        parts.append((dot_nn(ds, q), dot_nn(p, do)))
        dq = dot_nn(k_flip[rows_of_head(h)], ds)
        dq_flip[rows_of_head(h), :] = dq if first else dq + dq_in[rows_of_head(h), :]
        diagonal = diagonal_sums(ds_ref.at[h], nb, lane8)

        @pl.when(row == 0)
        def _():
            w_ref[h : h + 1, :] = diagonal

        @pl.when(row != 0)
        def _():
            w_ref[h : h + 1, :] += diagonal

    dk, dv = [jnp.where(low, one, two) for one, two in zip(*parts)]
    dq_ref[...] = dq_flip[...].T.astype(BF16) if last else dq_flip[...]
    dk_ref[...] = dk.astype(BF16)
    dv_ref[...] = dv.astype(BF16)


def attend_back(p, q, k, v, dctx, dots, lse, m, dq, last, start, count, after=()):
    _, rows, length, _ = q.shape
    first = dq is None

    def spec(*shape, start=start):
        return pl.BlockSpec(
            (pl.squeezed, pl.squeezed, *shape), lambda p, r: (p + start, r) + (0,) * len(shape)
        )

    blk, flip, stats = spec(length, LANES), spec(LANES, length), spec(8, length)
    out, out_flip = spec(length, LANES, start=0), spec(LANES, length, start=0)
    arrays = [p, q, k, v, dctx, dots, lse, m] + ([] if first else [dq])
    natural = shaped((count, rows, length, LANES), BF16)
    return call(
        functools.partial(attend_back_kernel, first, last),
        [
            natural if last else shaped((count, rows, LANES, length), F32),
            natural,
            natural,
            shaped((count, 2, 2 * length), F32),
        ],
        LONG if first and start == 0 else SHORT,
        after=after,
        grid=(count, rows),
        in_specs=[spec(2, length, length)]
        + [blk] * 3
        + [flip]
        + [stats] * 3
        + ([] if first else [out_flip]),
        out_specs=[out if last else out_flip, out, out]
        + [pl.BlockSpec((pl.squeezed, 2, 2 * length), lambda p, r: (p, 0, 0))],
        scratch_shapes=[
            pltpu.VMEM((2, length, length), BF16),
            pltpu.VMEM((LANES, length), F32),
        ],
    )(*arrays)


def ffn_kernel(head, *refs):
    core_ref, bo_ref, gain_ref, shift_ref, bd_ref = refs[:5]
    cot_ref, up_ref, down_ref, bias_ref, ctx_ref, wo_ref = refs[5:11]
    refs = refs[11:]
    if head:
        x_ref, res_ref, hid_ref, down_acc, hid_acc, keep_ref, send_ref, bias_grad = refs
    else:
        hid_ref, down_in, hid_in, res_ref, at_ref = refs[:5]
        mixed_ref, dres_ref, dctx_ref, dots_ref, sums_ref = refs[5:10]
        keep_ref, send_ref, bias_grad, down_acc, hid_acc = refs[10:]
    j = pl.program_id(0)

    @pl.when(j == 0)
    def _():
        if head:
            res = x_ref[...].astype(F32) + (
                dot_nn(all_pairs([ctx_ref]), wo_ref[...]) + row(bo_ref)
            )
            res_ref[...] = res
            y, _ = normalise(res)
            hid_ref[...] = (y * row(gain_ref) + row(shift_ref)).astype(BF16)
            down_acc[...] = jnp.zeros_like(down_acc)
            hid_acc[...] = jnp.zeros_like(hid_acc)
        else:
            down_acc[...] = down_in[...]
            hid_acc[...] = hid_in[...]

    hid, cot = hid_ref[...], cot_ref[...]
    up, down = up_ref[...], down_ref[...]
    pre = dot_nn(hid, up) + bias_ref[0]
    cdf = 0.5 + 0.5 * lax.erf(pre * 0.7071067811865476)
    slope = cdf + pre * (0.3989422804014327 * jnp.exp(-0.5 * pre * pre))
    act = (pre * cdf).astype(BF16)
    pre_grad = (dot_nt(cot, down) * slope).astype(BF16)
    down_acc[...] += dot_nn(act, down)
    hid_acc[...] += dot_nt(pre_grad, up)
    up_grad = dot_tn(hid, pre_grad).astype(BF16)
    down_grad = dot_tn(act, cot).astype(BF16)
    bias_grad[0] = column_sum(pre_grad.astype(F32))

    cb = up.shape[1] // LANES
    for core in range(2):

        @pl.when(core_ref[0] == core)
        def _():
            for c in range(cb):
                cols = slice(c * LANES, (c + 1) * LANES)
                (keep_ref, send_ref)[core][j * cb + c] = up_grad[:, cols]
                (send_ref, keep_ref)[core][j * cb + c] = down_grad[:, cols]

    if not head:

        @pl.when(j == pl.num_programs(0) - 1)
        def _():
            res = res_ref[...]
            cot = cot_ref[...].astype(F32)
            mixed_ref[...] = (res + (down_acc[...] + row(bd_ref))).astype(BF16)
            y, scale = normalise(res)
            dh = hid_acc[...]
            a = dh * row(gain_ref)
            dres = cot + scale * (
                a
                - jnp.mean(a, axis=-1, keepdims=True)
                - y * jnp.mean(a * y, axis=-1, keepdims=True)
            )
            dres_ref[...] = dres
            branch = dres.astype(BF16)
            dots_ref[...] = jnp.zeros_like(dots_ref)
            for p in range(dctx_ref.shape[0]):
                part = dot_nt(wo_ref[p * LANES : (p + 1) * LANES, :], branch).astype(BF16)
                dctx_ref[p] = part
                product = part.astype(F32) * at_ref[p]
                for h in range(2):
                    dots_ref[p, h : h + 1, :] = column_sum(product[rows_of_head(h)])
            sums_ref[0:1] = column_sum(dh * y)
            sums_ref[1:2] = column_sum(dh)
            sums_ref[2:3] = column_sum(branch.astype(F32))
            sums_ref[3:4] = column_sum(cot)
            out_grad = dot_tn(all_pairs([ctx_ref]), branch).astype(BF16)
            first = 2 * cb
            for at in range(first, keep_ref.shape[0]):
                if at >= first + cb // 2:
                    keep_ref[at] = jnp.zeros(keep_ref.shape[1:], BF16)
                    send_ref[at] = jnp.zeros(keep_ref.shape[1:], BF16)
                    continue
                low, high = [
                    out_grad[:, c * LANES : (c + 1) * LANES]
                    for c in (at - first, at - first + cb // 2)
                ]
                for core in range(2):

                    @pl.when(core_ref[0] == core)
                    def _():
                        (keep_ref, send_ref)[core][at] = low
                        (send_ref, keep_ref)[core][at] = high


def ffn(core, vectors, cot, up, down, bias, ctx, wo, start, steps, head=None, tail=None,
        after=()):
    rows, width = cot.shape
    once = pl.Buffered(1)
    whole = pl.BlockSpec((rows, width), lambda j: (0, 0), pipeline_mode=once)
    square = pl.BlockSpec((width, width), lambda j: (0, 0), pipeline_mode=once)
    vecs = pl.BlockSpec((8, width), lambda j: (0, 0))
    cb = width // LANES

    def pairs(*shape):
        return pl.BlockSpec((cb, *shape), lambda j: (0, 0, 0), pipeline_mode=once)

    full, half = shaped((rows, width), F32), shaped((rows, width), BF16)
    if head is not None:
        count = steps * cb
        outs, out_specs = [full, half, full, full], [whole] * 4
    else:
        count = steps * cb + cb // 2
        count += count % 2
        outs = [
            half, full, shaped((cb, LANES, rows), BF16), shaped((cb, 8, rows), F32),
            shaped((8, width), F32),
        ]
        out_specs = [whole, whole, pairs(LANES, rows), pairs(8, rows), vecs]
    extra = list(head if head is not None else tail)
    grad_spec = pl.BlockSpec((count, width, LANES), lambda j: (0, 0, 0), pipeline_mode=once)
    return call(
        functools.partial(ffn_kernel, head is not None),
        outs + [shaped((count, width, LANES), BF16)] * 2 + [shaped((steps, 1, width), F32)],
        30,
        after=after,
        vmem=56,
        grid=(steps,),
        in_specs=[
            SMEM,
            *[pl.BlockSpec((width,), lambda j: (0,))] * len(vectors),
            whole,
            pl.BlockSpec((width, width), lambda j: (0, j + start)),
            pl.BlockSpec((width, width), lambda j: (j + start, 0)),
            pl.BlockSpec((1, 1, width), lambda j: (j + start, 0, 0)),
            pairs(rows, LANES),
            square,
        ]
        + ([whole] if head is not None else [whole] * 4 + [pairs(LANES, rows)]),
        out_specs=out_specs + [grad_spec] * 2 + [pl.BlockSpec((1, 1, width), lambda j: (j, 0, 0))],
        scratch_shapes=[] if head is not None else [pltpu.VMEM((rows, width), F32)] * 2,
    )(core, *vectors, cot, up, down, bias, ctx, wo, *extra)


class Shared:
    def __init__(self, core_ref, keep_ref, send_ref):
        self.core_ref, self.refs, self.count = core_ref, (keep_ref, send_ref), 0

    def store(self, values):
        half = self.refs[0].shape[0]
        values = values.astype(BF16)
        for c in range(values.shape[1] // LANES):
            block = values[:, c * LANES : (c + 1) * LANES]
            owner, at = divmod(self.count, half)
            self.count += 1

            @pl.when(self.core_ref[0] == owner)
            def _():
                self.refs[0][at] = block

            @pl.when(self.core_ref[0] != owner)
            def _():
                self.refs[1][at] = block


def project_back_kernel(blocks, calls, *refs):
    refs = list(refs)

    def take(count):
        taken = refs[:count]
        del refs[:count]
        return taken

    core_ref, info_ref, bucket_ref, vec_ffn, *bias_grads = take(6)
    peer_sums = take(blocks - 1)
    n_refs, (x_ref,) = take(blocks), take(1)
    wq_ref, wk_ref, wv_ref = take(3)
    dq_refs = take(calls)
    dk_refs, dv_refs, w_refs = [[take(calls) for _ in range(blocks)] for _ in range(3)]
    (ng_ref,) = take(1)
    keep_ref, send_ref, small_ref = take(3)
    grads = Shared(core_ref, keep_ref, send_ref)
    dq = all_pairs(dq_refs)
    gk = gv = bias = None
    for b in range(blocks):
        dk, dv, norm = all_pairs(dk_refs[b]), all_pairs(dv_refs[b]), n_refs[b][...]
        if b == 0:
            ng = 0.125 * dot_nt(dq, wq_ref[...])
            ng = ng + dot_nt(dk, wk_ref[...]) + dot_nt(dv, wv_ref[...])
            grads.store(0.125 * dot_tn(norm, dq))
            ng_ref[...] = ng
            y, _ = normalise(x_ref[...].astype(F32))
            sums = [column_sum(ng * y), column_sum(ng)]
        k_part, v_part, b_part = dot_tn(norm, dk), dot_tn(norm, dv), column_sum(dv.astype(F32))
        gk = k_part if gk is None else gk + k_part
        gv = v_part if gv is None else gv + v_part
        bias = b_part if bias is None else bias + b_part
    for peer in peer_sums:
        sums = [mine + peer[i : i + 1] for i, mine in enumerate(sums)]
    grads.store(gk)
    grads.store(gv)
    small_ref[...] = jnp.zeros_like(small_ref)
    vectors = sums + [0.125 * column_sum(dq.astype(F32)), bias]
    vectors += [vec_ffn[i : i + 1] for i in range(4)]
    vectors += [ref[i] for ref in bias_grads for i in range(ref.shape[0])]
    at = 0
    for vec in vectors:
        for c in range(vec.shape[1] // LANES):
            small_ref[at : at + 1, :] = vec[:, c * LANES : (c + 1) * LANES]
            at += 1
    table = None
    span = w_refs[0][0].shape[2]
    for b in range(blocks):
        start = pl.multiple_of(info_ref[2 * b + 1], LANES)
        window = bucket_ref[:, pl.ds(start, span)]
        one_hot = jnp.where(
            lax.broadcasted_iota(jnp.int32, (TABLE_ROWS, span), 0) == window, 1.0, 0.0
        ).astype(BF16)
        w = jnp.concatenate([ref[p] for ref in w_refs[b] for p in range(ref.shape[0])], axis=0)
        w_hi = w.astype(BF16)
        w_lo = (w - w_hi.astype(F32)).astype(BF16)
        part = dot_nt(w_hi, one_hot) + dot_nt(w_lo, one_hot)
        table = part if table is None else table + part
    for c in range(TABLE_ROWS // LANES):
        small_ref[at : at + table.shape[0], :] = table[:, c * LANES : (c + 1) * LANES]
        at += table.shape[0]
    grads.store(small_ref[...])
    while grads.count < 2 * keep_ref.shape[0]:
        grads.store(jnp.zeros_like(small_ref))


TABLE_ROWS = 384


def project_back(core, info, bucket, vec_ffn, bias_grads, peer_sums, norms, x, weights, parts,
                 after=()):
    rows, width = norms[0].shape
    blocks = len(norms)
    whole = pl.BlockSpec(memory_space=pltpu.VMEM)
    arrays = [core, info, bucket, vec_ffn, *bias_grads, *peer_sums, *norms, x, *weights]
    arrays += [part[0].reshape(-1, rows, LANES) for part in parts[0]]
    for kind in (1, 2):
        arrays += [part[kind].reshape(-1, rows, LANES) for block in parts for part in block]
    arrays += [part[3] for block in parts for part in block]
    count = 3 * width // LANES + 1
    count += -count % 4
    ng, *grads = call(
        functools.partial(project_back_kernel, blocks, len(parts[0])),
        [shaped((rows, width), F32)] + [shaped((count // 2, width, LANES), BF16)] * 2,
        SHORT,
        after=after,
        grid=(1,),
        in_specs=[SMEM, SMEM] + [whole] * (len(arrays) - 2),
        scratch_shapes=[pltpu.VMEM((width, LANES), F32)],
    )(*arrays)
    return ng, grads


def peer_back_kernel(calls, *refs):
    x_ref, wk_ref, wv_ref = refs[:3]
    dk_refs, dv_refs = refs[3 : 3 + calls], refs[3 + calls : 3 + 2 * calls]
    ng_ref, sums_ref = refs[3 + 2 * calls :]
    dk, dv = all_pairs(dk_refs), all_pairs(dv_refs)
    ng = dot_nt(dk, wk_ref[...]) + dot_nt(dv, wv_ref[...])
    ng_ref[...] = ng.astype(BF16)
    y, _ = normalise(x_ref[...].astype(F32))
    sums_ref[0:1] = column_sum(ng * y)
    sums_ref[1:2] = column_sum(ng)


def peer_back(x, weights, parts, after=()):
    rows, width = x.shape
    arrays = [x, *weights[1:]]
    for kind in (1, 2):
        arrays += [part[kind].reshape(-1, rows, LANES) for part in parts]
    return call(
        functools.partial(peer_back_kernel, len(parts)),
        [shaped((rows, width), BF16), shaped((8, width), F32)],
        SHORT,
        after=after,
        grid=(1,),
        in_specs=[IN_VMEM] * len(arrays),
    )(*arrays)


def frames_back_kernel(count, *refs):
    x_ref, gain_ref, dres_ref, ng_ref = refs[:4]
    out_ref = refs[-1]
    y, scale = normalise(x_ref[...].astype(F32))
    ng = ng_ref[...]
    for other in refs[4 : 4 + count]:
        ng = ng + other[...].astype(F32)
    a = ng * row(gain_ref)
    out_ref[...] = dres_ref[...] + scale * (
        a - jnp.mean(a, axis=-1, keepdims=True) - y * jnp.mean(a * y, axis=-1, keepdims=True)
    )


def frames_back(x, gain, dres, ng, others, after=()):
    rows, width = x.shape
    tile = 128
    blk = pl.BlockSpec((tile, width), lambda i: (i, 0))
    vec = pl.BlockSpec((width,), lambda i: (0,))
    return call(
        functools.partial(frames_back_kernel, len(others)),
        shaped((rows, width), F32),
        4,
        after=after,
        grid=(rows // tile,),
        in_specs=[blk, vec, blk, blk] + [blk] * len(others),
        out_specs=blk,
    )(x, gain, dres, ng, *others)


def swap(x, bit):
    axis, mask = bit
    if isinstance(mask, int):
        mask = [(i, i ^ mask) for i in range(lax.axis_size(axis))]
    return lax.ppermute(x, axis, mask)


def side(bit):
    axis, mask = bit
    return ((lax.axis_index(axis) & mask) != 0).astype(jnp.int32)


CORE, ALONG, NEAR, FAR, ACROSS = ("batch", 1), ("batch", 2), ("batch", 4), ("batch", 8), ("blk", 1)

def local(kernel, sides, arrays, shapes, time=0.01):
    return pl.pallas_call(
        kernel,
        out_shape=[shaped(shape, BF16) for shape in shapes],
        in_specs=[SMEM] + [IN_VMEM] * len(arrays),
        out_specs=[IN_VMEM] * len(shapes),
        compiler_params=pltpu.CompilerParams(vmem_limit_bytes=4 * 1024 * 1024),
        cost_estimate=cost_of(time),
    )(sides, *arrays)


def both_halves(size, at):
    return [pl.ds(pl.multiple_of(k * size, 16), size) for k in (1 - at, at)]


def add(a, b):
    return (a.astype(F32) + b.astype(F32)).astype(BF16)


def sum_over_devices(keep, send, time):
    n, rows, _ = keep.shape
    half = n // 2
    x, y, z, w = range(4)
    sides = jnp.stack([side(bit) for bit in (ACROSS, ALONG, NEAR, FAR)])
    (got,) = yield [(send, CORE)]

    def first(s, keep, got, send_a, keep_a, send_b, keep_b):
        for k, bit, outs in ((0, x, (send_a, keep_a)), (1, y, (send_b, keep_b))):
            block = slice(k * half, (k + 1) * half)
            for rows_at, out in zip(both_halves(rows // 2, s[bit]), outs):
                out[...] = add(keep[block, rows_at, :], got[block, rows_at, :])

    shape = (half, rows // 2, LANES)
    send_a, keep_a, send_b, keep_b = local(first, sides, [keep, got], [shape] * 4)
    got_a, got_b = yield [(send_a, ACROSS), (send_b, ALONG)]

    def second(s, keep_a, got_a, keep_b, got_b, *outs):
        for k, bit, keep, got in ((0, y, keep_a, got_a), (1, x, keep_b, got_b)):
            for rows_at, out in zip(both_halves(rows // 4, s[bit]), outs[2 * k : 2 * k + 2]):
                out[...] = add(keep[:, rows_at, :], got[:, rows_at, :])

    shape = (half, rows // 4, LANES)
    send_a, keep_a, send_b, keep_b = local(
        second, sides, [keep_a, got_a, keep_b, got_b], [shape] * 4, time
    )
    got_a, got_b = yield [(send_a, ALONG), (send_b, ACROSS)]

    def third(s, keep_a, got_a, keep_b, got_b, *outs):
        for k, keep, got in ((0, keep_a, got_a), (1, keep_b, got_b)):
            for rows_at, out in zip(both_halves(rows // 8, s[z]), outs):
                out[k * half : (k + 1) * half] = add(keep[:, rows_at, :], got[:, rows_at, :])

    shape = (n, rows // 8, LANES)
    send, keep = local(third, sides, [keep_a, got_a, keep_b, got_b], [shape] * 2)
    (got,) = yield [(send, NEAR)]

    def fourth(s, keep, got, *outs):
        for rows_at, out in zip(both_halves(rows // 16, s[w]), outs):
            out[...] = add(keep[:, rows_at, :], got[:, rows_at, :])

    shape = (n, rows // 16, LANES)
    send, keep = local(fourth, sides, [keep, got], [shape] * 2)
    (got,) = yield [(send, FAR)]

    def fifth(s, keep, got, out):
        out[...] = add(keep[...], got[...])

    (held,) = local(fifth, sides, [keep, got], [shape])
    (got,) = yield [(held, FAR)]

    def join_far(s, held, got, out):
        for rows_at, ref in zip(both_halves(rows // 16, s[w]), (got, held)):
            out[:, rows_at, :] = ref[...]

    (held,) = local(join_far, sides, [held, got], [(n, rows // 8, LANES)])
    (got,) = yield [(held, NEAR)]

    def join_near(s, held, got, *outs):
        for k, out in enumerate(outs):
            for rows_at, ref in zip(both_halves(rows // 8, s[z]), (got, held)):
                out[:, rows_at, :] = ref[k * half : (k + 1) * half]

    held_a, held_b = local(join_near, sides, [held, got], [(half, rows // 4, LANES)] * 2)
    got_a, got_b = yield [(held_a, ALONG), (held_b, ACROSS)]

    def join_second(s, held_a, got_a, held_b, got_b, *outs):
        for bit, held, got, out in ((y, held_a, got_a, outs[0]), (x, held_b, got_b, outs[1])):
            for rows_at, ref in zip(both_halves(rows // 4, s[bit]), (got, held)):
                out[:, rows_at, :] = ref[...]

    held_a, held_b = local(
        join_second, sides, [held_a, got_a, held_b, got_b], [(half, rows // 2, LANES)] * 2
    )
    got_a, got_b = yield [(held_a, ACROSS), (held_b, ALONG)]

    def join_first(s, held_a, got_a, held_b, got_b, out):
        for k, bit, held, got in ((0, x, held_a, got_a), (1, y, held_b, got_b)):
            for rows_at, ref in zip(both_halves(rows // 2, s[bit]), (got, held)):
                out[k * half : (k + 1) * half, rows_at, :] = ref[...]

    (held,) = local(join_first, sides, [held_a, got_a, held_b, got_b], [(n, rows, LANES)])
    (got,) = yield [(held, CORE)]
    return held, got


def sum_plainly(keep, send, time):
    low = side(CORE) == 0
    first, second = [
        lax.psum(jnp.where(low, *pair), ("batch", "blk")) for pair in ((keep, send), (send, keep))
    ]
    yield [(first[:1, :8], CORE)]
    return jnp.where(low, first, second), jnp.where(low, second, first)


def send_back(x, b):
    blocks = lax.axis_size("blk")
    (got,) = yield [(x, ("blk", [(i, (i + b) % blocks) for i in range(blocks)]))]
    return got


def summed(keep, send, time=0.01):
    fits = lax.axis_size("blk") == 2 and lax.axis_size("batch") == 16
    return (sum_over_devices if fits else sum_plainly)(keep, send, time)


class Flow:
    def __init__(self, steps):
        self.steps = steps
        self.result = None
        self.take(next(steps))

    def take(self, pending):
        self.arrays = [array for array, _ in pending]
        self.got = [swap(array, bit) for array, bit in pending]

    def land(self, last):
        if self.result is not None:
            return last
        *got, _ = lax.optimization_barrier([*self.got, last])
        try:
            self.take(self.steps.send(got))
            return self.arrays[0]
        except StopIteration as end:
            self.arrays, self.result = [], end.value
            return jax.tree.leaves(end.value)[0]


class Order:
    def __init__(self, last):
        self.last = last
        self.flows = {}
        self.fresh = []

    def add(self, name, steps):
        self.flows[name] = Flow(steps)
        self.fresh += self.flows[name].arrays

    def kernel(self, run):
        result = run([self.last, *self.fresh])
        self.fresh = []
        self.last = jax.tree.leaves(result)[-1]
        return result

    def land(self, *names):
        for name in names:
            self.last = self.flows[name].land(self.last)
            self.fresh += self.flows[name].arrays

    def result(self, name):
        while self.flows[name].result is None:
            self.land(name)
        return self.flows[name].result


def place_kernel(plan, tile, core_ref, *refs):
    ins = refs[: 2 * (1 + max(step[0] for step in plan))]
    outs = refs[len(ins) :]
    rows = pl.ds(pl.multiple_of(pl.program_id(0) * tile, 16), tile)
    for core in range(2):

        @pl.when(core_ref[0] == core)
        def _():
            for source, half, column, out, slot, at in plan:
                x = ins[2 * source + (half ^ core)][column, rows, :].astype(F32)
                cols = slice(at * LANES, (at + 1) * LANES)
                if slot is None:
                    outs[out][:, cols] = x
                else:
                    outs[out][slot, :, cols] = x


def place(core, sums, plan, out_shapes, after=()):
    halves = [half for pair in sums for half in pair]
    tile = 96
    out_specs = []
    for shape in out_shapes:
        if len(shape) == 2:
            out_specs.append(pl.BlockSpec((tile, shape[1]), lambda i: (i, 0)))
        else:
            out_specs.append(pl.BlockSpec((shape[0], tile, shape[2]), lambda i: (0, i, 0)))
    return call(
        functools.partial(place_kernel, plan, tile),
        [shaped(shape, F32) for shape in out_shapes],
        7,
        after=after,
        grid=(halves[0].shape[1] // tile,),
        in_specs=[SMEM] + [IN_VMEM] * len(halves),
        out_specs=out_specs,
    )(core, *halves)


def per_device(
    frames,
    cotangent,
    query_weight,
    key_weight,
    value_weight,
    output_weight,
    up_weight,
    down_weight,
    attn_gain,
    attn_shift,
    query_bias,
    value_bias,
    output_bias,
    ffn_gain,
    ffn_shift,
    up_bias,
    down_bias,
    rel_table,
    utt_lengths,
    frame_mask,
    rel_bucket,
):
    rows_n, length, width = frames.shape
    blocks = lax.axis_size("blk")
    seq = length * blocks
    me = lax.axis_index("blk")
    rows = rows_n * length
    units = up_weight.shape[1]
    steps = units // width
    heads = rel_table.shape[1]
    buckets = rel_table.shape[0]
    core = side(CORE).reshape(1)
    weights = (query_weight, key_weight, value_weight)

    def from_peer(x, b):
        return lax.ppermute(x, "blk", [((i + b) % blocks, i) for i in range(blocks)])

    def split(x):
        return x.reshape(x.shape[0], rows_n, length, x.shape[2])

    def split_flip(x):
        return jnp.swapaxes(x.reshape(*x.shape[:2], rows_n, length), 1, 2)

    def join_flip(x):
        return jnp.swapaxes(x, 1, 2).reshape(x.shape[0], x.shape[2], rows)

    def flat(x):
        return x.reshape(rows, x.shape[-1])

    flat_frames = flat(frames)
    x_blocks = [flat_frames] + [from_peer(flat_frames, b) for b in range(1, blocks)]
    masks = [frame_mask] + [from_peer(frame_mask, b) for b in range(1, blocks)]
    starts = [((me + b) % blocks) * length for b in range(blocks)]
    info = jnp.stack(
        [x for start in starts for x in (start, seq - length + starts[0] - start)]
    ).astype(jnp.int32)
    bucket = jnp.concatenate([jnp.full((1,), -1, jnp.int32), rel_bucket]).reshape(1, -1)
    norms, keys, values, probs, tops = [], [], [], [], []
    state = None
    for b in range(blocks):
        last = b == blocks - 1
        norm, key_feat, window, *rest = project(
            info, utt_lengths, x_blocks[b], (attn_gain, attn_shift), masks[b], bucket, rel_table.T,
            weights[1:] if b else weights, (value_bias,) if b else (query_bias, value_bias), b,
        )
        if b == 0:
            query_feat, query, key, value = rest
            query = split(query)
        else:
            key, value = rest
        norms.append(norm)
        keys.append(split(key))
        values.append(split(value))
        p, m, out, stats, *context = attend(
            query, keys[b], values[b], query_feat, key_feat, window, state, last
        )
        probs.append(p)
        tops.append(m)
        state = (out, stats)

    attended, lse = state
    context = context[0].reshape(heads // 2, rows, LANES)
    cot = flat(cotangent)
    dense = (
        core, (output_bias, ffn_gain, ffn_shift, down_bias), cot, up_weight, down_weight,
        up_bias.reshape(steps, 1, width), context, output_weight,
    )
    half = steps // 2
    res, hid, *carry, keep, send, bias_one = ffn(*dense, 0, half, head=(flat_frames,))
    order = Order(bias_one)
    order.add("one", summed(keep, send))
    mixed, dres, dctx, dots, vec_ffn, keep, send, bias_two = order.kernel(
        lambda after: ffn(
            *dense, half, steps - half, tail=(hid, *carry, res, join_flip(attended)), after=after
        )
    )
    order.add("two", summed(keep, send, LONG))
    order.land("one")

    dctx, dots = split_flip(dctx), split_flip(dots)
    pairs = heads // 2
    half_pairs = pairs // 2
    parts = [[] for _ in range(blocks)]
    peer_sums, peer_ngs = [], []
    dqs = [None, None]
    for b in [*range(1, blocks), 0]:
        for i in range(2):

            def run(after):
                return attend_back(
                    probs[b], query, keys[b], values[b], dctx, dots, lse, tops[b], dqs[i], b == 0,
                    i * half_pairs, (half_pairs, pairs - half_pairs)[i], after=after,
                )

            parts[b].append(order.kernel(run))
            dqs[i] = parts[b][-1][0]
            if b == 1 and i == 0:
                order.land("two")
        if b:
            ng, peer_sum = order.kernel(
                lambda after: peer_back(x_blocks[b], weights, parts[b], after=after)
            )
            peer_sums.append(peer_sum)
            peer_ngs.append(ng)
        if b == 1:
            order.land("one")
    own_ng, shared = order.kernel(
        lambda after: project_back(
            core, info, bucket, vec_ffn, (bias_one, bias_two), peer_sums, norms, flat_frames,
            weights, parts, after=after,
        )
    )
    order.add("three", summed(*shared))
    for b, ng in enumerate(peer_ngs, 1):
        order.add(b, send_back(ng, b))
    order.land("one", "two", "three", "one", "one", "two", "one", *range(1, blocks))
    frames_grad = order.kernel(
        lambda after: frames_back(
            flat_frames, attn_gain, dres, own_ng, [order.result(b) for b in range(1, blocks)],
            after=after,
        )
    )
    order.land(
        "three", "two", "one", "three", "two", "one", "three", "two", "three", "one", "two",
        "three", "one", "three", "two", "three", "two", "two", "three",
    )
    sums = [order.result("one"), order.result("two")]

    cb = width // LANES
    plan = []
    for chunk in range(steps):
        which, first = divmod(chunk, half)
        for c in range(cb):
            column = first * cb + c
            plan.append((which, 0, column, 0, None, chunk * cb + c))
            plan.append((which, 1, column, 1, chunk, c))
    for c in range(cb):
        plan.append((1, c // (cb // 2), 2 * cb + c % (cb // 2), 2, None, c))
    shapes = [(width, units), (steps, width, width), (width, width)]
    up_total, down_total, output_total = order.kernel(
        lambda after: place(core, sums, plan, shapes, after=after)
    )
    last_sum = order.result("three")
    last_half = last_sum[0].shape[0]
    plan = [
        (0, n // last_half, n % last_half, n // cb, None, n % cb) for n in range(3 * cb + 1)
    ]
    query_total, key_total, value_total, small = place(
        core, [last_sum], plan, [(width, width)] * 3 + [(width, LANES)]
    )
    flat_small = small[: (8 + steps) * cb].reshape(-1, width)
    table_rows = small[(8 + steps) * cb : (8 + steps) * cb + heads * TABLE_ROWS // LANES]
    table_total = jnp.concatenate(
        [table_rows[i : i + heads] for i in range(0, table_rows.shape[0], heads)], axis=1
    )[:, :buckets].T
    return (
        mixed.reshape(frames.shape),
        frames_grad.reshape(frames.shape),
        query_total,
        key_total,
        value_total,
        output_total,
        up_total,
        down_total.reshape(units, width),
        flat_small[0],
        flat_small[1],
        flat_small[2],
        flat_small[3],
        flat_small[6],
        flat_small[4],
        flat_small[5],
        flat_small[8:].reshape(units),
        flat_small[7],
        table_total,
    )


def solution(mesh):
    batch3 = P("batch", "blk", None)
    in_specs = (batch3, batch3) + (P(),) * 16 + (P("batch", None), P("batch", "blk"), P())
    out_specs = (batch3, batch3) + (P(),) * 16
    return jax.shard_map(
        per_device, mesh=mesh, in_specs=in_specs, out_specs=out_specs, check_vma=False
    )
```

```python
import functools

import jax
import jax.numpy as jnp
from jax import lax
from jax.experimental import pallas as pl
from jax.experimental.pallas import tpu as pltpu
from jax.sharding import PartitionSpec as P

HD = 64
LANES = 128
EPSILON = 1e-05
MASKED = -1e30
BF16 = jnp.bfloat16
F32 = jnp.float32
COST = 1
SHORT, LONG = 0.05, 1000
LANDINGS = (
    "one", "two", "three", "one", "one", "two", "one", "three", "send_peers", "two", "one",
    "three", "two", "one", "three", "two", "peers", "frames", "three", "one", "two", "three",
    "one", "three", "two", "three", "two", "two", "place", "three", "three",
)
HIGHEST = lax.Precision.HIGHEST


def dot_nn(a, b):
    return lax.dot_general(a, b, (((1,), (0,)), ((), ())), preferred_element_type=F32)


def dot_nt(a, b):
    return lax.dot_general(a, b, (((1,), (1,)), ((), ())), preferred_element_type=F32)


def dot_tn(a, b):
    return lax.dot_general(a, b, (((0,), (0,)), ((), ())), preferred_element_type=F32)


def normalise(values):
    centre = values - jnp.mean(values, axis=-1, keepdims=True)
    scale = lax.rsqrt(jnp.mean(centre * centre, axis=-1, keepdims=True) + EPSILON)
    return centre * scale, scale


def column_sum(values):
    return jnp.sum(values, axis=0, keepdims=True)


def cost_of(time):
    return pl.CostEstimate(
        flops=int(time * COST * 1.1e9), bytes_accessed=int(time * COST * 3e6), transcendentals=0
    )


def call(kernel, out_shape, time, after=(), vmem=32, **kw):
    skip = len(after)

    def run(*refs):
        kernel(*refs[skip:])

    kw["in_specs"] = [pl.BlockSpec(memory_space=pl.ANY)] * skip + list(kw["in_specs"])
    program = pl.pallas_call(
        run,
        out_shape=out_shape,
        compiler_params=pltpu.CompilerParams(vmem_limit_bytes=vmem * 1024 * 1024),
        cost_estimate=cost_of(time),
        **kw,
    )
    return lambda *arrays: program(*after, *arrays)


SMEM = pl.BlockSpec(memory_space=pltpu.SMEM)
IN_VMEM = pl.BlockSpec(memory_space=pltpu.VMEM)


def shaped(shape, dtype):
    return jax.ShapeDtypeStruct(shape, dtype)


def row(ref):
    return ref[...].reshape(1, ref.shape[0])


def store_pairs(ref, values):
    for p in range(values.shape[1] // LANES):
        ref[p] = values[:, p * LANES : (p + 1) * LANES].astype(ref.dtype)


def all_pairs(refs):
    return jnp.concatenate([ref[p] for ref in refs for p in range(ref.shape[0])], axis=1)


def project_kernel(own, where, *refs):
    refs = list(refs)
    info_ref, lengths_ref, x_ref, gain_ref, shift_ref, mask_ref, bucket_ref, table_ref = refs[:8]
    refs = refs[8:]
    if own:
        bq_ref = refs.pop(0)
    bv_ref = refs.pop(0)
    if own:
        wq_ref, wk_ref, wv_ref, n_ref, kf_ref, win_ref, qf_ref, q_ref, k_ref, v_ref, norm = refs
    else:
        wk_ref, wv_ref, n_ref, kf_ref, win_ref, k_ref, v_ref, norm = refs
    rows_n, length, _ = kf_ref.shape

    @pl.when(pl.program_id(0) == 0)
    def _():
        y, _ = normalise(x_ref[...].astype(F32))
        norm[...] = (y * row(gain_ref) + row(shift_ref)).astype(BF16)
        n_ref[...] = norm[...]
        count = lengths_ref.shape[1]
        lane_row = lax.broadcasted_iota(jnp.int32, (1, LANES), 1)
        lane = lax.broadcasted_iota(jnp.int32, (length, LANES), 1)
        pos = info_ref[2 * where] + lax.broadcasted_iota(jnp.int32, (length, LANES), 0)
        for r in range(rows_n):
            end = jnp.int32(0)
            begins = jnp.zeros((1, LANES), jnp.int32)
            ends = jnp.zeros((1, LANES), jnp.int32)
            for u in range(count):
                begin, end = end, end + lengths_ref[r, u]
                begins = jnp.where(lane_row == u, begin, begins)
                ends = jnp.where(lane_row == u, end, ends)
            inside = (pos >= begins) & (pos < ends)
            seen = jnp.broadcast_to(mask_ref[r : r + 1, :].astype(F32), (LANES, length)).T > 0.5
            free = (lane >= count) | (inside & seen)
            kf_ref[r] = jnp.where(free, 0.0, MASKED).astype(BF16)
            if own:
                qf_ref[r] = jnp.where(inside, 1.0, 0.0).astype(BF16)
        buckets = table_ref.shape[1]
        at = pl.multiple_of(info_ref[2 * where + 1], LANES)
        window = bucket_ref[:, pl.ds(at, 2 * length)]
        one_hot = jnp.where(
            lax.broadcasted_iota(jnp.int32, (buckets, 2 * length), 0) == window, 1.0, 0.0
        ).astype(BF16)
        rest = table_ref[...]
        bias = None
        for _ in range(3):
            part = rest.astype(BF16)
            rest = rest - part.astype(F32)
            product = dot_nn(part, one_hot)
            bias = product if bias is None else bias + product
        for p in range(win_ref.shape[0]):
            win_ref[p] = bias[2 * p : 2 * p + 2]

    x = norm[...]
    if own:
        store_pairs(q_ref, (dot_nn(x, wq_ref[...]) + row(bq_ref)) * 0.125)
    store_pairs(k_ref, dot_nn(x, wk_ref[...]))
    store_pairs(v_ref, dot_nn(x, wv_ref[...]) + row(bv_ref))


def project(info, lengths, x, norm, mask, bucket, table, weights, biases, where, after=()):
    rows, width = x.shape
    rows_n, length = mask.shape
    pairs = table.shape[0] // 2
    cols = 256
    own = len(weights) == 3
    whole = pl.BlockSpec((rows, width), lambda j: (0, 0))
    part = pl.BlockSpec((width, cols), lambda j: (0, j))
    out = pl.BlockSpec((cols // LANES, rows, LANES), lambda j: (j, 0, 0))
    feat = pl.BlockSpec((rows_n, length, LANES), lambda j: (0, 0, 0))

    def fixed(array):
        return pl.BlockSpec(array.shape, lambda j: (0,) * array.ndim)

    count = len(weights)
    features = shaped((rows_n, length, LANES), BF16)
    window = shaped((pairs, 2, 2 * length), F32)
    return call(
        functools.partial(project_kernel, own, where),
        [shaped((rows, width), BF16), features, window]
        + [features] * own
        + [shaped((pairs, rows, LANES), BF16)] * count,
        5,
        after=after,
        vmem=56,
        grid=(width // cols,),
        in_specs=[SMEM, SMEM, whole, fixed(norm[0]), fixed(norm[1])]
        + [fixed(mask), fixed(bucket), fixed(table)]
        + [pl.BlockSpec((cols,), lambda j: (j,))] * len(biases)
        + [part] * count,
        out_specs=[whole, feat, fixed(window)] + [feat] * own + [out] * count,
        scratch_shapes=[pltpu.VMEM((rows, width), BF16)],
    )(info, lengths, x, *norm, mask, bucket, table, *biases, *weights)


def rows_of_head(h):
    return slice(h * HD, (h + 1) * HD)


def attend_kernel(own, last, chunk, *refs):
    refs = list(refs)
    q_ref, k_ref, v_ref, qf_ref, kf_ref, w_ref = refs[:6]
    refs = refs[6:]
    if not own:
        o_in, stats_in = refs[:2]
        refs = refs[2:]
    p_ref, m_ref, o_ref, stats_ref = refs[:4]
    cx_ref = refs[4] if last else None
    t_refs = refs[-2:]
    length = q_ref.shape[0]
    nb = length // LANES
    q = q_ref[...]
    k = k_ref[...]
    lane = lax.broadcasted_iota(jnp.int32, (length, LANES), 1)
    k_wide = jnp.concatenate([k, kf_ref[...]], axis=1)
    v_flip = v_ref[...].T
    ones = jnp.ones((16, length), BF16)
    eye = lax.broadcasted_iota(jnp.int32, (LANES, LANES), 0) == lax.broadcasted_iota(
        jnp.int32, (LANES, LANES), 1
    )
    zero = jnp.zeros((), BF16)
    for h in range(2):
        t_ref = t_refs[h]
        for a in range(2 * nb - 1):
            x = w_ref[h : h + 1, 2 * length - 256 - 128 * a : 2 * length - 128 * a]
            t = pltpu.roll(jnp.broadcast_to(x, (LANES, 256)), 0, 1, stride=1, stride_axis=0)
            t_ref[128 * a : 128 * a + 128, :] = t[:, LANES:]
        q_head = jnp.where((lane < HD) == (h == 0), q, zero)
        q_wide = jnp.concatenate([q_head, qf_ref[...]], axis=1)
        v_head = jnp.concatenate([v_flip[rows_of_head(h)], ones], axis=0)
        sums, tops = [], []
        for c in range(0, length, chunk):
            s = dot_nt(k_wide, q_wide[c : c + chunk])
            weights = []
            for i in range(c // LANES, (c + chunk) // LANES):
                first = 128 * (nb - 1 - i)
                here = slice(128 * i, 128 * i + 128)
                tile = s[:, 128 * i - c : 128 * i - c + 128] + t_ref[first : first + length, :]
                if own:
                    plain = dot_nt(k[here], q_head[here]) + t_ref[128 * (nb - 1) : 128 * nb, :]
                    fixed = jnp.where(eye, plain, tile[here])
                    around = [tile[: 128 * i], fixed, tile[128 * i + 128 :]]
                    tile = jnp.concatenate([x for x in around if x.shape[0]], axis=0)
                top = jnp.max(tile, axis=0, keepdims=True)
                weight = jnp.exp(tile - top).astype(BF16)
                p_ref[h, :, here] = weight
                weights.append(weight)
                tops.append(top)
            sums.append(dot_nn(v_head, jnp.concatenate(weights, axis=1)))
        o = jnp.concatenate(sums, axis=1)
        m = jnp.concatenate(tops, axis=1)
        o, l = o[:HD], o[HD : HD + 1]
        m_ref[h : h + 1, :] = m
        if not own:
            m_old = stats_in[h : h + 1, :]
            m_new = jnp.maximum(m_old, m)
            old, new = jnp.exp(m_old - m_new), jnp.exp(m - m_new)
            o = o_in[rows_of_head(h), :] * old + o * new
            l = stats_in[2 + h : 3 + h, :] * old + l * new
            m = m_new
        if last:
            o = o / l
            m = m + jnp.log(l)
        o_ref[rows_of_head(h), :] = o
        stats_ref[h : h + 1, :] = m
        stats_ref[2 + h : 3 + h, :] = l
    if last:
        cx_ref[...] = o_ref[...].T.astype(BF16)


def attend(q, k, v, qf, kf, window, state, last, chunk=256):
    pairs, rows, length, _ = q.shape
    nb = length // LANES
    own = state is None

    def spec(*shape):
        return pl.BlockSpec((pl.squeezed, pl.squeezed, *shape), lambda p, r: (p, r) + (0,) * len(shape))

    blk, flip, stats = spec(length, LANES), spec(LANES, length), spec(8, length)
    feat = pl.BlockSpec((pl.squeezed, length, LANES), lambda p, r: (r, 0, 0))
    stats_shape = shaped((pairs, rows, 8, length), F32)
    outs = [
        shaped((pairs, rows, 2, length, length), BF16),
        stats_shape,
        shaped((pairs, rows, LANES, length), F32),
        stats_shape,
    ] + [shaped((pairs, rows, length, LANES), BF16)] * last
    return call(
        functools.partial(attend_kernel, own, last, min(chunk, length)),
        outs,
        12,
        vmem=56,
        grid=(pairs, rows),
        in_specs=[blk] * 3
        + [feat] * 2
        + [pl.BlockSpec((pl.squeezed, 2, 2 * length), lambda p, r: (p, 0, 0))]
        + ([] if own else [flip, stats]),
        out_specs=[spec(2, length, length), stats, flip, stats] + [blk] * last,
        scratch_shapes=[pltpu.VMEM(((2 * nb - 1) * LANES, LANES), F32)] * 2,
    )(q, k, v, qf, kf, window, *([] if own else state))


def diagonal_sums(ds_ref, nb, lane8):
    length = nb * LANES
    tops, lows = [], []
    for a in range(2 * nb - 1):
        total = None
        for j in range(nb):
            i0 = 128 * (a - (nb - 1) + j)
            if 0 <= i0 < length:
                x = ds_ref[i0 : i0 + 128, 128 * j : 128 * j + 128].astype(F32)
                total = x if total is None else total + x
        whole, top = total[:8], total[:8]
        for g in range(1, 16):
            x = pltpu.roll(total[8 * g : 8 * g + 8], 128 - 8 * g, 1)
            whole = whole + x
            top = top + jnp.where(lane8 < 128 - 8 * g, x, 0.0)
        tops.append(top)
        lows.append(whole - top)
    pieces = []
    for g in range(2 * nb):
        a = 2 * nb - 1 - g
        if a == 2 * nb - 1:
            pieces.append(lows[a - 1])
        elif a == 0:
            pieces.append(tops[a])
        else:
            pieces.append(tops[a] + lows[a - 1])
    z = jnp.concatenate(pieces, axis=1)
    sub = lax.broadcasted_iota(jnp.int32, z.shape, 0)
    for bit in (1, 2, 4):
        z = jnp.where((sub & bit) != 0, pltpu.roll(z, 2 * length - bit, 1), z)
    return column_sum(z)


def attend_back_kernel(first, last, *refs):
    refs = list(refs)
    p_ref, q_ref, k_ref, v_ref, dc_ref, dot_ref, lse_ref, m_ref = refs[:8]
    refs = refs[8:]
    dq_in = None if first else refs.pop(0)
    dq_ref, dk_ref, dv_ref, w_ref, ds_ref, dq_flip = refs
    length = q_ref.shape[0]
    nb = length // LANES
    q, k, v = q_ref[...], k_ref[...], v_ref[...]
    lane = lax.broadcasted_iota(jnp.int32, (length, LANES), 1)
    line = lax.broadcasted_iota(jnp.int32, (LANES, length), 0)
    lane8 = lax.broadcasted_iota(jnp.int32, (8, LANES), 1)
    low = lane < HD
    zero = jnp.zeros((), BF16)
    k_flip = k.T
    v_wide = jnp.concatenate([v, jnp.where(lane < 2, -1.0, 0.0).astype(BF16)], axis=1)
    scaled, dots = [], []
    for h in range(2):
        factor = jnp.exp(m_ref[h : h + 1, :] - lse_ref[h : h + 1, :])
        scaled.append((dc_ref[rows_of_head(h), :].astype(F32) * factor).astype(BF16))
        dots.append(dot_ref[h : h + 1, :] * factor)
    do_flip = jnp.concatenate(scaled, axis=0)
    do = do_flip.T
    row = pl.program_id(1)
    parts = []
    for h in range(2):
        dot_hi = dots[h].astype(BF16)
        dot_lo = (dots[h] - dot_hi.astype(F32)).astype(BF16)
        feat = jnp.where(line == 0, dot_hi, jnp.where(line == 1, dot_lo, zero))
        mine = jnp.where((line < HD) == (h == 0), do_flip, zero)
        p = p_ref[h]
        dp = dot_nn(v_wide, jnp.concatenate([mine, feat], axis=0))
        ds = (p.astype(F32) * dp).astype(BF16)
        ds_ref[h] = ds
        parts.append((dot_nn(ds, q), dot_nn(p, do)))
        dq = dot_nn(k_flip[rows_of_head(h)], ds)
        dq_flip[rows_of_head(h), :] = dq if first else dq + dq_in[rows_of_head(h), :]
        diagonal = diagonal_sums(ds_ref.at[h], nb, lane8)

        @pl.when(row == 0)
        def _():
            w_ref[h : h + 1, :] = diagonal

        @pl.when(row != 0)
        def _():
            w_ref[h : h + 1, :] += diagonal

    dk, dv = [jnp.where(low, one, two) for one, two in zip(*parts)]
    dq_ref[...] = dq_flip[...].T.astype(BF16) if last else dq_flip[...]
    dk_ref[...] = dk.astype(BF16)
    dv_ref[...] = dv.astype(BF16)


def attend_back(p, q, k, v, dctx, dots, lse, m, dq, last, start, count, after=()):
    _, rows, length, _ = q.shape
    first = dq is None

    def spec(*shape, start=start):
        return pl.BlockSpec(
            (pl.squeezed, pl.squeezed, *shape), lambda p, r: (p + start, r) + (0,) * len(shape)
        )

    blk, flip, stats = spec(length, LANES), spec(LANES, length), spec(8, length)
    out, out_flip = spec(length, LANES, start=0), spec(LANES, length, start=0)
    arrays = [p, q, k, v, dctx, dots, lse, m] + ([] if first else [dq])
    natural = shaped((count, rows, length, LANES), BF16)
    return call(
        functools.partial(attend_back_kernel, first, last),
        [
            natural if last else shaped((count, rows, LANES, length), F32),
            natural,
            natural,
            shaped((count, 2, 2 * length), F32),
        ],
        LONG if first and start == 0 else SHORT,
        after=after,
        grid=(count, rows),
        in_specs=[spec(2, length, length)]
        + [blk] * 3
        + [flip]
        + [stats] * 3
        + ([] if first else [out_flip]),
        out_specs=[out if last else out_flip, out, out]
        + [pl.BlockSpec((pl.squeezed, 2, 2 * length), lambda p, r: (p, 0, 0))],
        scratch_shapes=[
            pltpu.VMEM((2, length, length), BF16),
            pltpu.VMEM((LANES, length), F32),
        ],
    )(*arrays)


def ffn_kernel(head, *refs):
    core_ref, bo_ref, gain_ref, shift_ref, bd_ref = refs[:5]
    cot_ref, up_ref, down_ref, bias_ref, ctx_in, wo_in = refs[5:11]
    refs = refs[11:]
    if head:
        x_ref, res_out, hid_out, down_acc, hid_acc, keep_out, send_out, bias_grad = refs[:8]
        res_ref, hid_ref, keep_ref, send_ref, sems, more_sems = refs[8:]
        ctx_ref, wo_ref = ctx_in, wo_in
        later = [(res_ref, res_out), (hid_ref, hid_out)]
    else:
        hid_ref, down_in, hid_in, res_in, at_in = refs[:5]
        mixed_ref, dres_ref, dctx_ref, dots_ref, sums_ref = refs[5:10]
        keep_out, send_out, bias_grad, keep_ref, send_ref, sems, more_sems = refs[10:17]
        ctx_ref, wo_ref, down_first, hid_first, res_ref, at_ref, down_acc, hid_acc = refs[17:]
        early = [
            (ctx_in, ctx_ref), (wo_in, wo_ref), (down_in, down_first), (hid_in, hid_first),
            (res_in, res_ref), (at_in, at_ref),
        ]
    j = pl.program_id(0)
    steps = pl.num_programs(0)
    cb = up_ref.shape[1] // LANES

    def moves(pairs):
        return [
            pltpu.make_async_copy(src, dst, more_sems.at[i]) for i, (src, dst) in enumerate(pairs)
        ]

    def part(at, count, index):
        here = pl.ds(at, count)
        return [
            pltpu.make_async_copy(src.at[here], dst.at[here], sems.at[k, index])
            for k, (src, dst) in enumerate(((keep_ref, keep_out), (send_ref, send_out)))
        ]

    @pl.when(j == 0)
    def _():
        down_acc[...] = jnp.zeros_like(down_acc)
        hid_acc[...] = jnp.zeros_like(hid_acc)
        if head:
            res = x_ref[...].astype(F32) + (
                dot_nn(all_pairs([ctx_ref]), wo_ref[...]) + row(bo_ref)
            )
            res_ref[...] = res
            y, _ = normalise(res)
            hid_ref[...] = (y * row(gain_ref) + row(shift_ref)).astype(BF16)
        for copy in moves(later if head else early):
            copy.start()

    hid, cot = hid_ref[...], cot_ref[...]
    up, down = up_ref[...], down_ref[...]
    pre = dot_nn(hid, up) + bias_ref[0]
    cdf = 0.5 + 0.5 * lax.erf(pre * 0.7071067811865476)
    slope = cdf + pre * (0.3989422804014327 * jnp.exp(-0.5 * pre * pre))
    act = (pre * cdf).astype(BF16)
    pre_grad = (dot_nt(cot, down) * slope).astype(BF16)
    up_grad = dot_tn(hid, pre_grad).astype(BF16)
    down_grad = dot_tn(act, cot).astype(BF16)

    for core in range(2):

        @pl.when(core_ref[0] == core)
        def _():
            for c in range(cb):
                cols = slice(c * LANES, (c + 1) * LANES)
                (keep_ref, send_ref)[core][j * cb + c] = up_grad[:, cols]
                (send_ref, keep_ref)[core][j * cb + c] = down_grad[:, cols]

    for copy in part(j * cb, cb, j):
        copy.start()
    down_acc[...] += dot_nn(act, down)
    hid_acc[...] += dot_nt(pre_grad, up)
    bias_grad[0] = column_sum(pre_grad.astype(F32))

    @pl.when(j == steps - 1)
    def _():
        if head:
            for copy in moves(later):
                copy.wait()
        else:
            for copy in moves(early):
                copy.wait()
            res = res_ref[...]
            cot = cot_ref[...].astype(F32)
            down_sum = down_first[...] + down_acc[...]
            mixed_ref[...] = (res + (down_sum + row(bd_ref))).astype(BF16)
            y, scale = normalise(res)
            dh = hid_first[...] + hid_acc[...]
            a = dh * row(gain_ref)
            dres = cot + scale * (
                a
                - jnp.mean(a, axis=-1, keepdims=True)
                - y * jnp.mean(a * y, axis=-1, keepdims=True)
            )
            dres_ref[...] = dres
            branch = dres.astype(BF16)
            out_grad = dot_tn(all_pairs([ctx_ref]), branch).astype(BF16)
            first, own = 2 * cb, cb // 2
            for core in range(2):

                @pl.when(core_ref[0] == core)
                def _():
                    for c in range(own):
                        low = out_grad[:, c * LANES : (c + 1) * LANES]
                        high = out_grad[:, (own + c) * LANES : (own + c + 1) * LANES]
                        (keep_ref, send_ref)[core][first + c] = low
                        (send_ref, keep_ref)[core][first + c] = high

            for copy in part(first, own, sems.shape[1] - 1):
                copy.start()
            dots_ref[...] = jnp.zeros_like(dots_ref)
            for p in range(dctx_ref.shape[0]):
                grad = dot_nt(wo_ref[p * LANES : (p + 1) * LANES, :], branch).astype(BF16)
                dctx_ref[p] = grad
                product = grad.astype(F32) * at_ref[p]
                for h in range(2):
                    dots_ref[p, h : h + 1, :] = column_sum(product[rows_of_head(h)])
            sums_ref[0:1] = column_sum(dh * y)
            sums_ref[1:2] = column_sum(dh)
            sums_ref[2:3] = column_sum(branch.astype(F32))
            sums_ref[3:4] = column_sum(cot)
            for copy in part(first, own, sems.shape[1] - 1):
                copy.wait()
        for k in range(keep_ref.shape[0] // cb):
            for copy in part(k * cb, cb, k):
                copy.wait()


def ffn(core, vectors, cot, up, down, bias, ctx, wo, start, steps, head=None, tail=None,
        after=()):
    rows, width = cot.shape
    once = pl.Buffered(1)
    whole = pl.BlockSpec((rows, width), lambda j: (0, 0), pipeline_mode=once)
    square = pl.BlockSpec((width, width), lambda j: (0, 0), pipeline_mode=once)
    vecs = pl.BlockSpec((8, width), lambda j: (0, 0))
    anywhere = pl.BlockSpec(memory_space=pl.ANY)
    cb = width // LANES

    def pairs(*shape):
        return pl.BlockSpec((cb, *shape), lambda j: (0, 0, 0), pipeline_mode=once)

    full, half = shaped((rows, width), F32), shaped((rows, width), BF16)
    wide, thin = pltpu.VMEM((rows, width), F32), pltpu.VMEM((rows, width), BF16)
    if head is not None:
        count = steps * cb
        outs, out_specs = [full, half, full, full], [anywhere] * 2 + [whole] * 2
        extra, extra_specs = list(head), [whole]
    else:
        count = steps * cb + cb // 2
        outs = [
            half, full, shaped((cb, LANES, rows), BF16), shaped((cb, 8, rows), F32),
            shaped((8, width), F32),
        ]
        out_specs = [whole, whole, pairs(LANES, rows), pairs(8, rows), vecs]
        extra, extra_specs = list(tail), [whole] + [anywhere] * 4
    grads = pltpu.VMEM((count, width, LANES), BF16)
    sems = [pltpu.SemaphoreType.DMA((2, steps + (head is None)))]
    sems += [pltpu.SemaphoreType.DMA((2 if head is not None else 6,))]
    if head is not None:
        scratch = [wide, thin, grads, grads, *sems]
    else:
        scratch = [grads, grads, *sems, pltpu.VMEM((cb, rows, LANES), BF16)]
        scratch += [pltpu.VMEM((width, width), BF16), wide, wide, wide]
        scratch += [pltpu.VMEM((cb, LANES, rows), F32), wide, wide]
    return call(
        functools.partial(ffn_kernel, head is not None),
        outs + [shaped((count, width, LANES), BF16)] * 2 + [shaped((steps, 1, width), F32)],
        30,
        after=after,
        vmem=56,
        grid=(steps,),
        in_specs=[
            SMEM,
            *[pl.BlockSpec((width,), lambda j: (0,))] * len(vectors),
            whole,
            pl.BlockSpec((width, width), lambda j: (0, j + start)),
            pl.BlockSpec((width, width), lambda j: (j + start, 0)),
            pl.BlockSpec((1, 1, width), lambda j: (j + start, 0, 0)),
            pairs(rows, LANES) if head is not None else anywhere,
            square if head is not None else anywhere,
        ]
        + extra_specs,
        out_specs=out_specs
        + [anywhere] * 2
        + [pl.BlockSpec((1, 1, width), lambda j: (j, 0, 0))],
        scratch_shapes=scratch,
    )(core, *vectors, cot, up, down, bias, ctx, wo, *extra)


class Shared:
    def __init__(self, core_ref, keep_ref, send_ref):
        self.core_ref, self.refs, self.count = core_ref, (keep_ref, send_ref), 0

    def store(self, values):
        half = self.refs[0].shape[0]
        values = values.astype(BF16)
        for c in range(values.shape[1] // LANES):
            block = values[:, c * LANES : (c + 1) * LANES]
            owner, at = divmod(self.count, half)
            self.count += 1

            @pl.when(self.core_ref[0] == owner)
            def _():
                self.refs[0][at] = block

            @pl.when(self.core_ref[0] != owner)
            def _():
                self.refs[1][at] = block


def project_back_kernel(blocks, calls, *refs):
    refs = list(refs)

    def take(count):
        taken = refs[:count]
        del refs[:count]
        return taken

    core_ref, info_ref, bucket_ref, vec_ffn, *bias_grads = take(6)
    peer_sums = take(blocks - 1)
    n_refs, (x_ref,) = take(blocks), take(1)
    wq_ref, wk_ref, wv_ref = take(3)
    dq_refs = take(calls)
    dk_refs, dv_refs, w_refs = [[take(calls) for _ in range(blocks)] for _ in range(3)]
    (ng_ref,) = take(1)
    keep_ref, send_ref, small_ref = take(3)
    grads = Shared(core_ref, keep_ref, send_ref)
    dq = all_pairs(dq_refs)
    gk = gv = bias = None
    for b in range(blocks):
        dk, dv, norm = all_pairs(dk_refs[b]), all_pairs(dv_refs[b]), n_refs[b][...]
        if b == 0:
            ng = 0.125 * dot_nt(dq, wq_ref[...])
            ng = ng + dot_nt(dk, wk_ref[...]) + dot_nt(dv, wv_ref[...])
            grads.store(0.125 * dot_tn(norm, dq))
            ng_ref[...] = ng
            y, _ = normalise(x_ref[...].astype(F32))
            sums = [column_sum(ng * y), column_sum(ng)]
        k_part, v_part, b_part = dot_tn(norm, dk), dot_tn(norm, dv), column_sum(dv.astype(F32))
        gk = k_part if gk is None else gk + k_part
        gv = v_part if gv is None else gv + v_part
        bias = b_part if bias is None else bias + b_part
    for peer in peer_sums:
        sums = [mine + peer[i : i + 1] for i, mine in enumerate(sums)]
    grads.store(gk)
    grads.store(gv)
    small_ref[...] = jnp.zeros_like(small_ref)
    vectors = sums + [0.125 * column_sum(dq.astype(F32)), bias]
    vectors += [vec_ffn[i : i + 1] for i in range(4)]
    vectors += [ref[i] for ref in bias_grads for i in range(ref.shape[0])]
    at = 0
    for vec in vectors:
        for c in range(vec.shape[1] // LANES):
            small_ref[at : at + 1, :] = vec[:, c * LANES : (c + 1) * LANES]
            at += 1
    table = None
    span = w_refs[0][0].shape[2]
    for b in range(blocks):
        start = pl.multiple_of(info_ref[2 * b + 1], LANES)
        window = bucket_ref[:, pl.ds(start, span)]
        one_hot = jnp.where(
            lax.broadcasted_iota(jnp.int32, (TABLE_ROWS, span), 0) == window, 1.0, 0.0
        ).astype(BF16)
        w = jnp.concatenate([ref[p] for ref in w_refs[b] for p in range(ref.shape[0])], axis=0)
        w_hi = w.astype(BF16)
        w_lo = (w - w_hi.astype(F32)).astype(BF16)
        part = dot_nt(w_hi, one_hot) + dot_nt(w_lo, one_hot)
        table = part if table is None else table + part
    for c in range(TABLE_ROWS // LANES):
        small_ref[at : at + table.shape[0], :] = table[:, c * LANES : (c + 1) * LANES]
        at += table.shape[0]
    grads.store(small_ref[...])
    while grads.count < 2 * keep_ref.shape[0]:
        grads.store(jnp.zeros_like(small_ref))


TABLE_ROWS = 384


def project_back(core, info, bucket, vec_ffn, bias_grads, peer_sums, norms, x, weights, parts,
                 after=()):
    rows, width = norms[0].shape
    blocks = len(norms)
    whole = pl.BlockSpec(memory_space=pltpu.VMEM)
    arrays = [core, info, bucket, vec_ffn, *bias_grads, *peer_sums, *norms, x, *weights]
    arrays += [part[0].reshape(-1, rows, LANES) for part in parts[0]]
    for kind in (1, 2):
        arrays += [part[kind].reshape(-1, rows, LANES) for block in parts for part in block]
    arrays += [part[3] for block in parts for part in block]
    count = 3 * width // LANES + 1
    count += count % 2
    ng, *grads = call(
        functools.partial(project_back_kernel, blocks, len(parts[0])),
        [shaped((rows, width), F32)] + [shaped((count // 2, width, LANES), BF16)] * 2,
        SHORT,
        after=after,
        grid=(1,),
        in_specs=[SMEM, SMEM] + [whole] * (len(arrays) - 2),
        scratch_shapes=[pltpu.VMEM((width, LANES), F32)],
    )(*arrays)
    return ng, grads


def peer_back_kernel(calls, *refs):
    x_ref, wk_ref, wv_ref = refs[:3]
    dk_refs, dv_refs = refs[3 : 3 + calls], refs[3 + calls : 3 + 2 * calls]
    ng_ref, sums_ref = refs[3 + 2 * calls :]
    dk, dv = all_pairs(dk_refs), all_pairs(dv_refs)
    ng = dot_nt(dk, wk_ref[...]) + dot_nt(dv, wv_ref[...])
    ng_ref[...] = ng.astype(BF16)
    y, _ = normalise(x_ref[...].astype(F32))
    sums_ref[0:1] = column_sum(ng * y)
    sums_ref[1:2] = column_sum(ng)


def peer_back(x, weights, parts, after=()):
    rows, width = x.shape
    arrays = [x, *weights[1:]]
    for kind in (1, 2):
        arrays += [part[kind].reshape(-1, rows, LANES) for part in parts]
    return call(
        functools.partial(peer_back_kernel, len(parts)),
        [shaped((rows, width), BF16), shaped((8, width), F32)],
        SHORT,
        after=after,
        grid=(1,),
        in_specs=[IN_VMEM] * len(arrays),
    )(*arrays)


def frames_back_kernel(count, *refs):
    x_ref, gain_ref, dres_ref, ng_ref = refs[:4]
    out_ref = refs[-1]
    y, scale = normalise(x_ref[...].astype(F32))
    ng = ng_ref[...]
    for other in refs[4 : 4 + count]:
        ng = ng + other[...].astype(F32)
    a = ng * row(gain_ref)
    out_ref[...] = dres_ref[...] + scale * (
        a - jnp.mean(a, axis=-1, keepdims=True) - y * jnp.mean(a * y, axis=-1, keepdims=True)
    )


def frames_back(x, gain, dres, ng, others, after=()):
    rows, width = x.shape
    tile = 128
    blk = pl.BlockSpec((tile, width), lambda i: (i, 0))
    vec = pl.BlockSpec((width,), lambda i: (0,))
    return call(
        functools.partial(frames_back_kernel, len(others)),
        shaped((rows, width), F32),
        4,
        after=after,
        grid=(rows // tile,),
        in_specs=[blk, vec, blk, blk] + [blk] * len(others),
        out_specs=blk,
    )(x, gain, dres, ng, *others)


def swap(x, bit):
    axis, mask = bit
    if isinstance(mask, int):
        mask = [(i, i ^ mask) for i in range(lax.axis_size(axis))]
    return lax.ppermute(x, axis, mask)


def side(bit):
    axis, mask = bit
    return ((lax.axis_index(axis) & mask) != 0).astype(jnp.int32)


CORE, ALONG, NEAR, FAR, ACROSS = ("batch", 1), ("batch", 2), ("batch", 4), ("batch", 8), ("blk", 1)

def local(kernel, sides, arrays, shapes, time=0.01):
    return pl.pallas_call(
        kernel,
        out_shape=[shaped(shape, BF16) for shape in shapes],
        in_specs=[SMEM] + [IN_VMEM] * len(arrays),
        out_specs=[IN_VMEM] * len(shapes),
        compiler_params=pltpu.CompilerParams(vmem_limit_bytes=4 * 1024 * 1024),
        cost_estimate=cost_of(time),
    )(sides, *arrays)


def both_halves(size, at):
    return [pl.ds(pl.multiple_of(k * size, 16), size) for k in (1 - at, at)]


def add(a, b):
    return (a.astype(F32) + b.astype(F32)).astype(BF16)


def sum_over_devices(keep, send, time):
    n, rows, _ = keep.shape
    count_a = n // 2
    count_b = n - count_a
    halves = (slice(0, count_a), slice(count_a, n))
    x, y, z, w = range(4)
    sides = jnp.stack([side(bit) for bit in (ACROSS, ALONG, NEAR, FAR)])
    (got,) = yield [(send, CORE)]

    def first(s, keep, got, send_a, keep_a, send_b, keep_b):
        for k, bit, outs in ((0, x, (send_a, keep_a)), (1, y, (send_b, keep_b))):
            block = halves[k]
            for rows_at, out in zip(both_halves(rows // 2, s[bit]), outs):
                out[...] = add(keep[block, rows_at, :], got[block, rows_at, :])

    def shapes(size):
        return [(count_a, size, LANES), (count_b, size, LANES)]

    send_a, keep_a, send_b, keep_b = local(
        first, sides, [keep, got], [x for x in shapes(rows // 2) for _ in range(2)]
    )
    got_a, got_b = yield [(send_a, ACROSS), (send_b, ALONG)]

    def second(s, keep_a, got_a, keep_b, got_b, *outs):
        for k, bit, keep, got in ((0, y, keep_a, got_a), (1, x, keep_b, got_b)):
            for rows_at, out in zip(both_halves(rows // 4, s[bit]), outs[2 * k : 2 * k + 2]):
                out[...] = add(keep[:, rows_at, :], got[:, rows_at, :])

    send_a, keep_a, send_b, keep_b = local(
        second,
        sides,
        [keep_a, got_a, keep_b, got_b],
        [x for x in shapes(rows // 4) for _ in range(2)],
        time,
    )
    got_a, got_b = yield [(send_a, ALONG), (send_b, ACROSS)]

    def third(s, keep_a, got_a, keep_b, got_b, *outs):
        for k, keep, got in ((0, keep_a, got_a), (1, keep_b, got_b)):
            for rows_at, out in zip(both_halves(rows // 8, s[z]), outs):
                out[halves[k]] = add(keep[:, rows_at, :], got[:, rows_at, :])

    shape = (n, rows // 8, LANES)
    send, keep = local(third, sides, [keep_a, got_a, keep_b, got_b], [shape] * 2)
    (got,) = yield [(send, NEAR)]

    def fourth(s, keep, got, *outs):
        for rows_at, out in zip(both_halves(rows // 16, s[w]), outs):
            out[...] = add(keep[:, rows_at, :], got[:, rows_at, :])

    shape = (n, rows // 16, LANES)
    send, keep = local(fourth, sides, [keep, got], [shape] * 2)
    (got,) = yield [(send, FAR)]

    def fifth(s, keep, got, out):
        out[...] = add(keep[...], got[...])

    (held,) = local(fifth, sides, [keep, got], [shape])
    (got,) = yield [(held, FAR)]

    def join_far(s, held, got, out):
        for rows_at, ref in zip(both_halves(rows // 16, s[w]), (got, held)):
            out[:, rows_at, :] = ref[...]

    (held,) = local(join_far, sides, [held, got], [(n, rows // 8, LANES)])
    (got,) = yield [(held, NEAR)]

    def join_near(s, held, got, *outs):
        for k, out in enumerate(outs):
            for rows_at, ref in zip(both_halves(rows // 8, s[z]), (got, held)):
                out[:, rows_at, :] = ref[halves[k]]

    held_a, held_b = local(join_near, sides, [held, got], shapes(rows // 4))
    got_a, got_b = yield [(held_a, ALONG), (held_b, ACROSS)]

    def join_second(s, held_a, got_a, held_b, got_b, *outs):
        for bit, held, got, out in ((y, held_a, got_a, outs[0]), (x, held_b, got_b, outs[1])):
            for rows_at, ref in zip(both_halves(rows // 4, s[bit]), (got, held)):
                out[:, rows_at, :] = ref[...]

    held_a, held_b = local(
        join_second, sides, [held_a, got_a, held_b, got_b], shapes(rows // 2)
    )
    got_a, got_b = yield [(held_a, ACROSS), (held_b, ALONG)]

    def join_first(s, held_a, got_a, held_b, got_b, out):
        for k, bit, held, got in ((0, x, held_a, got_a), (1, y, held_b, got_b)):
            for rows_at, ref in zip(both_halves(rows // 2, s[bit]), (got, held)):
                out[halves[k], rows_at, :] = ref[...]

    (held,) = local(join_first, sides, [held_a, got_a, held_b, got_b], [(n, rows, LANES)])
    (got,) = yield [(held, CORE)]
    return held, got


def sum_plainly(keep, send, time):
    low = side(CORE) == 0
    first, second = [
        lax.psum(jnp.where(low, *pair), ("batch", "blk")) for pair in ((keep, send), (send, keep))
    ]
    yield [(first[:1, :8], CORE)]
    return jnp.where(low, first, second), jnp.where(low, second, first)


def send_back(x, b):
    blocks = lax.axis_size("blk")
    (got,) = yield [(x, ("blk", [(i, (i + b) % blocks) for i in range(blocks)]))]
    return got


def summed(keep, send, time=0.01):
    fits = lax.axis_size("blk") == 2 and lax.axis_size("batch") == 16
    return (sum_over_devices if fits else sum_plainly)(keep, send, time)


class Flow:
    def __init__(self, steps):
        self.steps = steps
        self.result = None
        self.take(next(steps))

    def take(self, pending):
        self.arrays = [array for array, _ in pending]
        self.got = [swap(array, bit) for array, bit in pending]

    def land(self, last):
        if self.result is not None:
            return last
        *got, _ = lax.optimization_barrier([*self.got, last])
        try:
            self.take(self.steps.send(got))
            return self.arrays[0]
        except StopIteration as end:
            self.arrays, self.result = [], end.value
            return jax.tree.leaves(end.value)[0]


class Order:
    def __init__(self, last):
        self.last = last
        self.flows = {}
        self.fresh = []

    def add(self, name, steps):
        self.flows[name] = Flow(steps)
        self.fresh += self.flows[name].arrays

    def later(self, array):
        return lax.optimization_barrier((array, self.last))[0]

    def kernel(self, run):
        result = run([self.last, *self.fresh])
        self.fresh = []
        self.last = jax.tree.leaves(result)[-1]
        return result

    def land(self, *names):
        for name in names:
            self.last = self.flows[name].land(self.last)
            self.fresh += self.flows[name].arrays

    def result(self, name):
        while self.flows[name].result is None:
            self.land(name)
        return self.flows[name].result


def place_kernel(plan, tile, core_ref, *refs):
    ins = refs[: 2 * (1 + max(step[0] for step in plan))]
    outs = refs[len(ins) :]
    rows = pl.ds(pl.multiple_of(pl.program_id(0) * tile, 16), tile)
    for core in range(2):

        @pl.when(core_ref[0] == core)
        def _():
            for source, half, column, out, slot, at in plan:
                x = ins[2 * source + (half ^ core)][column, rows, :].astype(F32)
                cols = slice(at * LANES, (at + 1) * LANES)
                if slot is None:
                    outs[out][:, cols] = x
                else:
                    outs[out][slot, :, cols] = x


def place(core, sums, plan, out_shapes, after=()):
    halves = [half for pair in sums for half in pair]
    tile = 96
    out_specs = []
    for shape in out_shapes:
        if len(shape) == 2:
            out_specs.append(pl.BlockSpec((tile, shape[1]), lambda i: (i, 0)))
        else:
            out_specs.append(pl.BlockSpec((shape[0], tile, shape[2]), lambda i: (0, i, 0)))
    return call(
        functools.partial(place_kernel, plan, tile),
        [shaped(shape, F32) for shape in out_shapes],
        7,
        after=after,
        grid=(halves[0].shape[1] // tile,),
        in_specs=[SMEM] + [IN_VMEM] * len(halves),
        out_specs=out_specs,
    )(core, *halves)


def per_device(
    frames,
    cotangent,
    query_weight,
    key_weight,
    value_weight,
    output_weight,
    up_weight,
    down_weight,
    attn_gain,
    attn_shift,
    query_bias,
    value_bias,
    output_bias,
    ffn_gain,
    ffn_shift,
    up_bias,
    down_bias,
    rel_table,
    utt_lengths,
    frame_mask,
    rel_bucket,
):
    rows_n, length, width = frames.shape
    blocks = lax.axis_size("blk")
    seq = length * blocks
    me = lax.axis_index("blk")
    rows = rows_n * length
    units = up_weight.shape[1]
    steps = units // width
    heads = rel_table.shape[1]
    buckets = rel_table.shape[0]
    core = side(CORE).reshape(1)
    weights = (query_weight, key_weight, value_weight)

    def from_peer(x, b):
        return lax.ppermute(x, "blk", [((i + b) % blocks, i) for i in range(blocks)])

    def split(x):
        return x.reshape(x.shape[0], rows_n, length, x.shape[2])

    def split_flip(x):
        return jnp.swapaxes(x.reshape(*x.shape[:2], rows_n, length), 1, 2)

    def join_flip(x):
        return jnp.swapaxes(x, 1, 2).reshape(x.shape[0], x.shape[2], rows)

    def flat(x):
        return x.reshape(rows, x.shape[-1])

    flat_frames = flat(frames)
    x_blocks = [flat_frames] + [from_peer(flat_frames, b) for b in range(1, blocks)]
    masks = [frame_mask] + [from_peer(frame_mask, b) for b in range(1, blocks)]
    starts = [((me + b) % blocks) * length for b in range(blocks)]
    info = jnp.stack(
        [x for start in starts for x in (start, seq - length + starts[0] - start)]
    ).astype(jnp.int32)
    bucket = jnp.concatenate([jnp.full((1,), -1, jnp.int32), rel_bucket]).reshape(1, -1)
    norms, keys, values, probs, tops = [], [], [], [], []
    state = None
    for b in range(blocks):
        last = b == blocks - 1
        norm, key_feat, window, *rest = project(
            info, utt_lengths, x_blocks[b], (attn_gain, attn_shift), masks[b], bucket, rel_table.T,
            weights[1:] if b else weights, (value_bias,) if b else (query_bias, value_bias), b,
        )
        if b == 0:
            query_feat, query, key, value = rest
            query = split(query)
        else:
            key, value = rest
        norms.append(norm)
        keys.append(split(key))
        values.append(split(value))
        p, m, out, stats, *context = attend(
            query, keys[b], values[b], query_feat, key_feat, window, state, last
        )
        probs.append(p)
        tops.append(m)
        state = (out, stats)

    attended, lse = state
    context = context[0].reshape(heads // 2, rows, LANES)
    cot = flat(cotangent)
    dense = (
        core, (output_bias, ffn_gain, ffn_shift, down_bias), cot, up_weight, down_weight,
        up_bias.reshape(steps, 1, width), context, output_weight,
    )
    half = steps // 2
    res, hid, *carry, keep, send, bias_one = ffn(*dense, 0, half, head=(flat_frames,))
    order = Order(bias_one)
    order.add("one", summed(keep, send))
    mixed, dres, dctx, dots, vec_ffn, keep, send, bias_two = order.kernel(
        lambda after: ffn(
            *dense, half, steps - half, tail=(hid, *carry, res, join_flip(attended)), after=after
        )
    )
    order.add("two", summed(keep, send, LONG))
    order.land("one")

    dctx, dots = split_flip(dctx), split_flip(dots)
    pairs = heads // 2
    half_pairs = pairs // 2
    parts = [[] for _ in range(blocks)]
    peer_sums, peer_ngs = [], []
    dqs = [None, None]
    for b in [*range(1, blocks), 0]:
        for i in range(2):

            def run(after):
                return attend_back(
                    probs[b], query, keys[b], values[b], dctx, dots, lse, tops[b], dqs[i], b == 0,
                    i * half_pairs, (half_pairs, pairs - half_pairs)[i], after=after,
                )

            parts[b].append(order.kernel(run))
            dqs[i] = parts[b][-1][0]
            if b == 1 and i == 0:
                order.land("two")
        if b:
            ng, peer_sum = order.kernel(
                lambda after: peer_back(x_blocks[b], weights, parts[b], after=after)
            )
            peer_sums.append(peer_sum)
            peer_ngs.append(ng)
        if b == 1:
            order.land("one")
    own_ng, shared = order.kernel(
        lambda after: project_back(
            core, info, bucket, vec_ffn, (bias_one, bias_two), peer_sums, norms, flat_frames,
            weights, parts, after=after,
        )
    )
    order.add("three", summed(*shared))
    def place_frames():
        return order.kernel(
            lambda after: frames_back(
                flat_frames, attn_gain, dres, own_ng, [order.result(b) for b in range(1, blocks)],
                after=after,
            )
        )

    cb = width // LANES
    plan = []
    for chunk in range(steps):
        which, first = divmod(chunk, half)
        for c in range(cb):
            column = first * cb + c
            plan.append((which, 0, column, 0, None, chunk * cb + c))
            plan.append((which, 1, column, 1, chunk, c))
    for c in range(cb):
        plan.append((1, c // (cb // 2), 2 * cb + c % (cb // 2), 2, None, c))
    shapes = [(width, units), (steps, width, width), (width, width)]

    def place_dense():
        sums = [order.result("one"), order.result("two")]
        return order.kernel(lambda after: place(core, sums, plan, shapes, after=after))

    for name in LANDINGS:
        if name == "frames":
            frames_grad = place_frames()
        elif name == "place":
            up_total, down_total, output_total = place_dense()
        elif name == "send_peers":
            for b, ng in enumerate(peer_ngs, 1):
                order.add(b, send_back(order.later(ng), b))
        elif name == "peers":
            order.land(*range(1, blocks))
        else:
            order.land(name)
    halves = order.result("three")
    last_half = halves[0].shape[0]
    plan = [
        (0, n // last_half, n % last_half, n // cb, None, n % cb) for n in range(3 * cb + 1)
    ]
    shapes = [(width, width)] * 3 + [(width, LANES)]
    query_total, key_total, value_total, small = place(
        core, [halves], plan, shapes
    )
    flat_small = small[: (8 + steps) * cb].reshape(-1, width)
    table_rows = small[(8 + steps) * cb : (8 + steps) * cb + heads * TABLE_ROWS // LANES]
    table_total = jnp.concatenate(
        [table_rows[i : i + heads] for i in range(0, table_rows.shape[0], heads)], axis=1
    )[:, :buckets].T
    return (
        mixed.reshape(frames.shape),
        frames_grad.reshape(frames.shape),
        query_total,
        key_total,
        value_total,
        output_total,
        up_total,
        down_total.reshape(units, width),
        flat_small[0],
        flat_small[1],
        flat_small[2],
        flat_small[3],
        flat_small[6],
        flat_small[4],
        flat_small[5],
        flat_small[8:].reshape(units),
        flat_small[7],
        table_total,
    )


def solution(mesh):
    batch3 = P("batch", "blk", None)
    in_specs = (batch3, batch3) + (P(),) * 16 + (P("batch", None), P("batch", "blk"), P())
    out_specs = (batch3, batch3) + (P(),) * 16
    return jax.shard_map(
        per_device, mesh=mesh, in_specs=in_specs, out_specs=out_specs, check_vma=False
    )
```

```python
import functools

import jax
import jax.numpy as jnp
from jax import lax
from jax.experimental import pallas as pl
from jax.experimental.pallas import tpu as pltpu
from jax.sharding import PartitionSpec as P

HD = 64
LANES = 128
EPSILON = 1e-05
MASKED = -1e30
BF16 = jnp.bfloat16
F32 = jnp.float32
COST = 1
SHORT, LONG = 0.05, 1000
LANDINGS = (
    "one", "two", "three", "one", "two", "one", "three", "one", "send_peers", "two", "one",
    "three", "two", "three", "one", "two", "peers", "frames", "three", "one", "two", "three",
    "one", "two", "three", "three", "two", "two", "place", "three", "three",
)
HIGHEST = lax.Precision.HIGHEST


def dot_nn(a, b):
    return lax.dot_general(a, b, (((1,), (0,)), ((), ())), preferred_element_type=F32)


def dot_nt(a, b):
    return lax.dot_general(a, b, (((1,), (1,)), ((), ())), preferred_element_type=F32)


def dot_tn(a, b):
    return lax.dot_general(a, b, (((0,), (0,)), ((), ())), preferred_element_type=F32)


def normalise(values):
    centre = values - jnp.mean(values, axis=-1, keepdims=True)
    scale = lax.rsqrt(jnp.mean(centre * centre, axis=-1, keepdims=True) + EPSILON)
    return centre * scale, scale


def column_sum(values):
    return jnp.sum(values, axis=0, keepdims=True)


def cost_of(time):
    return pl.CostEstimate(
        flops=int(time * COST * 1.1e9), bytes_accessed=int(time * COST * 3e6), transcendentals=0
    )


def call(kernel, out_shape, time, after=(), vmem=32, **kw):
    skip = len(after)

    def run(*refs):
        kernel(*refs[skip:])

    kw["in_specs"] = [pl.BlockSpec(memory_space=pl.ANY)] * skip + list(kw["in_specs"])
    program = pl.pallas_call(
        run,
        out_shape=out_shape,
        compiler_params=pltpu.CompilerParams(vmem_limit_bytes=vmem * 1024 * 1024),
        cost_estimate=cost_of(time),
        **kw,
    )
    return lambda *arrays: program(*after, *arrays)


SMEM = pl.BlockSpec(memory_space=pltpu.SMEM)
IN_VMEM = pl.BlockSpec(memory_space=pltpu.VMEM)


def shaped(shape, dtype):
    return jax.ShapeDtypeStruct(shape, dtype)


def row(ref):
    return ref[...].reshape(1, ref.shape[0])


def store_pairs(ref, values):
    for p in range(values.shape[1] // LANES):
        ref[p] = values[:, p * LANES : (p + 1) * LANES].astype(ref.dtype)


def all_pairs(refs):
    return jnp.concatenate([ref[p] for ref in refs for p in range(ref.shape[0])], axis=1)


def project_kernel(own, where, *refs):
    refs = list(refs)
    info_ref, lengths_ref, x_ref, gain_ref, shift_ref, mask_ref, bucket_ref, table_ref = refs[:8]
    refs = refs[8:]
    if own:
        bq_ref = refs.pop(0)
    bv_ref = refs.pop(0)
    if own:
        wq_ref, wk_ref, wv_ref, n_ref, kf_ref, win_ref, qf_ref, q_ref, k_ref, v_ref, norm = refs
    else:
        wk_ref, wv_ref, n_ref, kf_ref, win_ref, k_ref, v_ref, norm = refs
    rows_n, length, _ = kf_ref.shape

    @pl.when(pl.program_id(0) == 0)
    def _():
        y, _ = normalise(x_ref[...].astype(F32))
        norm[...] = (y * row(gain_ref) + row(shift_ref)).astype(BF16)
        n_ref[...] = norm[...]
        count = lengths_ref.shape[1]
        lane_row = lax.broadcasted_iota(jnp.int32, (1, LANES), 1)
        lane = lax.broadcasted_iota(jnp.int32, (length, LANES), 1)
        pos = info_ref[2 * where] + lax.broadcasted_iota(jnp.int32, (length, LANES), 0)
        for r in range(rows_n):
            end = jnp.int32(0)
            begins = jnp.zeros((1, LANES), jnp.int32)
            ends = jnp.zeros((1, LANES), jnp.int32)
            for u in range(count):
                begin, end = end, end + lengths_ref[r, u]
                begins = jnp.where(lane_row == u, begin, begins)
                ends = jnp.where(lane_row == u, end, ends)
            inside = (pos >= begins) & (pos < ends)
            seen = jnp.broadcast_to(mask_ref[r : r + 1, :].astype(F32), (LANES, length)).T > 0.5
            free = (lane >= count) | (inside & seen)
            kf_ref[r] = jnp.where(free, 0.0, MASKED).astype(BF16)
            if own:
                qf_ref[r] = jnp.where(inside, 1.0, 0.0).astype(BF16)
        buckets = table_ref.shape[1]
        at = pl.multiple_of(info_ref[2 * where + 1], LANES)
        window = bucket_ref[:, pl.ds(at, 2 * length)]
        one_hot = jnp.where(
            lax.broadcasted_iota(jnp.int32, (buckets, 2 * length), 0) == window, 1.0, 0.0
        ).astype(BF16)
        rest = table_ref[...]
        bias = None
        for _ in range(3):
            part = rest.astype(BF16)
            rest = rest - part.astype(F32)
            product = dot_nn(part, one_hot)
            bias = product if bias is None else bias + product
        for p in range(win_ref.shape[0]):
            win_ref[p] = bias[2 * p : 2 * p + 2]

    x = norm[...]
    if own:
        store_pairs(q_ref, (dot_nn(x, wq_ref[...]) + row(bq_ref)) * 0.125)
    store_pairs(k_ref, dot_nn(x, wk_ref[...]))
    store_pairs(v_ref, dot_nn(x, wv_ref[...]) + row(bv_ref))


def project(info, lengths, x, norm, mask, bucket, table, weights, biases, where, after=()):
    rows, width = x.shape
    rows_n, length = mask.shape
    pairs = table.shape[0] // 2
    cols = 256
    own = len(weights) == 3
    whole = pl.BlockSpec((rows, width), lambda j: (0, 0))
    part = pl.BlockSpec((width, cols), lambda j: (0, j))
    out = pl.BlockSpec((cols // LANES, rows, LANES), lambda j: (j, 0, 0))
    feat = pl.BlockSpec((rows_n, length, LANES), lambda j: (0, 0, 0))

    def fixed(array):
        return pl.BlockSpec(array.shape, lambda j: (0,) * array.ndim)

    count = len(weights)
    features = shaped((rows_n, length, LANES), BF16)
    window = shaped((pairs, 2, 2 * length), F32)
    return call(
        functools.partial(project_kernel, own, where),
        [shaped((rows, width), BF16), features, window]
        + [features] * own
        + [shaped((pairs, rows, LANES), BF16)] * count,
        5,
        after=after,
        vmem=56,
        grid=(width // cols,),
        in_specs=[SMEM, SMEM, whole, fixed(norm[0]), fixed(norm[1])]
        + [fixed(mask), fixed(bucket), fixed(table)]
        + [pl.BlockSpec((cols,), lambda j: (j,))] * len(biases)
        + [part] * count,
        out_specs=[whole, feat, fixed(window)] + [feat] * own + [out] * count,
        scratch_shapes=[pltpu.VMEM((rows, width), BF16)],
    )(info, lengths, x, *norm, mask, bucket, table, *biases, *weights)


def rows_of_head(h):
    return slice(h * HD, (h + 1) * HD)


def attend_kernel(own, last, chunk, *refs):
    refs = list(refs)
    q_ref, k_ref, v_ref, qf_ref, kf_ref, w_ref = refs[:6]
    refs = refs[6:]
    if not own:
        o_in, stats_in = refs[:2]
        refs = refs[2:]
    p_ref, m_ref, o_ref, stats_ref = refs[:4]
    cx_ref = refs[4] if last else None
    t_refs = refs[-2:]
    length = q_ref.shape[0]
    nb = length // LANES
    q = q_ref[...]
    k = k_ref[...]
    lane = lax.broadcasted_iota(jnp.int32, (length, LANES), 1)
    k_wide = jnp.concatenate([k, kf_ref[...]], axis=1)
    v_flip = v_ref[...].T
    ones = jnp.ones((16, length), BF16)
    eye = lax.broadcasted_iota(jnp.int32, (LANES, LANES), 0) == lax.broadcasted_iota(
        jnp.int32, (LANES, LANES), 1
    )
    zero = jnp.zeros((), BF16)
    for h in range(2):
        t_ref = t_refs[h]
        for a in range(2 * nb - 1):
            x = w_ref[h : h + 1, 2 * length - 256 - 128 * a : 2 * length - 128 * a]
            t = pltpu.roll(jnp.broadcast_to(x, (LANES, 256)), 0, 1, stride=1, stride_axis=0)
            t_ref[128 * a : 128 * a + 128, :] = t[:, LANES:]
        q_head = jnp.where((lane < HD) == (h == 0), q, zero)
        q_wide = jnp.concatenate([q_head, qf_ref[...]], axis=1)
        v_head = jnp.concatenate([v_flip[rows_of_head(h)], ones], axis=0)
        sums, tops = [], []
        for c in range(0, length, chunk):
            s = dot_nt(k_wide, q_wide[c : c + chunk])
            weights = []
            for i in range(c // LANES, (c + chunk) // LANES):
                first = 128 * (nb - 1 - i)
                here = slice(128 * i, 128 * i + 128)
                tile = s[:, 128 * i - c : 128 * i - c + 128] + t_ref[first : first + length, :]
                if own:
                    plain = dot_nt(k[here], q_head[here]) + t_ref[128 * (nb - 1) : 128 * nb, :]
                    fixed = jnp.where(eye, plain, tile[here])
                    around = [tile[: 128 * i], fixed, tile[128 * i + 128 :]]
                    tile = jnp.concatenate([x for x in around if x.shape[0]], axis=0)
                top = jnp.max(tile, axis=0, keepdims=True)
                weight = jnp.exp(tile - top).astype(BF16)
                p_ref[h, :, here] = weight
                weights.append(weight)
                tops.append(top)
            sums.append(dot_nn(v_head, jnp.concatenate(weights, axis=1)))
        o = jnp.concatenate(sums, axis=1)
        m = jnp.concatenate(tops, axis=1)
        o, l = o[:HD], o[HD : HD + 1]
        m_ref[h : h + 1, :] = m
        if not own:
            m_old = stats_in[h : h + 1, :]
            m_new = jnp.maximum(m_old, m)
            old, new = jnp.exp(m_old - m_new), jnp.exp(m - m_new)
            o = o_in[rows_of_head(h), :] * old + o * new
            l = stats_in[2 + h : 3 + h, :] * old + l * new
            m = m_new
        if last:
            o = o / l
            m = m + jnp.log(l)
        o_ref[rows_of_head(h), :] = o
        stats_ref[h : h + 1, :] = m
        stats_ref[2 + h : 3 + h, :] = l
    if last:
        cx_ref[...] = o_ref[...].T.astype(BF16)


def attend(q, k, v, qf, kf, window, state, last, chunk=256):
    pairs, rows, length, _ = q.shape
    nb = length // LANES
    own = state is None

    def spec(*shape):
        return pl.BlockSpec((pl.squeezed, pl.squeezed, *shape), lambda p, r: (p, r) + (0,) * len(shape))

    blk, flip, stats = spec(length, LANES), spec(LANES, length), spec(8, length)
    feat = pl.BlockSpec((pl.squeezed, length, LANES), lambda p, r: (r, 0, 0))
    stats_shape = shaped((pairs, rows, 8, length), F32)
    outs = [
        shaped((pairs, rows, 2, length, length), BF16),
        stats_shape,
        shaped((pairs, rows, LANES, length), F32),
        stats_shape,
    ] + [shaped((pairs, rows, length, LANES), BF16)] * last
    return call(
        functools.partial(attend_kernel, own, last, min(chunk, length)),
        outs,
        12,
        vmem=56,
        grid=(pairs, rows),
        in_specs=[blk] * 3
        + [feat] * 2
        + [pl.BlockSpec((pl.squeezed, 2, 2 * length), lambda p, r: (p, 0, 0))]
        + ([] if own else [flip, stats]),
        out_specs=[spec(2, length, length), stats, flip, stats] + [blk] * last,
        scratch_shapes=[pltpu.VMEM(((2 * nb - 1) * LANES, LANES), F32)] * 2,
    )(q, k, v, qf, kf, window, *([] if own else state))


def diagonal_sums(ds_ref, nb, lane8):
    length = nb * LANES
    tops, lows = [], []
    for a in range(2 * nb - 1):
        total = None
        for j in range(nb):
            i0 = 128 * (a - (nb - 1) + j)
            if 0 <= i0 < length:
                x = ds_ref[i0 : i0 + 128, 128 * j : 128 * j + 128].astype(F32)
                total = x if total is None else total + x
        whole, top = total[:8], total[:8]
        for g in range(1, 16):
            x = pltpu.roll(total[8 * g : 8 * g + 8], 128 - 8 * g, 1)
            whole = whole + x
            top = top + jnp.where(lane8 < 128 - 8 * g, x, 0.0)
        tops.append(top)
        lows.append(whole - top)
    pieces = []
    for g in range(2 * nb):
        a = 2 * nb - 1 - g
        if a == 2 * nb - 1:
            pieces.append(lows[a - 1])
        elif a == 0:
            pieces.append(tops[a])
        else:
            pieces.append(tops[a] + lows[a - 1])
    z = jnp.concatenate(pieces, axis=1)
    sub = lax.broadcasted_iota(jnp.int32, z.shape, 0)
    for bit in (1, 2, 4):
        z = jnp.where((sub & bit) != 0, pltpu.roll(z, 2 * length - bit, 1), z)
    return column_sum(z)


def attend_back_kernel(first, last, *refs):
    refs = list(refs)
    p_ref, q_ref, k_ref, v_ref, dc_ref, dot_ref, lse_ref, m_ref = refs[:8]
    refs = refs[8:]
    dq_in = None if first else refs.pop(0)
    dq_ref, dk_ref, dv_ref, w_ref, ds_ref, dq_flip = refs
    length = q_ref.shape[0]
    nb = length // LANES
    q, k, v = q_ref[...], k_ref[...], v_ref[...]
    lane = lax.broadcasted_iota(jnp.int32, (length, LANES), 1)
    line = lax.broadcasted_iota(jnp.int32, (LANES, length), 0)
    lane8 = lax.broadcasted_iota(jnp.int32, (8, LANES), 1)
    low = lane < HD
    zero = jnp.zeros((), BF16)
    k_flip = k.T
    v_wide = jnp.concatenate([v, jnp.where(lane < 2, -1.0, 0.0).astype(BF16)], axis=1)
    scaled, dots = [], []
    for h in range(2):
        factor = jnp.exp(m_ref[h : h + 1, :] - lse_ref[h : h + 1, :])
        scaled.append((dc_ref[rows_of_head(h), :].astype(F32) * factor).astype(BF16))
        dots.append(dot_ref[h : h + 1, :] * factor)
    do_flip = jnp.concatenate(scaled, axis=0)
    do = do_flip.T
    row = pl.program_id(1)
    parts = []
    for h in range(2):
        dot_hi = dots[h].astype(BF16)
        dot_lo = (dots[h] - dot_hi.astype(F32)).astype(BF16)
        feat = jnp.where(line == 0, dot_hi, jnp.where(line == 1, dot_lo, zero))
        mine = jnp.where((line < HD) == (h == 0), do_flip, zero)
        p = p_ref[h]
        dp = dot_nn(v_wide, jnp.concatenate([mine, feat], axis=0))
        ds = (p.astype(F32) * dp).astype(BF16)
        ds_ref[h] = ds
        parts.append((dot_nn(ds, q), dot_nn(p, do)))
        dq = dot_nn(k_flip[rows_of_head(h)], ds)
        dq_flip[rows_of_head(h), :] = dq if first else dq + dq_in[rows_of_head(h), :]
        diagonal = diagonal_sums(ds_ref.at[h], nb, lane8)

        @pl.when(row == 0)
        def _():
            w_ref[h : h + 1, :] = diagonal

        @pl.when(row != 0)
        def _():
            w_ref[h : h + 1, :] += diagonal

    dk, dv = [jnp.where(low, one, two) for one, two in zip(*parts)]
    dq_ref[...] = dq_flip[...].T.astype(BF16) if last else dq_flip[...]
    dk_ref[...] = dk.astype(BF16)
    dv_ref[...] = dv.astype(BF16)


def attend_back(p, q, k, v, dctx, dots, lse, m, dq, last, start, count, after=()):
    _, rows, length, _ = q.shape
    first = dq is None

    def spec(*shape, start=start):
        return pl.BlockSpec(
            (pl.squeezed, pl.squeezed, *shape), lambda p, r: (p + start, r) + (0,) * len(shape)
        )

    blk, flip, stats = spec(length, LANES), spec(LANES, length), spec(8, length)
    out, out_flip = spec(length, LANES, start=0), spec(LANES, length, start=0)
    arrays = [p, q, k, v, dctx, dots, lse, m] + ([] if first else [dq])
    natural = shaped((count, rows, length, LANES), BF16)
    return call(
        functools.partial(attend_back_kernel, first, last),
        [
            natural if last else shaped((count, rows, LANES, length), F32),
            natural,
            natural,
            shaped((count, 2, 2 * length), F32),
        ],
        LONG if first and start == 0 else SHORT,
        after=after,
        grid=(count, rows),
        in_specs=[spec(2, length, length)]
        + [blk] * 3
        + [flip]
        + [stats] * 3
        + ([] if first else [out_flip]),
        out_specs=[out if last else out_flip, out, out]
        + [pl.BlockSpec((pl.squeezed, 2, 2 * length), lambda p, r: (p, 0, 0))],
        scratch_shapes=[
            pltpu.VMEM((2, length, length), BF16),
            pltpu.VMEM((LANES, length), F32),
        ],
    )(*arrays)


def ffn_kernel(head, *refs):
    core_ref, bo_ref, gain_ref, shift_ref, bd_ref = refs[:5]
    cot_ref, up_ref, down_ref, bias_ref, ctx_in, wo_in = refs[5:11]
    refs = refs[11:]
    if head:
        x_ref, res_out, hid_out, down_acc, hid_acc, keep_out, send_out, bias_grad = refs[:8]
        res_ref, hid_ref, keep_ref, send_ref, sems, more_sems = refs[8:]
        ctx_ref, wo_ref = ctx_in, wo_in
        later = [(res_ref, res_out), (hid_ref, hid_out)]
    else:
        hid_ref, down_in, hid_in, res_in, at_in = refs[:5]
        mixed_ref, dres_ref, dctx_ref, dots_ref, sums_ref = refs[5:10]
        keep_out, send_out, bias_grad, keep_ref, send_ref, sems, more_sems = refs[10:17]
        ctx_ref, wo_ref, down_first, hid_first, res_ref, at_ref, down_acc, hid_acc = refs[17:]
        early = [
            (ctx_in, ctx_ref), (wo_in, wo_ref), (down_in, down_first), (hid_in, hid_first),
            (res_in, res_ref), (at_in, at_ref),
        ]
    j = pl.program_id(0)
    steps = pl.num_programs(0)
    cb = up_ref.shape[1] // LANES

    def moves(pairs):
        return [
            pltpu.make_async_copy(src, dst, more_sems.at[i]) for i, (src, dst) in enumerate(pairs)
        ]

    def part(at, count, index):
        here = pl.ds(at, count)
        return [
            pltpu.make_async_copy(src.at[here], dst.at[here], sems.at[k, index])
            for k, (src, dst) in enumerate(((keep_ref, keep_out), (send_ref, send_out)))
        ]

    @pl.when(j == 0)
    def _():
        down_acc[...] = jnp.zeros_like(down_acc)
        hid_acc[...] = jnp.zeros_like(hid_acc)
        if head:
            res = x_ref[...].astype(F32) + (
                dot_nn(all_pairs([ctx_ref]), wo_ref[...]) + row(bo_ref)
            )
            res_ref[...] = res
            y, _ = normalise(res)
            hid_ref[...] = (y * row(gain_ref) + row(shift_ref)).astype(BF16)
        for copy in moves(later if head else early):
            copy.start()

    hid, cot = hid_ref[...], cot_ref[...]
    up, down = up_ref[...], down_ref[...]
    pre = dot_nn(hid, up) + bias_ref[0]
    cdf = 0.5 + 0.5 * lax.erf(pre * 0.7071067811865476)
    slope = cdf + pre * (0.3989422804014327 * jnp.exp(-0.5 * pre * pre))
    act = (pre * cdf).astype(BF16)
    pre_grad = (dot_nt(cot, down) * slope).astype(BF16)
    up_grad = dot_tn(hid, pre_grad).astype(BF16)
    down_grad = dot_tn(act, cot).astype(BF16)

    for core in range(2):

        @pl.when(core_ref[0] == core)
        def _():
            for c in range(cb):
                cols = slice(c * LANES, (c + 1) * LANES)
                (keep_ref, send_ref)[core][j * cb + c] = up_grad[:, cols]
                (send_ref, keep_ref)[core][j * cb + c] = down_grad[:, cols]

    for copy in part(j * cb, cb, j):
        copy.start()
    down_acc[...] += dot_nn(act, down)
    hid_acc[...] += dot_nt(pre_grad, up)
    bias_grad[0] = column_sum(pre_grad.astype(F32))

    @pl.when(j == steps - 1)
    def _():
        if head:
            for copy in moves(later):
                copy.wait()
        else:
            for copy in moves(early):
                copy.wait()
            res = res_ref[...]
            cot = cot_ref[...].astype(F32)
            down_sum = down_first[...] + down_acc[...]
            mixed_ref[...] = (res + (down_sum + row(bd_ref))).astype(BF16)
            y, scale = normalise(res)
            dh = hid_first[...] + hid_acc[...]
            a = dh * row(gain_ref)
            dres = cot + scale * (
                a
                - jnp.mean(a, axis=-1, keepdims=True)
                - y * jnp.mean(a * y, axis=-1, keepdims=True)
            )
            dres_ref[...] = dres
            branch = dres.astype(BF16)
            out_grad = dot_tn(all_pairs([ctx_ref]), branch).astype(BF16)
            first, own = 2 * cb, cb // 2
            for core in range(2):

                @pl.when(core_ref[0] == core)
                def _():
                    for c in range(own):
                        low = out_grad[:, c * LANES : (c + 1) * LANES]
                        high = out_grad[:, (own + c) * LANES : (own + c + 1) * LANES]
                        (keep_ref, send_ref)[core][first + c] = low
                        (send_ref, keep_ref)[core][first + c] = high

            for copy in part(first, own, sems.shape[1] - 1):
                copy.start()
            dots_ref[...] = jnp.zeros_like(dots_ref)
            for p in range(dctx_ref.shape[0]):
                grad = dot_nt(wo_ref[p * LANES : (p + 1) * LANES, :], branch).astype(BF16)
                dctx_ref[p] = grad
                product = grad.astype(F32) * at_ref[p]
                for h in range(2):
                    dots_ref[p, h : h + 1, :] = column_sum(product[rows_of_head(h)])
            sums_ref[0:1] = column_sum(dh * y)
            sums_ref[1:2] = column_sum(dh)
            sums_ref[2:3] = column_sum(branch.astype(F32))
            sums_ref[3:4] = column_sum(cot)
            for copy in part(first, own, sems.shape[1] - 1):
                copy.wait()
        for k in range(keep_ref.shape[0] // cb):
            for copy in part(k * cb, cb, k):
                copy.wait()


def ffn(core, vectors, cot, up, down, bias, ctx, wo, start, steps, head=None, tail=None,
        after=()):
    rows, width = cot.shape
    once = pl.Buffered(1)
    whole = pl.BlockSpec((rows, width), lambda j: (0, 0), pipeline_mode=once)
    square = pl.BlockSpec((width, width), lambda j: (0, 0), pipeline_mode=once)
    vecs = pl.BlockSpec((8, width), lambda j: (0, 0))
    anywhere = pl.BlockSpec(memory_space=pl.ANY)
    cb = width // LANES

    def pairs(*shape):
        return pl.BlockSpec((cb, *shape), lambda j: (0, 0, 0), pipeline_mode=once)

    full, half = shaped((rows, width), F32), shaped((rows, width), BF16)
    wide, thin = pltpu.VMEM((rows, width), F32), pltpu.VMEM((rows, width), BF16)
    if head is not None:
        count = steps * cb
        outs, out_specs = [full, half, full, full], [anywhere] * 2 + [whole] * 2
        extra, extra_specs = list(head), [whole]
    else:
        count = steps * cb + cb // 2
        outs = [
            half, full, shaped((cb, LANES, rows), BF16), shaped((cb, 8, rows), F32),
            shaped((8, width), F32),
        ]
        out_specs = [whole, whole, pairs(LANES, rows), pairs(8, rows), vecs]
        extra, extra_specs = list(tail), [whole] + [anywhere] * 4
    grads = pltpu.VMEM((count, width, LANES), BF16)
    sems = [pltpu.SemaphoreType.DMA((2, steps + (head is None)))]
    sems += [pltpu.SemaphoreType.DMA((2 if head is not None else 6,))]
    if head is not None:
        scratch = [wide, thin, grads, grads, *sems]
    else:
        scratch = [grads, grads, *sems, pltpu.VMEM((cb, rows, LANES), BF16)]
        scratch += [pltpu.VMEM((width, width), BF16), wide, wide, wide]
        scratch += [pltpu.VMEM((cb, LANES, rows), F32), wide, wide]
    return call(
        functools.partial(ffn_kernel, head is not None),
        outs + [shaped((count, width, LANES), BF16)] * 2 + [shaped((steps, 1, width), F32)],
        30,
        after=after,
        vmem=56,
        grid=(steps,),
        in_specs=[
            SMEM,
            *[pl.BlockSpec((width,), lambda j: (0,))] * len(vectors),
            whole,
            pl.BlockSpec((width, width), lambda j: (0, j + start)),
            pl.BlockSpec((width, width), lambda j: (j + start, 0)),
            pl.BlockSpec((1, 1, width), lambda j: (j + start, 0, 0)),
            pairs(rows, LANES) if head is not None else anywhere,
            square if head is not None else anywhere,
        ]
        + extra_specs,
        out_specs=out_specs
        + [anywhere] * 2
        + [pl.BlockSpec((1, 1, width), lambda j: (j, 0, 0))],
        scratch_shapes=scratch,
    )(core, *vectors, cot, up, down, bias, ctx, wo, *extra)


class Shared:
    def __init__(self, core_ref, keep_ref, send_ref):
        self.core_ref, self.refs, self.count = core_ref, (keep_ref, send_ref), 0

    def store(self, values):
        half = self.refs[0].shape[0]
        values = values.astype(BF16)
        for c in range(values.shape[1] // LANES):
            block = values[:, c * LANES : (c + 1) * LANES]
            owner, at = divmod(self.count, half)
            self.count += 1

            @pl.when(self.core_ref[0] == owner)
            def _():
                self.refs[0][at] = block

            @pl.when(self.core_ref[0] != owner)
            def _():
                self.refs[1][at] = block


def project_back_kernel(blocks, calls, *refs):
    refs = list(refs)

    def take(count):
        taken = refs[:count]
        del refs[:count]
        return taken

    core_ref, info_ref, bucket_ref, vec_ffn, *bias_grads = take(6)
    peer_sums = take(blocks - 1)
    n_refs, (x_ref,) = take(blocks), take(1)
    wq_ref, wk_ref, wv_ref = take(3)
    dq_refs = take(calls)
    dk_refs, dv_refs, w_refs = [[take(calls) for _ in range(blocks)] for _ in range(3)]
    (ng_ref,) = take(1)
    keep_ref, send_ref, small_ref = take(3)
    grads = Shared(core_ref, keep_ref, send_ref)
    dq = all_pairs(dq_refs)
    gk = gv = bias = None
    for b in range(blocks):
        dk, dv, norm = all_pairs(dk_refs[b]), all_pairs(dv_refs[b]), n_refs[b][...]
        if b == 0:
            ng = 0.125 * dot_nt(dq, wq_ref[...])
            ng = ng + dot_nt(dk, wk_ref[...]) + dot_nt(dv, wv_ref[...])
            grads.store(0.125 * dot_tn(norm, dq))
            ng_ref[...] = ng
            y, _ = normalise(x_ref[...].astype(F32))
            sums = [column_sum(ng * y), column_sum(ng)]
        k_part, v_part, b_part = dot_tn(norm, dk), dot_tn(norm, dv), column_sum(dv.astype(F32))
        gk = k_part if gk is None else gk + k_part
        gv = v_part if gv is None else gv + v_part
        bias = b_part if bias is None else bias + b_part
    for peer in peer_sums:
        sums = [mine + peer[i : i + 1] for i, mine in enumerate(sums)]
    grads.store(gk)
    grads.store(gv)
    small_ref[...] = jnp.zeros_like(small_ref)
    vectors = sums + [0.125 * column_sum(dq.astype(F32)), bias]
    vectors += [vec_ffn[i : i + 1] for i in range(4)]
    vectors += [ref[i] for ref in bias_grads for i in range(ref.shape[0])]
    at = 0
    for vec in vectors:
        for c in range(vec.shape[1] // LANES):
            small_ref[at : at + 1, :] = vec[:, c * LANES : (c + 1) * LANES]
            at += 1
    table = None
    span = w_refs[0][0].shape[2]
    for b in range(blocks):
        start = pl.multiple_of(info_ref[2 * b + 1], LANES)
        window = bucket_ref[:, pl.ds(start, span)]
        one_hot = jnp.where(
            lax.broadcasted_iota(jnp.int32, (TABLE_ROWS, span), 0) == window, 1.0, 0.0
        ).astype(BF16)
        w = jnp.concatenate([ref[p] for ref in w_refs[b] for p in range(ref.shape[0])], axis=0)
        w_hi = w.astype(BF16)
        w_lo = (w - w_hi.astype(F32)).astype(BF16)
        part = dot_nt(w_hi, one_hot) + dot_nt(w_lo, one_hot)
        table = part if table is None else table + part
    for c in range(TABLE_ROWS // LANES):
        small_ref[at : at + table.shape[0], :] = table[:, c * LANES : (c + 1) * LANES]
        at += table.shape[0]
    grads.store(small_ref[...])
    while grads.count < 2 * keep_ref.shape[0]:
        grads.store(jnp.zeros_like(small_ref))


TABLE_ROWS = 384


def project_back(core, info, bucket, vec_ffn, bias_grads, peer_sums, norms, x, weights, parts,
                 after=()):
    rows, width = norms[0].shape
    blocks = len(norms)
    whole = pl.BlockSpec(memory_space=pltpu.VMEM)
    arrays = [core, info, bucket, vec_ffn, *bias_grads, *peer_sums, *norms, x, *weights]
    arrays += [part[0].reshape(-1, rows, LANES) for part in parts[0]]
    for kind in (1, 2):
        arrays += [part[kind].reshape(-1, rows, LANES) for block in parts for part in block]
    arrays += [part[3] for block in parts for part in block]
    count = 3 * width // LANES + 1
    count += count % 2
    ng, *grads = call(
        functools.partial(project_back_kernel, blocks, len(parts[0])),
        [shaped((rows, width), F32)] + [shaped((count // 2, width, LANES), BF16)] * 2,
        SHORT,
        after=after,
        grid=(1,),
        in_specs=[SMEM, SMEM] + [whole] * (len(arrays) - 2),
        scratch_shapes=[pltpu.VMEM((width, LANES), F32)],
    )(*arrays)
    return ng, grads


def peer_back_kernel(calls, *refs):
    x_ref, wk_ref, wv_ref = refs[:3]
    dk_refs, dv_refs = refs[3 : 3 + calls], refs[3 + calls : 3 + 2 * calls]
    ng_ref, sums_ref = refs[3 + 2 * calls :]
    dk, dv = all_pairs(dk_refs), all_pairs(dv_refs)
    ng = dot_nt(dk, wk_ref[...]) + dot_nt(dv, wv_ref[...])
    ng_ref[...] = ng.astype(BF16)
    y, _ = normalise(x_ref[...].astype(F32))
    sums_ref[0:1] = column_sum(ng * y)
    sums_ref[1:2] = column_sum(ng)


def peer_back(x, weights, parts, after=()):
    rows, width = x.shape
    arrays = [x, *weights[1:]]
    for kind in (1, 2):
        arrays += [part[kind].reshape(-1, rows, LANES) for part in parts]
    return call(
        functools.partial(peer_back_kernel, len(parts)),
        [shaped((rows, width), BF16), shaped((8, width), F32)],
        SHORT,
        after=after,
        grid=(1,),
        in_specs=[IN_VMEM] * len(arrays),
    )(*arrays)


def frames_back_kernel(count, *refs):
    x_ref, gain_ref, dres_ref, ng_ref = refs[:4]
    out_ref = refs[-1]
    y, scale = normalise(x_ref[...].astype(F32))
    ng = ng_ref[...]
    for other in refs[4 : 4 + count]:
        ng = ng + other[...].astype(F32)
    a = ng * row(gain_ref)
    out_ref[...] = dres_ref[...] + scale * (
        a - jnp.mean(a, axis=-1, keepdims=True) - y * jnp.mean(a * y, axis=-1, keepdims=True)
    )


def frames_back(x, gain, dres, ng, others, after=()):
    rows, width = x.shape
    tile = 128
    blk = pl.BlockSpec((tile, width), lambda i: (i, 0))
    vec = pl.BlockSpec((width,), lambda i: (0,))
    return call(
        functools.partial(frames_back_kernel, len(others)),
        shaped((rows, width), F32),
        4,
        after=after,
        grid=(rows // tile,),
        in_specs=[blk, vec, blk, blk] + [blk] * len(others),
        out_specs=blk,
    )(x, gain, dres, ng, *others)


def swap(x, bit):
    axis, mask = bit
    if isinstance(mask, int):
        mask = [(i, i ^ mask) for i in range(lax.axis_size(axis))]
    return lax.ppermute(x, axis, mask)


def side(bit):
    axis, mask = bit
    return ((lax.axis_index(axis) & mask) != 0).astype(jnp.int32)


CORE, ALONG, NEAR, FAR, ACROSS = ("batch", 1), ("batch", 2), ("batch", 4), ("batch", 8), ("blk", 1)

def local(kernel, sides, arrays, shapes, time=1.5):
    return pl.pallas_call(
        kernel,
        out_shape=[shaped(shape, BF16) for shape in shapes],
        in_specs=[SMEM] + [IN_VMEM] * len(arrays),
        out_specs=[IN_VMEM] * len(shapes),
        compiler_params=pltpu.CompilerParams(vmem_limit_bytes=4 * 1024 * 1024),
        cost_estimate=cost_of(time),
    )(sides, *arrays)


def both_halves(size, at):
    return [pl.ds(pl.multiple_of(k * size, 16), size) for k in (1 - at, at)]


def add(a, b):
    return (a.astype(F32) + b.astype(F32)).astype(BF16)


def sum_over_devices(keep, send, time):
    n, rows, _ = keep.shape
    count_a = n // 2
    count_b = n - count_a
    halves = (slice(0, count_a), slice(count_a, n))
    x, y, z, w = range(4)
    sides = jnp.stack([side(bit) for bit in (ACROSS, ALONG, NEAR, FAR)])
    (got,) = yield [(send, CORE)]

    def first(s, keep, got, send_a, keep_a, send_b, keep_b):
        for k, bit, outs in ((0, x, (send_a, keep_a)), (1, y, (send_b, keep_b))):
            block = halves[k]
            for rows_at, out in zip(both_halves(rows // 2, s[bit]), outs):
                out[...] = add(keep[block, rows_at, :], got[block, rows_at, :])

    def shapes(size):
        return [(count_a, size, LANES), (count_b, size, LANES)]

    send_a, keep_a, send_b, keep_b = local(
        first, sides, [keep, got], [x for x in shapes(rows // 2) for _ in range(2)]
    )
    got_a, got_b = yield [(send_a, ACROSS), (send_b, ALONG)]

    def second(s, keep_a, got_a, keep_b, got_b, *outs):
        for k, bit, keep, got in ((0, y, keep_a, got_a), (1, x, keep_b, got_b)):
            for rows_at, out in zip(both_halves(rows // 4, s[bit]), outs[2 * k : 2 * k + 2]):
                out[...] = add(keep[:, rows_at, :], got[:, rows_at, :])

    send_a, keep_a, send_b, keep_b = local(
        second,
        sides,
        [keep_a, got_a, keep_b, got_b],
        [x for x in shapes(rows // 4) for _ in range(2)],
        time,
    )
    got_a, got_b = yield [(send_a, ALONG), (send_b, ACROSS)]

    def third(s, keep_a, got_a, keep_b, got_b, *outs):
        for k, keep, got in ((0, keep_a, got_a), (1, keep_b, got_b)):
            for rows_at, out in zip(both_halves(rows // 8, s[z]), outs):
                out[halves[k]] = add(keep[:, rows_at, :], got[:, rows_at, :])

    shape = (n, rows // 8, LANES)
    send, keep = local(third, sides, [keep_a, got_a, keep_b, got_b], [shape] * 2)
    (got,) = yield [(send, NEAR)]

    def fourth(s, keep, got, *outs):
        for rows_at, out in zip(both_halves(rows // 16, s[w]), outs):
            out[...] = add(keep[:, rows_at, :], got[:, rows_at, :])

    shape = (n, rows // 16, LANES)
    send, keep = local(fourth, sides, [keep, got], [shape] * 2)
    (got,) = yield [(send, FAR)]

    def fifth(s, keep, got, out):
        out[...] = add(keep[...], got[...])

    (held,) = local(fifth, sides, [keep, got], [shape])
    (got,) = yield [(held, FAR)]

    def join_far(s, held, got, out):
        for rows_at, ref in zip(both_halves(rows // 16, s[w]), (got, held)):
            out[:, rows_at, :] = ref[...]

    (held,) = local(join_far, sides, [held, got], [(n, rows // 8, LANES)])
    (got,) = yield [(held, NEAR)]

    def join_near(s, held, got, *outs):
        for k, out in enumerate(outs):
            for rows_at, ref in zip(both_halves(rows // 8, s[z]), (got, held)):
                out[:, rows_at, :] = ref[halves[k]]

    held_a, held_b = local(join_near, sides, [held, got], shapes(rows // 4))
    got_a, got_b = yield [(held_a, ALONG), (held_b, ACROSS)]

    def join_second(s, held_a, got_a, held_b, got_b, *outs):
        for bit, held, got, out in ((y, held_a, got_a, outs[0]), (x, held_b, got_b, outs[1])):
            for rows_at, ref in zip(both_halves(rows // 4, s[bit]), (got, held)):
                out[:, rows_at, :] = ref[...]

    held_a, held_b = local(
        join_second, sides, [held_a, got_a, held_b, got_b], shapes(rows // 2)
    )
    got_a, got_b = yield [(held_a, ACROSS), (held_b, ALONG)]

    def join_first(s, held_a, got_a, held_b, got_b, out):
        for k, bit, held, got in ((0, x, held_a, got_a), (1, y, held_b, got_b)):
            for rows_at, ref in zip(both_halves(rows // 2, s[bit]), (got, held)):
                out[halves[k], rows_at, :] = ref[...]

    (held,) = local(join_first, sides, [held_a, got_a, held_b, got_b], [(n, rows, LANES)])
    (got,) = yield [(held, CORE)]
    return held, got


def sum_plainly(keep, send, time):
    low = side(CORE) == 0
    first, second = [
        lax.psum(jnp.where(low, *pair), ("batch", "blk")) for pair in ((keep, send), (send, keep))
    ]
    yield [(first[:1, :8], CORE)]
    return jnp.where(low, first, second), jnp.where(low, second, first)


def send_back(x, b):
    blocks = lax.axis_size("blk")
    (got,) = yield [(x, ("blk", [(i, (i + b) % blocks) for i in range(blocks)]))]
    return got


def summed(keep, send, time=1.5):
    fits = lax.axis_size("blk") == 2 and lax.axis_size("batch") == 16
    return (sum_over_devices if fits else sum_plainly)(keep, send, time)


class Flow:
    def __init__(self, steps):
        self.steps = steps
        self.result = None
        self.take(next(steps))

    def take(self, pending):
        self.arrays = [array for array, _ in pending]
        self.got = [swap(array, bit) for array, bit in pending]

    def land(self, last):
        if self.result is not None:
            return last
        *got, _ = lax.optimization_barrier([*self.got, last])
        try:
            self.take(self.steps.send(got))
            return self.arrays[0]
        except StopIteration as end:
            self.arrays, self.result = [], end.value
            return jax.tree.leaves(end.value)[0]


class Order:
    def __init__(self, last):
        self.last = last
        self.flows = {}
        self.fresh = []

    def add(self, name, steps):
        self.flows[name] = Flow(steps)
        self.fresh += self.flows[name].arrays

    def later(self, array):
        return lax.optimization_barrier((array, self.last))[0]

    def kernel(self, run):
        result = run([self.last, *self.fresh])
        self.fresh = []
        self.last = jax.tree.leaves(result)[-1]
        return result

    def land(self, *names):
        for name in names:
            self.last = self.flows[name].land(self.last)
            self.fresh += self.flows[name].arrays

    def result(self, name):
        while self.flows[name].result is None:
            self.land(name)
        return self.flows[name].result


def place_kernel(plan, tile, core_ref, *refs):
    ins = refs[: 2 * (1 + max(step[0] for step in plan))]
    outs = refs[len(ins) :]
    rows = pl.ds(pl.multiple_of(pl.program_id(0) * tile, 16), tile)
    for core in range(2):

        @pl.when(core_ref[0] == core)
        def _():
            for source, half, column, out, slot, at in plan:
                x = ins[2 * source + (half ^ core)][column, rows, :].astype(F32)
                cols = slice(at * LANES, (at + 1) * LANES)
                if slot is None:
                    outs[out][:, cols] = x
                else:
                    outs[out][slot, :, cols] = x


def place(core, sums, plan, out_shapes, after=()):
    halves = [half for pair in sums for half in pair]
    tile = 96
    out_specs = []
    for shape in out_shapes:
        if len(shape) == 2:
            out_specs.append(pl.BlockSpec((tile, shape[1]), lambda i: (i, 0)))
        else:
            out_specs.append(pl.BlockSpec((shape[0], tile, shape[2]), lambda i: (0, i, 0)))
    return call(
        functools.partial(place_kernel, plan, tile),
        [shaped(shape, F32) for shape in out_shapes],
        7,
        after=after,
        grid=(halves[0].shape[1] // tile,),
        in_specs=[SMEM] + [IN_VMEM] * len(halves),
        out_specs=out_specs,
    )(core, *halves)


def per_device(
    frames,
    cotangent,
    query_weight,
    key_weight,
    value_weight,
    output_weight,
    up_weight,
    down_weight,
    attn_gain,
    attn_shift,
    query_bias,
    value_bias,
    output_bias,
    ffn_gain,
    ffn_shift,
    up_bias,
    down_bias,
    rel_table,
    utt_lengths,
    frame_mask,
    rel_bucket,
):
    rows_n, length, width = frames.shape
    blocks = lax.axis_size("blk")
    seq = length * blocks
    me = lax.axis_index("blk")
    rows = rows_n * length
    units = up_weight.shape[1]
    steps = units // width
    heads = rel_table.shape[1]
    buckets = rel_table.shape[0]
    core = side(CORE).reshape(1)
    weights = (query_weight, key_weight, value_weight)

    def from_peer(x, b):
        return lax.ppermute(x, "blk", [((i + b) % blocks, i) for i in range(blocks)])

    def split(x):
        return x.reshape(x.shape[0], rows_n, length, x.shape[2])

    def split_flip(x):
        return jnp.swapaxes(x.reshape(*x.shape[:2], rows_n, length), 1, 2)

    def join_flip(x):
        return jnp.swapaxes(x, 1, 2).reshape(x.shape[0], x.shape[2], rows)

    def flat(x):
        return x.reshape(rows, x.shape[-1])

    flat_frames = flat(frames)
    x_blocks = [flat_frames] + [from_peer(flat_frames, b) for b in range(1, blocks)]
    masks = [frame_mask] + [from_peer(frame_mask, b) for b in range(1, blocks)]
    starts = [((me + b) % blocks) * length for b in range(blocks)]
    info = jnp.stack(
        [x for start in starts for x in (start, seq - length + starts[0] - start)]
    ).astype(jnp.int32)
    bucket = jnp.concatenate([jnp.full((1,), -1, jnp.int32), rel_bucket]).reshape(1, -1)
    norms, keys, values, probs, tops = [], [], [], [], []
    state = None
    for b in range(blocks):
        last = b == blocks - 1
        norm, key_feat, window, *rest = project(
            info, utt_lengths, x_blocks[b], (attn_gain, attn_shift), masks[b], bucket, rel_table.T,
            weights[1:] if b else weights, (value_bias,) if b else (query_bias, value_bias), b,
        )
        if b == 0:
            query_feat, query, key, value = rest
            query = split(query)
        else:
            key, value = rest
        norms.append(norm)
        keys.append(split(key))
        values.append(split(value))
        p, m, out, stats, *context = attend(
            query, keys[b], values[b], query_feat, key_feat, window, state, last
        )
        probs.append(p)
        tops.append(m)
        state = (out, stats)

    attended, lse = state
    context = context[0].reshape(heads // 2, rows, LANES)
    cot = flat(cotangent)
    dense = (
        core, (output_bias, ffn_gain, ffn_shift, down_bias), cot, up_weight, down_weight,
        up_bias.reshape(steps, 1, width), context, output_weight,
    )
    half = steps // 2
    res, hid, *carry, keep, send, bias_one = ffn(*dense, 0, half, head=(flat_frames,))
    order = Order(bias_one)
    order.add("one", summed(keep, send))
    mixed, dres, dctx, dots, vec_ffn, keep, send, bias_two = order.kernel(
        lambda after: ffn(
            *dense, half, steps - half, tail=(hid, *carry, res, join_flip(attended)), after=after
        )
    )
    order.add("two", summed(keep, send, LONG))
    order.land("one")

    dctx, dots = split_flip(dctx), split_flip(dots)
    pairs = heads // 2
    half_pairs = pairs // 2
    parts = [[] for _ in range(blocks)]
    peer_sums, peer_ngs = [], []
    dqs = [None, None]
    for b in [*range(1, blocks), 0]:
        for i in range(2):

            def run(after):
                return attend_back(
                    probs[b], query, keys[b], values[b], dctx, dots, lse, tops[b], dqs[i], b == 0,
                    i * half_pairs, (half_pairs, pairs - half_pairs)[i], after=after,
                )

            parts[b].append(order.kernel(run))
            dqs[i] = parts[b][-1][0]
            if b == 1 and i == 0:
                order.land("two")
        if b:
            ng, peer_sum = order.kernel(
                lambda after: peer_back(x_blocks[b], weights, parts[b], after=after)
            )
            peer_sums.append(peer_sum)
            peer_ngs.append(ng)
        if b == 1:
            order.land("one")
    own_ng, shared = order.kernel(
        lambda after: project_back(
            core, info, bucket, vec_ffn, (bias_one, bias_two), peer_sums, norms, flat_frames,
            weights, parts, after=after,
        )
    )
    order.add("three", summed(*shared))
    def place_frames():
        return order.kernel(
            lambda after: frames_back(
                flat_frames, attn_gain, dres, own_ng, [order.result(b) for b in range(1, blocks)],
                after=after,
            )
        )

    cb = width // LANES
    plan = []
    for chunk in range(steps):
        which, first = divmod(chunk, half)
        for c in range(cb):
            column = first * cb + c
            plan.append((which, 0, column, 0, None, chunk * cb + c))
            plan.append((which, 1, column, 1, chunk, c))
    for c in range(cb):
        plan.append((1, c // (cb // 2), 2 * cb + c % (cb // 2), 2, None, c))
    shapes = [(width, units), (steps, width, width), (width, width)]

    def place_dense():
        sums = [order.result("one"), order.result("two")]
        return order.kernel(lambda after: place(core, sums, plan, shapes, after=after))

    for name in LANDINGS:
        if name == "frames":
            frames_grad = place_frames()
        elif name == "place":
            up_total, down_total, output_total = place_dense()
        elif name == "send_peers":
            for b, ng in enumerate(peer_ngs, 1):
                order.add(b, send_back(order.later(ng), b))
        elif name == "peers":
            order.land(*range(1, blocks))
        else:
            order.land(name)
    halves = order.result("three")
    last_half = halves[0].shape[0]
    plan = [
        (0, n // last_half, n % last_half, n // cb, None, n % cb) for n in range(3 * cb + 1)
    ]
    shapes = [(width, width)] * 3 + [(width, LANES)]
    query_total, key_total, value_total, small = place(
        core, [halves], plan, shapes
    )
    flat_small = small[: (8 + steps) * cb].reshape(-1, width)
    table_rows = small[(8 + steps) * cb : (8 + steps) * cb + heads * TABLE_ROWS // LANES]
    table_total = jnp.concatenate(
        [table_rows[i : i + heads] for i in range(0, table_rows.shape[0], heads)], axis=1
    )[:, :buckets].T
    return (
        mixed.reshape(frames.shape),
        frames_grad.reshape(frames.shape),
        query_total,
        key_total,
        value_total,
        output_total,
        up_total,
        down_total.reshape(units, width),
        flat_small[0],
        flat_small[1],
        flat_small[2],
        flat_small[3],
        flat_small[6],
        flat_small[4],
        flat_small[5],
        flat_small[8:].reshape(units),
        flat_small[7],
        table_total,
    )


def solution(mesh):
    batch3 = P("batch", "blk", None)
    in_specs = (batch3, batch3) + (P(),) * 16 + (P("batch", None), P("batch", "blk"), P())
    out_specs = (batch3, batch3) + (P(),) * 16
    return jax.shard_map(
        per_device, mesh=mesh, in_specs=in_specs, out_specs=out_specs, check_vma=False
    )
```

```python
import functools

import jax
import jax.numpy as jnp
from jax import lax
from jax.experimental import pallas as pl
from jax.experimental.pallas import tpu as pltpu
from jax.sharding import PartitionSpec as P

HD = 64
LANES = 128
EPSILON = 1e-05
MASKED = -1e30
BF16 = jnp.bfloat16
F32 = jnp.float32
COST = 1
SHORT, LONG = 0.05, 1000
LANDINGS = (
    "one", "two", "three", "one", "two", "one", "three", "one", "two", "send_peers", "one",
    "three", "two", "three", "one", "two", "peers", "frames", "three", "one", "two", "three",
    "one", "two", "three", "three", "two", "two", "place", "three", "three",
)
HIGHEST = lax.Precision.HIGHEST


def dot_nn(a, b):
    return lax.dot_general(a, b, (((1,), (0,)), ((), ())), preferred_element_type=F32)


def dot_nt(a, b):
    return lax.dot_general(a, b, (((1,), (1,)), ((), ())), preferred_element_type=F32)


def dot_tn(a, b):
    return lax.dot_general(a, b, (((0,), (0,)), ((), ())), preferred_element_type=F32)


def normalise(values):
    centre = values - jnp.mean(values, axis=-1, keepdims=True)
    scale = lax.rsqrt(jnp.mean(centre * centre, axis=-1, keepdims=True) + EPSILON)
    return centre * scale, scale


def column_sum(values):
    return jnp.sum(values, axis=0, keepdims=True)


def cost_of(time):
    return pl.CostEstimate(
        flops=int(time * COST * 1.1e9), bytes_accessed=int(time * COST * 3e6), transcendentals=0
    )


def call(kernel, out_shape, time, after=(), vmem=32, **kw):
    skip = len(after)

    def run(*refs):
        kernel(*refs[skip:])

    kw["in_specs"] = [pl.BlockSpec(memory_space=pl.ANY)] * skip + list(kw["in_specs"])
    program = pl.pallas_call(
        run,
        out_shape=out_shape,
        compiler_params=pltpu.CompilerParams(vmem_limit_bytes=vmem * 1024 * 1024),
        cost_estimate=cost_of(time),
        **kw,
    )
    return lambda *arrays: program(*after, *arrays)


SMEM = pl.BlockSpec(memory_space=pltpu.SMEM)
IN_VMEM = pl.BlockSpec(memory_space=pltpu.VMEM)


def shaped(shape, dtype):
    return jax.ShapeDtypeStruct(shape, dtype)


def row(ref):
    return ref[...].reshape(1, ref.shape[0])


def store_pairs(ref, values):
    for p in range(values.shape[1] // LANES):
        ref[p] = values[:, p * LANES : (p + 1) * LANES].astype(ref.dtype)


def all_pairs(refs):
    return jnp.concatenate([ref[p] for ref in refs for p in range(ref.shape[0])], axis=1)


def project_kernel(own, where, *refs):
    refs = list(refs)
    info_ref, lengths_ref, x_ref, gain_ref, shift_ref, mask_ref, bucket_ref, table_ref = refs[:8]
    refs = refs[8:]
    if own:
        bq_ref = refs.pop(0)
    bv_ref = refs.pop(0)
    if own:
        wq_ref, wk_ref, wv_ref, n_ref, kf_ref, win_ref, qf_ref, q_ref, k_ref, v_ref, norm = refs
    else:
        wk_ref, wv_ref, n_ref, kf_ref, win_ref, k_ref, v_ref, norm = refs
    rows_n, length, _ = kf_ref.shape

    @pl.when(pl.program_id(0) == 0)
    def _():
        y, _ = normalise(x_ref[...].astype(F32))
        norm[...] = (y * row(gain_ref) + row(shift_ref)).astype(BF16)
        n_ref[...] = norm[...]
        count = lengths_ref.shape[1]
        lane_row = lax.broadcasted_iota(jnp.int32, (1, LANES), 1)
        lane = lax.broadcasted_iota(jnp.int32, (length, LANES), 1)
        pos = info_ref[2 * where] + lax.broadcasted_iota(jnp.int32, (length, LANES), 0)
        for r in range(rows_n):
            end = jnp.int32(0)
            begins = jnp.zeros((1, LANES), jnp.int32)
            ends = jnp.zeros((1, LANES), jnp.int32)
            for u in range(count):
                begin, end = end, end + lengths_ref[r, u]
                begins = jnp.where(lane_row == u, begin, begins)
                ends = jnp.where(lane_row == u, end, ends)
            inside = (pos >= begins) & (pos < ends)
            seen = jnp.broadcast_to(mask_ref[r : r + 1, :].astype(F32), (LANES, length)).T > 0.5
            free = (lane >= count) | (inside & seen)
            kf_ref[r] = jnp.where(free, 0.0, MASKED).astype(BF16)
            if own:
                qf_ref[r] = jnp.where(inside, 1.0, 0.0).astype(BF16)
        buckets = table_ref.shape[1]
        at = pl.multiple_of(info_ref[2 * where + 1], LANES)
        window = bucket_ref[:, pl.ds(at, 2 * length)]
        one_hot = jnp.where(
            lax.broadcasted_iota(jnp.int32, (buckets, 2 * length), 0) == window, 1.0, 0.0
        ).astype(BF16)
        rest = table_ref[...]
        bias = None
        for _ in range(3):
            part = rest.astype(BF16)
            rest = rest - part.astype(F32)
            product = dot_nn(part, one_hot)
            bias = product if bias is None else bias + product
        for p in range(win_ref.shape[0]):
            win_ref[p] = bias[2 * p : 2 * p + 2]

    x = norm[...]
    if own:
        store_pairs(q_ref, (dot_nn(x, wq_ref[...]) + row(bq_ref)) * 0.125)
    store_pairs(k_ref, dot_nn(x, wk_ref[...]))
    store_pairs(v_ref, dot_nn(x, wv_ref[...]) + row(bv_ref))


def project(info, lengths, x, norm, mask, bucket, table, weights, biases, where, after=()):
    rows, width = x.shape
    rows_n, length = mask.shape
    pairs = table.shape[0] // 2
    cols = 256
    own = len(weights) == 3
    whole = pl.BlockSpec((rows, width), lambda j: (0, 0))
    part = pl.BlockSpec((width, cols), lambda j: (0, j))
    out = pl.BlockSpec((cols // LANES, rows, LANES), lambda j: (j, 0, 0))
    feat = pl.BlockSpec((rows_n, length, LANES), lambda j: (0, 0, 0))

    def fixed(array):
        return pl.BlockSpec(array.shape, lambda j: (0,) * array.ndim)

    count = len(weights)
    features = shaped((rows_n, length, LANES), BF16)
    window = shaped((pairs, 2, 2 * length), F32)
    return call(
        functools.partial(project_kernel, own, where),
        [shaped((rows, width), BF16), features, window]
        + [features] * own
        + [shaped((pairs, rows, LANES), BF16)] * count,
        5,
        after=after,
        vmem=56,
        grid=(width // cols,),
        in_specs=[SMEM, SMEM, whole, fixed(norm[0]), fixed(norm[1])]
        + [fixed(mask), fixed(bucket), fixed(table)]
        + [pl.BlockSpec((cols,), lambda j: (j,))] * len(biases)
        + [part] * count,
        out_specs=[whole, feat, fixed(window)] + [feat] * own + [out] * count,
        scratch_shapes=[pltpu.VMEM((rows, width), BF16)],
    )(info, lengths, x, *norm, mask, bucket, table, *biases, *weights)


def rows_of_head(h):
    return slice(h * HD, (h + 1) * HD)


def attend_kernel(own, last, chunk, *refs):
    refs = list(refs)
    q_ref, k_ref, v_ref, qf_ref, kf_ref, w_ref = refs[:6]
    refs = refs[6:]
    if not own:
        o_in, stats_in = refs[:2]
        refs = refs[2:]
    p_ref, m_ref, o_ref, stats_ref = refs[:4]
    cx_ref = refs[4] if last else None
    t_refs = refs[-2:]
    length = q_ref.shape[0]
    nb = length // LANES
    q = q_ref[...]
    k = k_ref[...]
    lane = lax.broadcasted_iota(jnp.int32, (length, LANES), 1)
    k_wide = jnp.concatenate([k, kf_ref[...]], axis=1)
    v_flip = v_ref[...].T
    ones = jnp.ones((16, length), BF16)
    eye = lax.broadcasted_iota(jnp.int32, (LANES, LANES), 0) == lax.broadcasted_iota(
        jnp.int32, (LANES, LANES), 1
    )
    zero = jnp.zeros((), BF16)
    for h in range(2):
        t_ref = t_refs[h]
        for a in range(2 * nb - 1):
            x = w_ref[h : h + 1, 2 * length - 256 - 128 * a : 2 * length - 128 * a]
            t = pltpu.roll(jnp.broadcast_to(x, (LANES, 256)), 0, 1, stride=1, stride_axis=0)
            t_ref[128 * a : 128 * a + 128, :] = t[:, LANES:]
        q_head = jnp.where((lane < HD) == (h == 0), q, zero)
        q_wide = jnp.concatenate([q_head, qf_ref[...]], axis=1)
        v_head = jnp.concatenate([v_flip[rows_of_head(h)], ones], axis=0)
        sums, tops = [], []
        for c in range(0, length, chunk):
            s = dot_nt(k_wide, q_wide[c : c + chunk])
            weights = []
            for i in range(c // LANES, (c + chunk) // LANES):
                first = 128 * (nb - 1 - i)
                here = slice(128 * i, 128 * i + 128)
                tile = s[:, 128 * i - c : 128 * i - c + 128] + t_ref[first : first + length, :]
                if own:
                    plain = dot_nt(k[here], q_head[here]) + t_ref[128 * (nb - 1) : 128 * nb, :]
                    fixed = jnp.where(eye, plain, tile[here])
                    around = [tile[: 128 * i], fixed, tile[128 * i + 128 :]]
                    tile = jnp.concatenate([x for x in around if x.shape[0]], axis=0)
                top = jnp.max(tile, axis=0, keepdims=True)
                weight = jnp.exp(tile - top).astype(BF16)
                p_ref[h, :, here] = weight
                weights.append(weight)
                tops.append(top)
            sums.append(dot_nn(v_head, jnp.concatenate(weights, axis=1)))
        o = jnp.concatenate(sums, axis=1)
        m = jnp.concatenate(tops, axis=1)
        o, l = o[:HD], o[HD : HD + 1]
        m_ref[h : h + 1, :] = m
        if not own:
            m_old = stats_in[h : h + 1, :]
            m_new = jnp.maximum(m_old, m)
            old, new = jnp.exp(m_old - m_new), jnp.exp(m - m_new)
            o = o_in[rows_of_head(h), :] * old + o * new
            l = stats_in[2 + h : 3 + h, :] * old + l * new
            m = m_new
        if last:
            o = o / l
            m = m + jnp.log(l)
        o_ref[rows_of_head(h), :] = o
        stats_ref[h : h + 1, :] = m
        stats_ref[2 + h : 3 + h, :] = l
    if last:
        cx_ref[...] = o_ref[...].T.astype(BF16)


def attend(q, k, v, qf, kf, window, state, last, chunk=256):
    pairs, rows, length, _ = q.shape
    nb = length // LANES
    own = state is None

    def spec(*shape):
        return pl.BlockSpec((pl.squeezed, pl.squeezed, *shape), lambda p, r: (p, r) + (0,) * len(shape))

    blk, flip, stats = spec(length, LANES), spec(LANES, length), spec(8, length)
    feat = pl.BlockSpec((pl.squeezed, length, LANES), lambda p, r: (r, 0, 0))
    stats_shape = shaped((pairs, rows, 8, length), F32)
    outs = [
        shaped((pairs, rows, 2, length, length), BF16),
        stats_shape,
        shaped((pairs, rows, LANES, length), F32),
        stats_shape,
    ] + [shaped((pairs, rows, length, LANES), BF16)] * last
    return call(
        functools.partial(attend_kernel, own, last, min(chunk, length)),
        outs,
        12,
        vmem=56,
        grid=(pairs, rows),
        in_specs=[blk] * 3
        + [feat] * 2
        + [pl.BlockSpec((pl.squeezed, 2, 2 * length), lambda p, r: (p, 0, 0))]
        + ([] if own else [flip, stats]),
        out_specs=[spec(2, length, length), stats, flip, stats] + [blk] * last,
        scratch_shapes=[pltpu.VMEM(((2 * nb - 1) * LANES, LANES), F32)] * 2,
    )(q, k, v, qf, kf, window, *([] if own else state))


def diagonal_sums(ds_ref, nb, lane8):
    length = nb * LANES
    tops, lows = [], []
    for a in range(2 * nb - 1):
        total = None
        for j in range(nb):
            i0 = 128 * (a - (nb - 1) + j)
            if 0 <= i0 < length:
                x = ds_ref[i0 : i0 + 128, 128 * j : 128 * j + 128].astype(F32)
                total = x if total is None else total + x
        whole, top = total[:8], total[:8]
        for g in range(1, 16):
            x = pltpu.roll(total[8 * g : 8 * g + 8], 128 - 8 * g, 1)
            whole = whole + x
            top = top + jnp.where(lane8 < 128 - 8 * g, x, 0.0)
        tops.append(top)
        lows.append(whole - top)
    pieces = []
    for g in range(2 * nb):
        a = 2 * nb - 1 - g
        if a == 2 * nb - 1:
            pieces.append(lows[a - 1])
        elif a == 0:
            pieces.append(tops[a])
        else:
            pieces.append(tops[a] + lows[a - 1])
    z = jnp.concatenate(pieces, axis=1)
    sub = lax.broadcasted_iota(jnp.int32, z.shape, 0)
    for bit in (1, 2, 4):
        z = jnp.where((sub & bit) != 0, pltpu.roll(z, 2 * length - bit, 1), z)
    return column_sum(z)


def attend_back_kernel(first, last, *refs):
    refs = list(refs)
    p_ref, q_ref, k_ref, v_ref, dc_ref, dot_ref, lse_ref, m_ref = refs[:8]
    refs = refs[8:]
    dq_in = None if first else refs.pop(0)
    dq_ref, dk_ref, dv_ref, w_ref, ds_ref, dq_flip = refs
    length = q_ref.shape[0]
    nb = length // LANES
    q, k, v = q_ref[...], k_ref[...], v_ref[...]
    lane = lax.broadcasted_iota(jnp.int32, (length, LANES), 1)
    line = lax.broadcasted_iota(jnp.int32, (LANES, length), 0)
    lane8 = lax.broadcasted_iota(jnp.int32, (8, LANES), 1)
    low = lane < HD
    zero = jnp.zeros((), BF16)
    k_flip = k.T
    v_wide = jnp.concatenate([v, jnp.where(lane < 2, -1.0, 0.0).astype(BF16)], axis=1)
    scaled, dots = [], []
    for h in range(2):
        factor = jnp.exp(m_ref[h : h + 1, :] - lse_ref[h : h + 1, :])
        scaled.append((dc_ref[rows_of_head(h), :].astype(F32) * factor).astype(BF16))
        dots.append(dot_ref[h : h + 1, :] * factor)
    do_flip = jnp.concatenate(scaled, axis=0)
    do = do_flip.T
    row = pl.program_id(1)
    parts = []
    for h in range(2):
        dot_hi = dots[h].astype(BF16)
        dot_lo = (dots[h] - dot_hi.astype(F32)).astype(BF16)
        feat = jnp.where(line == 0, dot_hi, jnp.where(line == 1, dot_lo, zero))
        mine = jnp.where((line < HD) == (h == 0), do_flip, zero)
        p = p_ref[h]
        dp = dot_nn(v_wide, jnp.concatenate([mine, feat], axis=0))
        ds = (p.astype(F32) * dp).astype(BF16)
        ds_ref[h] = ds
        parts.append((dot_nn(ds, q), dot_nn(p, do)))
        dq = dot_nn(k_flip[rows_of_head(h)], ds)
        dq_flip[rows_of_head(h), :] = dq if first else dq + dq_in[rows_of_head(h), :]
        diagonal = diagonal_sums(ds_ref.at[h], nb, lane8)

        @pl.when(row == 0)
        def _():
            w_ref[h : h + 1, :] = diagonal

        @pl.when(row != 0)
        def _():
            w_ref[h : h + 1, :] += diagonal

    dk, dv = [jnp.where(low, one, two) for one, two in zip(*parts)]
    dq_ref[...] = dq_flip[...].T.astype(BF16) if last else dq_flip[...]
    dk_ref[...] = dk.astype(BF16)
    dv_ref[...] = dv.astype(BF16)


def attend_back(p, q, k, v, dctx, dots, lse, m, dq, last, start, count, after=()):
    _, rows, length, _ = q.shape
    first = dq is None

    def spec(*shape, start=start):
        return pl.BlockSpec(
            (pl.squeezed, pl.squeezed, *shape), lambda p, r: (p + start, r) + (0,) * len(shape)
        )

    blk, flip, stats = spec(length, LANES), spec(LANES, length), spec(8, length)
    out, out_flip = spec(length, LANES, start=0), spec(LANES, length, start=0)
    arrays = [p, q, k, v, dctx, dots, lse, m] + ([] if first else [dq])
    natural = shaped((count, rows, length, LANES), BF16)
    return call(
        functools.partial(attend_back_kernel, first, last),
        [
            natural if last else shaped((count, rows, LANES, length), F32),
            natural,
            natural,
            shaped((count, 2, 2 * length), F32),
        ],
        LONG if first and start == 0 else SHORT,
        after=after,
        grid=(count, rows),
        in_specs=[spec(2, length, length)]
        + [blk] * 3
        + [flip]
        + [stats] * 3
        + ([] if first else [out_flip]),
        out_specs=[out if last else out_flip, out, out]
        + [pl.BlockSpec((pl.squeezed, 2, 2 * length), lambda p, r: (p, 0, 0))],
        scratch_shapes=[
            pltpu.VMEM((2, length, length), BF16),
            pltpu.VMEM((LANES, length), F32),
        ],
    )(*arrays)


def ffn_kernel(head, *refs):
    core_ref, bo_ref, gain_ref, shift_ref, bd_ref = refs[:5]
    cot_ref, up_ref, down_ref, bias_ref, ctx_in, wo_in = refs[5:11]
    refs = refs[11:]
    if head:
        x_ref, res_out, hid_out, down_acc, hid_acc, keep_out, send_out, bias_grad = refs[:8]
        res_ref, hid_ref, keep_ref, send_ref, sems, more_sems = refs[8:]
        ctx_ref, wo_ref = ctx_in, wo_in
        later = [(res_ref, res_out), (hid_ref, hid_out)]
    else:
        hid_ref, down_in, hid_in, res_in, at_in = refs[:5]
        mixed_ref, dres_ref, dctx_ref, dots_ref, sums_ref = refs[5:10]
        keep_out, send_out, bias_grad, keep_ref, send_ref, sems, more_sems = refs[10:17]
        ctx_ref, wo_ref, down_first, hid_first, res_ref, at_ref, down_acc, hid_acc = refs[17:]
        early = [
            (ctx_in, ctx_ref), (wo_in, wo_ref), (down_in, down_first), (hid_in, hid_first),
            (res_in, res_ref), (at_in, at_ref),
        ]
    j = pl.program_id(0)
    steps = pl.num_programs(0)
    cb = up_ref.shape[1] // LANES

    def moves(pairs):
        return [
            pltpu.make_async_copy(src, dst, more_sems.at[i]) for i, (src, dst) in enumerate(pairs)
        ]

    def part(at, count, index):
        here = pl.ds(at, count)
        return [
            pltpu.make_async_copy(src.at[here], dst.at[here], sems.at[k, index])
            for k, (src, dst) in enumerate(((keep_ref, keep_out), (send_ref, send_out)))
        ]

    @pl.when(j == 0)
    def _():
        down_acc[...] = jnp.zeros_like(down_acc)
        hid_acc[...] = jnp.zeros_like(hid_acc)
        if head:
            res = x_ref[...].astype(F32) + (
                dot_nn(all_pairs([ctx_ref]), wo_ref[...]) + row(bo_ref)
            )
            res_ref[...] = res
            y, _ = normalise(res)
            hid_ref[...] = (y * row(gain_ref) + row(shift_ref)).astype(BF16)
        for copy in moves(later if head else early):
            copy.start()

    hid, cot = hid_ref[...], cot_ref[...]
    up, down = up_ref[...], down_ref[...]
    pre = dot_nn(hid, up) + bias_ref[0]
    cdf = 0.5 + 0.5 * lax.erf(pre * 0.7071067811865476)
    slope = cdf + pre * (0.3989422804014327 * jnp.exp(-0.5 * pre * pre))
    act = (pre * cdf).astype(BF16)
    pre_grad = (dot_nt(cot, down) * slope).astype(BF16)
    up_grad = dot_tn(hid, pre_grad).astype(BF16)
    down_grad = dot_tn(act, cot).astype(BF16)

    for core in range(2):

        @pl.when(core_ref[0] == core)
        def _():
            for c in range(cb):
                cols = slice(c * LANES, (c + 1) * LANES)
                (keep_ref, send_ref)[core][j * cb + c] = up_grad[:, cols]
                (send_ref, keep_ref)[core][j * cb + c] = down_grad[:, cols]

    for copy in part(j * cb, cb, j):
        copy.start()
    down_acc[...] += dot_nn(act, down)
    hid_acc[...] += dot_nt(pre_grad, up)
    bias_grad[0] = column_sum(pre_grad.astype(F32))

    @pl.when(j == steps - 1)
    def _():
        if head:
            for copy in moves(later):
                copy.wait()
        else:
            for copy in moves(early):
                copy.wait()
            res = res_ref[...]
            cot = cot_ref[...].astype(F32)
            down_sum = down_first[...] + down_acc[...]
            mixed_ref[...] = (res + (down_sum + row(bd_ref))).astype(BF16)
            y, scale = normalise(res)
            dh = hid_first[...] + hid_acc[...]
            a = dh * row(gain_ref)
            dres = cot + scale * (
                a
                - jnp.mean(a, axis=-1, keepdims=True)
                - y * jnp.mean(a * y, axis=-1, keepdims=True)
            )
            dres_ref[...] = dres
            branch = dres.astype(BF16)
            out_grad = dot_tn(all_pairs([ctx_ref]), branch).astype(BF16)
            first, own = 2 * cb, cb // 2
            for core in range(2):

                @pl.when(core_ref[0] == core)
                def _():
                    for c in range(own):
                        low = out_grad[:, c * LANES : (c + 1) * LANES]
                        high = out_grad[:, (own + c) * LANES : (own + c + 1) * LANES]
                        (keep_ref, send_ref)[core][first + c] = low
                        (send_ref, keep_ref)[core][first + c] = high

            for copy in part(first, own, sems.shape[1] - 1):
                copy.start()
            dots_ref[...] = jnp.zeros_like(dots_ref)
            for p in range(dctx_ref.shape[0]):
                grad = dot_nt(wo_ref[p * LANES : (p + 1) * LANES, :], branch).astype(BF16)
                dctx_ref[p] = grad
                product = grad.astype(F32) * at_ref[p]
                for h in range(2):
                    dots_ref[p, h : h + 1, :] = column_sum(product[rows_of_head(h)])
            sums_ref[0:1] = column_sum(dh * y)
            sums_ref[1:2] = column_sum(dh)
            sums_ref[2:3] = column_sum(branch.astype(F32))
            sums_ref[3:4] = column_sum(cot)
            for copy in part(first, own, sems.shape[1] - 1):
                copy.wait()
        for k in range(keep_ref.shape[0] // cb):
            for copy in part(k * cb, cb, k):
                copy.wait()


def ffn(core, vectors, cot, up, down, bias, ctx, wo, start, steps, head=None, tail=None,
        after=()):
    rows, width = cot.shape
    once = pl.Buffered(1)
    whole = pl.BlockSpec((rows, width), lambda j: (0, 0), pipeline_mode=once)
    square = pl.BlockSpec((width, width), lambda j: (0, 0), pipeline_mode=once)
    vecs = pl.BlockSpec((8, width), lambda j: (0, 0))
    anywhere = pl.BlockSpec(memory_space=pl.ANY)
    cb = width // LANES

    def pairs(*shape):
        return pl.BlockSpec((cb, *shape), lambda j: (0, 0, 0), pipeline_mode=once)

    full, half = shaped((rows, width), F32), shaped((rows, width), BF16)
    wide, thin = pltpu.VMEM((rows, width), F32), pltpu.VMEM((rows, width), BF16)
    if head is not None:
        count = steps * cb
        outs, out_specs = [full, half, full, full], [anywhere] * 2 + [whole] * 2
        extra, extra_specs = list(head), [whole]
    else:
        count = steps * cb + cb // 2
        outs = [
            half, full, shaped((cb, LANES, rows), BF16), shaped((cb, 8, rows), F32),
            shaped((8, width), F32),
        ]
        out_specs = [whole, whole, pairs(LANES, rows), pairs(8, rows), vecs]
        extra, extra_specs = list(tail), [whole] + [anywhere] * 4
    grads = pltpu.VMEM((count, width, LANES), BF16)
    sems = [pltpu.SemaphoreType.DMA((2, steps + (head is None)))]
    sems += [pltpu.SemaphoreType.DMA((2 if head is not None else 6,))]
    if head is not None:
        scratch = [wide, thin, grads, grads, *sems]
    else:
        scratch = [grads, grads, *sems, pltpu.VMEM((cb, rows, LANES), BF16)]
        scratch += [pltpu.VMEM((width, width), BF16), wide, wide, wide]
        scratch += [pltpu.VMEM((cb, LANES, rows), F32), wide, wide]
    return call(
        functools.partial(ffn_kernel, head is not None),
        outs + [shaped((count, width, LANES), BF16)] * 2 + [shaped((steps, 1, width), F32)],
        30,
        after=after,
        vmem=56,
        grid=(steps,),
        in_specs=[
            SMEM,
            *[pl.BlockSpec((width,), lambda j: (0,))] * len(vectors),
            whole,
            pl.BlockSpec((width, width), lambda j: (0, j + start)),
            pl.BlockSpec((width, width), lambda j: (j + start, 0)),
            pl.BlockSpec((1, 1, width), lambda j: (j + start, 0, 0)),
            pairs(rows, LANES) if head is not None else anywhere,
            square if head is not None else anywhere,
        ]
        + extra_specs,
        out_specs=out_specs
        + [anywhere] * 2
        + [pl.BlockSpec((1, 1, width), lambda j: (j, 0, 0))],
        scratch_shapes=scratch,
    )(core, *vectors, cot, up, down, bias, ctx, wo, *extra)


class Shared:
    def __init__(self, core_ref, keep_ref, send_ref):
        self.core_ref, self.refs, self.count = core_ref, (keep_ref, send_ref), 0

    def store(self, values):
        half = self.refs[0].shape[0]
        values = values.astype(BF16)
        for c in range(values.shape[1] // LANES):
            block = values[:, c * LANES : (c + 1) * LANES]
            owner, at = divmod(self.count, half)
            self.count += 1

            @pl.when(self.core_ref[0] == owner)
            def _():
                self.refs[0][at] = block

            @pl.when(self.core_ref[0] != owner)
            def _():
                self.refs[1][at] = block


def project_back_kernel(blocks, calls, *refs):
    refs = list(refs)

    def take(count):
        taken = refs[:count]
        del refs[:count]
        return taken

    core_ref, info_ref, bucket_ref, vec_ffn, *bias_grads = take(6)
    peer_sums = take(blocks - 1)
    n_refs, (x_ref,) = take(blocks), take(1)
    wq_ref, wk_ref, wv_ref = take(3)
    dq_refs = take(calls)
    dk_refs, dv_refs, w_refs = [[take(calls) for _ in range(blocks)] for _ in range(3)]
    (ng_ref,) = take(1)
    keep_ref, send_ref, small_ref = take(3)
    grads = Shared(core_ref, keep_ref, send_ref)
    dq = all_pairs(dq_refs)
    gk = gv = bias = None
    for b in range(blocks):
        dk, dv, norm = all_pairs(dk_refs[b]), all_pairs(dv_refs[b]), n_refs[b][...]
        if b == 0:
            ng = 0.125 * dot_nt(dq, wq_ref[...])
            ng = ng + dot_nt(dk, wk_ref[...]) + dot_nt(dv, wv_ref[...])
            grads.store(0.125 * dot_tn(norm, dq))
            ng_ref[...] = ng
            y, _ = normalise(x_ref[...].astype(F32))
            sums = [column_sum(ng * y), column_sum(ng)]
        k_part, v_part, b_part = dot_tn(norm, dk), dot_tn(norm, dv), column_sum(dv.astype(F32))
        gk = k_part if gk is None else gk + k_part
        gv = v_part if gv is None else gv + v_part
        bias = b_part if bias is None else bias + b_part
    for peer in peer_sums:
        sums = [mine + peer[i : i + 1] for i, mine in enumerate(sums)]
    grads.store(gk)
    grads.store(gv)
    small_ref[...] = jnp.zeros_like(small_ref)
    vectors = sums + [0.125 * column_sum(dq.astype(F32)), bias]
    vectors += [vec_ffn[i : i + 1] for i in range(4)]
    vectors += [ref[i] for ref in bias_grads for i in range(ref.shape[0])]
    at = 0
    for vec in vectors:
        for c in range(vec.shape[1] // LANES):
            small_ref[at : at + 1, :] = vec[:, c * LANES : (c + 1) * LANES]
            at += 1
    table = None
    span = w_refs[0][0].shape[2]
    for b in range(blocks):
        start = pl.multiple_of(info_ref[2 * b + 1], LANES)
        window = bucket_ref[:, pl.ds(start, span)]
        one_hot = jnp.where(
            lax.broadcasted_iota(jnp.int32, (TABLE_ROWS, span), 0) == window, 1.0, 0.0
        ).astype(BF16)
        w = jnp.concatenate([ref[p] for ref in w_refs[b] for p in range(ref.shape[0])], axis=0)
        w_hi = w.astype(BF16)
        w_lo = (w - w_hi.astype(F32)).astype(BF16)
        part = dot_nt(w_hi, one_hot) + dot_nt(w_lo, one_hot)
        table = part if table is None else table + part
    for c in range(TABLE_ROWS // LANES):
        small_ref[at : at + table.shape[0], :] = table[:, c * LANES : (c + 1) * LANES]
        at += table.shape[0]
    grads.store(small_ref[...])
    while grads.count < 2 * keep_ref.shape[0]:
        grads.store(jnp.zeros_like(small_ref))


TABLE_ROWS = 384


def project_back(core, info, bucket, vec_ffn, bias_grads, peer_sums, norms, x, weights, parts,
                 after=()):
    rows, width = norms[0].shape
    blocks = len(norms)
    whole = pl.BlockSpec(memory_space=pltpu.VMEM)
    arrays = [core, info, bucket, vec_ffn, *bias_grads, *peer_sums, *norms, x, *weights]
    arrays += [part[0].reshape(-1, rows, LANES) for part in parts[0]]
    for kind in (1, 2):
        arrays += [part[kind].reshape(-1, rows, LANES) for block in parts for part in block]
    arrays += [part[3] for block in parts for part in block]
    count = 3 * width // LANES + 1
    count += count % 2
    ng, *grads = call(
        functools.partial(project_back_kernel, blocks, len(parts[0])),
        [shaped((rows, width), F32)] + [shaped((count // 2, width, LANES), BF16)] * 2,
        SHORT,
        after=after,
        grid=(1,),
        in_specs=[SMEM, SMEM] + [whole] * (len(arrays) - 2),
        scratch_shapes=[pltpu.VMEM((width, LANES), F32)],
    )(*arrays)
    return ng, grads


def peer_back_kernel(calls, *refs):
    x_ref, wk_ref, wv_ref = refs[:3]
    dk_refs, dv_refs = refs[3 : 3 + calls], refs[3 + calls : 3 + 2 * calls]
    ng_ref, sums_ref = refs[3 + 2 * calls :]
    dk, dv = all_pairs(dk_refs), all_pairs(dv_refs)
    ng = dot_nt(dk, wk_ref[...]) + dot_nt(dv, wv_ref[...])
    ng_ref[...] = ng.astype(BF16)
    y, _ = normalise(x_ref[...].astype(F32))
    sums_ref[0:1] = column_sum(ng * y)
    sums_ref[1:2] = column_sum(ng)


def peer_back(x, weights, parts, after=()):
    rows, width = x.shape
    arrays = [x, *weights[1:]]
    for kind in (1, 2):
        arrays += [part[kind].reshape(-1, rows, LANES) for part in parts]
    return call(
        functools.partial(peer_back_kernel, len(parts)),
        [shaped((rows, width), BF16), shaped((8, width), F32)],
        SHORT,
        after=after,
        grid=(1,),
        in_specs=[IN_VMEM] * len(arrays),
    )(*arrays)


def frames_back_kernel(count, *refs):
    x_ref, gain_ref, dres_ref, ng_ref = refs[:4]
    out_ref = refs[-1]
    y, scale = normalise(x_ref[...].astype(F32))
    ng = ng_ref[...]
    for other in refs[4 : 4 + count]:
        ng = ng + other[...].astype(F32)
    a = ng * row(gain_ref)
    out_ref[...] = dres_ref[...] + scale * (
        a - jnp.mean(a, axis=-1, keepdims=True) - y * jnp.mean(a * y, axis=-1, keepdims=True)
    )


def frames_back(x, gain, dres, ng, others, after=()):
    rows, width = x.shape
    tile = 128
    blk = pl.BlockSpec((tile, width), lambda i: (i, 0))
    vec = pl.BlockSpec((width,), lambda i: (0,))
    return call(
        functools.partial(frames_back_kernel, len(others)),
        shaped((rows, width), F32),
        4,
        after=after,
        grid=(rows // tile,),
        in_specs=[blk, vec, blk, blk] + [blk] * len(others),
        out_specs=blk,
    )(x, gain, dres, ng, *others)


def swap(x, bit):
    axis, mask = bit
    if isinstance(mask, int):
        mask = [(i, i ^ mask) for i in range(lax.axis_size(axis))]
    return lax.ppermute(x, axis, mask)


def side(bit):
    axis, mask = bit
    return ((lax.axis_index(axis) & mask) != 0).astype(jnp.int32)


CORE, ALONG, NEAR, FAR, ACROSS = ("batch", 1), ("batch", 2), ("batch", 4), ("batch", 8), ("blk", 1)

def local(kernel, sides, arrays, shapes, time=1.0):
    return pl.pallas_call(
        kernel,
        out_shape=[shaped(shape, BF16) for shape in shapes],
        in_specs=[SMEM] + [IN_VMEM] * len(arrays),
        out_specs=[IN_VMEM] * len(shapes),
        compiler_params=pltpu.CompilerParams(vmem_limit_bytes=4 * 1024 * 1024),
        cost_estimate=cost_of(time),
    )(sides, *arrays)


def both_halves(size, at):
    return [pl.ds(pl.multiple_of(k * size, 16), size) for k in (1 - at, at)]


def add(a, b):
    return (a.astype(F32) + b.astype(F32)).astype(BF16)


def sum_over_devices(keep, send, time):
    n, rows, _ = keep.shape
    count_a = n // 2
    count_b = n - count_a
    halves = (slice(0, count_a), slice(count_a, n))
    x, y, z, w = range(4)
    sides = jnp.stack([side(bit) for bit in (ACROSS, ALONG, NEAR, FAR)])
    (got,) = yield [(send, CORE)]

    def first(s, keep, got, send_a, keep_a, send_b, keep_b):
        for k, bit, outs in ((0, x, (send_a, keep_a)), (1, y, (send_b, keep_b))):
            block = halves[k]
            for rows_at, out in zip(both_halves(rows // 2, s[bit]), outs):
                out[...] = add(keep[block, rows_at, :], got[block, rows_at, :])

    def shapes(size):
        return [(count_a, size, LANES), (count_b, size, LANES)]

    send_a, keep_a, send_b, keep_b = local(
        first, sides, [keep, got], [x for x in shapes(rows // 2) for _ in range(2)]
    )
    got_a, got_b = yield [(send_a, ACROSS), (send_b, ALONG)]

    def second(s, keep_a, got_a, keep_b, got_b, *outs):
        for k, bit, keep, got in ((0, y, keep_a, got_a), (1, x, keep_b, got_b)):
            for rows_at, out in zip(both_halves(rows // 4, s[bit]), outs[2 * k : 2 * k + 2]):
                out[...] = add(keep[:, rows_at, :], got[:, rows_at, :])

    send_a, keep_a, send_b, keep_b = local(
        second,
        sides,
        [keep_a, got_a, keep_b, got_b],
        [x for x in shapes(rows // 4) for _ in range(2)],
        time,
    )
    got_a, got_b = yield [(send_a, ALONG), (send_b, ACROSS)]

    def third(s, keep_a, got_a, keep_b, got_b, *outs):
        for k, keep, got in ((0, keep_a, got_a), (1, keep_b, got_b)):
            for rows_at, out in zip(both_halves(rows // 8, s[z]), outs):
                out[halves[k]] = add(keep[:, rows_at, :], got[:, rows_at, :])

    shape = (n, rows // 8, LANES)
    send, keep = local(third, sides, [keep_a, got_a, keep_b, got_b], [shape] * 2)
    (got,) = yield [(send, NEAR)]

    def fourth(s, keep, got, *outs):
        for rows_at, out in zip(both_halves(rows // 16, s[w]), outs):
            out[...] = add(keep[:, rows_at, :], got[:, rows_at, :])

    shape = (n, rows // 16, LANES)
    send, keep = local(fourth, sides, [keep, got], [shape] * 2)
    (got,) = yield [(send, FAR)]

    def fifth(s, keep, got, out):
        out[...] = add(keep[...], got[...])

    (held,) = local(fifth, sides, [keep, got], [shape])
    (got,) = yield [(held, FAR)]

    def join_far(s, held, got, out):
        for rows_at, ref in zip(both_halves(rows // 16, s[w]), (got, held)):
            out[:, rows_at, :] = ref[...]

    (held,) = local(join_far, sides, [held, got], [(n, rows // 8, LANES)])
    (got,) = yield [(held, NEAR)]

    def join_near(s, held, got, *outs):
        for k, out in enumerate(outs):
            for rows_at, ref in zip(both_halves(rows // 8, s[z]), (got, held)):
                out[:, rows_at, :] = ref[halves[k]]

    held_a, held_b = local(join_near, sides, [held, got], shapes(rows // 4))
    got_a, got_b = yield [(held_a, ALONG), (held_b, ACROSS)]

    def join_second(s, held_a, got_a, held_b, got_b, *outs):
        for bit, held, got, out in ((y, held_a, got_a, outs[0]), (x, held_b, got_b, outs[1])):
            for rows_at, ref in zip(both_halves(rows // 4, s[bit]), (got, held)):
                out[:, rows_at, :] = ref[...]

    held_a, held_b = local(
        join_second, sides, [held_a, got_a, held_b, got_b], shapes(rows // 2)
    )
    got_a, got_b = yield [(held_a, ACROSS), (held_b, ALONG)]

    def join_first(s, held_a, got_a, held_b, got_b, out):
        for k, bit, held, got in ((0, x, held_a, got_a), (1, y, held_b, got_b)):
            for rows_at, ref in zip(both_halves(rows // 2, s[bit]), (got, held)):
                out[halves[k], rows_at, :] = ref[...]

    (held,) = local(join_first, sides, [held_a, got_a, held_b, got_b], [(n, rows, LANES)])
    (got,) = yield [(held, CORE)]
    return held, got


def sum_plainly(keep, send, time):
    low = side(CORE) == 0
    first, second = [
        lax.psum(jnp.where(low, *pair), ("batch", "blk")) for pair in ((keep, send), (send, keep))
    ]
    yield [(first[:1, :8], CORE)]
    return jnp.where(low, first, second), jnp.where(low, second, first)


def send_back(x, b):
    blocks = lax.axis_size("blk")
    (got,) = yield [(x, ("blk", [(i, (i + b) % blocks) for i in range(blocks)]))]
    return got


def summed(keep, send, time=1.0):
    fits = lax.axis_size("blk") == 2 and lax.axis_size("batch") == 16
    return (sum_over_devices if fits else sum_plainly)(keep, send, time)


class Flow:
    def __init__(self, steps):
        self.steps = steps
        self.result = None
        self.take(next(steps))

    def take(self, pending):
        self.arrays = [array for array, _ in pending]
        self.got = [swap(array, bit) for array, bit in pending]

    def land(self, last):
        if self.result is not None:
            return last
        *got, _ = lax.optimization_barrier([*self.got, last])
        try:
            self.take(self.steps.send(got))
            return self.arrays[0]
        except StopIteration as end:
            self.arrays, self.result = [], end.value
            return jax.tree.leaves(end.value)[0]


class Order:
    def __init__(self, last):
        self.last = last
        self.flows = {}
        self.fresh = []

    def add(self, name, steps):
        self.flows[name] = Flow(steps)
        self.fresh += self.flows[name].arrays

    def later(self, array):
        return lax.optimization_barrier((array, self.last))[0]

    def kernel(self, run):
        result = run([self.last, *self.fresh])
        self.fresh = []
        self.last = jax.tree.leaves(result)[-1]
        return result

    def land(self, *names):
        for name in names:
            self.last = self.flows[name].land(self.last)
            self.fresh += self.flows[name].arrays

    def result(self, name):
        while self.flows[name].result is None:
            self.land(name)
        return self.flows[name].result


def place_kernel(plan, tile, core_ref, *refs):
    ins = refs[: 2 * (1 + max(step[0] for step in plan))]
    outs = refs[len(ins) :]
    rows = pl.ds(pl.multiple_of(pl.program_id(0) * tile, 16), tile)
    for core in range(2):

        @pl.when(core_ref[0] == core)
        def _():
            for source, half, column, out, slot, at in plan:
                x = ins[2 * source + (half ^ core)][column, rows, :].astype(F32)
                cols = slice(at * LANES, (at + 1) * LANES)
                if slot is None:
                    outs[out][:, cols] = x
                else:
                    outs[out][slot, :, cols] = x


def place(core, sums, plan, out_shapes, after=()):
    halves = [half for pair in sums for half in pair]
    tile = 96
    out_specs = []
    for shape in out_shapes:
        if len(shape) == 2:
            out_specs.append(pl.BlockSpec((tile, shape[1]), lambda i: (i, 0)))
        else:
            out_specs.append(pl.BlockSpec((shape[0], tile, shape[2]), lambda i: (0, i, 0)))
    return call(
        functools.partial(place_kernel, plan, tile),
        [shaped(shape, F32) for shape in out_shapes],
        7,
        after=after,
        grid=(halves[0].shape[1] // tile,),
        in_specs=[SMEM] + [IN_VMEM] * len(halves),
        out_specs=out_specs,
    )(core, *halves)


def per_device(
    frames,
    cotangent,
    query_weight,
    key_weight,
    value_weight,
    output_weight,
    up_weight,
    down_weight,
    attn_gain,
    attn_shift,
    query_bias,
    value_bias,
    output_bias,
    ffn_gain,
    ffn_shift,
    up_bias,
    down_bias,
    rel_table,
    utt_lengths,
    frame_mask,
    rel_bucket,
):
    rows_n, length, width = frames.shape
    blocks = lax.axis_size("blk")
    seq = length * blocks
    me = lax.axis_index("blk")
    rows = rows_n * length
    units = up_weight.shape[1]
    steps = units // width
    heads = rel_table.shape[1]
    buckets = rel_table.shape[0]
    core = side(CORE).reshape(1)
    weights = (query_weight, key_weight, value_weight)

    def from_peer(x, b):
        return lax.ppermute(x, "blk", [((i + b) % blocks, i) for i in range(blocks)])

    def split(x):
        return x.reshape(x.shape[0], rows_n, length, x.shape[2])

    def split_flip(x):
        return jnp.swapaxes(x.reshape(*x.shape[:2], rows_n, length), 1, 2)

    def join_flip(x):
        return jnp.swapaxes(x, 1, 2).reshape(x.shape[0], x.shape[2], rows)

    def flat(x):
        return x.reshape(rows, x.shape[-1])

    flat_frames = flat(frames)
    x_blocks = [flat_frames] + [from_peer(flat_frames, b) for b in range(1, blocks)]
    masks = [frame_mask] + [from_peer(frame_mask, b) for b in range(1, blocks)]
    starts = [((me + b) % blocks) * length for b in range(blocks)]
    info = jnp.stack(
        [x for start in starts for x in (start, seq - length + starts[0] - start)]
    ).astype(jnp.int32)
    bucket = jnp.concatenate([jnp.full((1,), -1, jnp.int32), rel_bucket]).reshape(1, -1)
    norms, keys, values, probs, tops = [], [], [], [], []
    state = None
    for b in range(blocks):
        last = b == blocks - 1
        norm, key_feat, window, *rest = project(
            info, utt_lengths, x_blocks[b], (attn_gain, attn_shift), masks[b], bucket, rel_table.T,
            weights[1:] if b else weights, (value_bias,) if b else (query_bias, value_bias), b,
        )
        if b == 0:
            query_feat, query, key, value = rest
            query = split(query)
        else:
            key, value = rest
        norms.append(norm)
        keys.append(split(key))
        values.append(split(value))
        p, m, out, stats, *context = attend(
            query, keys[b], values[b], query_feat, key_feat, window, state, last
        )
        probs.append(p)
        tops.append(m)
        state = (out, stats)

    attended, lse = state
    context = context[0].reshape(heads // 2, rows, LANES)
    cot = flat(cotangent)
    dense = (
        core, (output_bias, ffn_gain, ffn_shift, down_bias), cot, up_weight, down_weight,
        up_bias.reshape(steps, 1, width), context, output_weight,
    )
    half = steps // 2
    res, hid, *carry, keep, send, bias_one = ffn(*dense, 0, half, head=(flat_frames,))
    order = Order(bias_one)
    order.add("one", summed(keep, send))
    mixed, dres, dctx, dots, vec_ffn, keep, send, bias_two = order.kernel(
        lambda after: ffn(
            *dense, half, steps - half, tail=(hid, *carry, res, join_flip(attended)), after=after
        )
    )
    order.add("two", summed(keep, send, LONG))
    order.land("one")

    dctx, dots = split_flip(dctx), split_flip(dots)
    pairs = heads // 2
    half_pairs = pairs // 2
    parts = [[] for _ in range(blocks)]
    peer_sums, peer_ngs = [], []
    dqs = [None, None]
    for b in [*range(1, blocks), 0]:
        for i in range(2):

            def run(after):
                return attend_back(
                    probs[b], query, keys[b], values[b], dctx, dots, lse, tops[b], dqs[i], b == 0,
                    i * half_pairs, (half_pairs, pairs - half_pairs)[i], after=after,
                )

            parts[b].append(order.kernel(run))
            dqs[i] = parts[b][-1][0]
            if b == 1 and i == 0:
                order.land("two")
        if b:
            ng, peer_sum = order.kernel(
                lambda after: peer_back(x_blocks[b], weights, parts[b], after=after)
            )
            peer_sums.append(peer_sum)
            peer_ngs.append(ng)
        if b == 1:
            order.land("one")
    own_ng, shared = order.kernel(
        lambda after: project_back(
            core, info, bucket, vec_ffn, (bias_one, bias_two), peer_sums, norms, flat_frames,
            weights, parts, after=after,
        )
    )
    order.add("three", summed(*shared))
    def place_frames():
        return order.kernel(
            lambda after: frames_back(
                flat_frames, attn_gain, dres, own_ng, [order.result(b) for b in range(1, blocks)],
                after=after,
            )
        )

    cb = width // LANES
    plan = []
    for chunk in range(steps):
        which, first = divmod(chunk, half)
        for c in range(cb):
            column = first * cb + c
            plan.append((which, 0, column, 0, None, chunk * cb + c))
            plan.append((which, 1, column, 1, chunk, c))
    for c in range(cb):
        plan.append((1, c // (cb // 2), 2 * cb + c % (cb // 2), 2, None, c))
    shapes = [(width, units), (steps, width, width), (width, width)]

    def place_dense():
        sums = [order.result("one"), order.result("two")]
        return order.kernel(lambda after: place(core, sums, plan, shapes, after=after))

    for name in LANDINGS:
        if name == "frames":
            frames_grad = place_frames()
        elif name == "place":
            up_total, down_total, output_total = place_dense()
        elif name == "send_peers":
            for b, ng in enumerate(peer_ngs, 1):
                order.add(b, send_back(order.later(ng), b))
        elif name == "peers":
            order.land(*range(1, blocks))
        else:
            order.land(name)
    halves = order.result("three")
    last_half = halves[0].shape[0]
    plan = [
        (0, n // last_half, n % last_half, n // cb, None, n % cb) for n in range(3 * cb + 1)
    ]
    shapes = [(width, width)] * 3 + [(width, LANES)]
    query_total, key_total, value_total, small = place(
        core, [halves], plan, shapes
    )
    flat_small = small[: (8 + steps) * cb].reshape(-1, width)
    table_rows = small[(8 + steps) * cb : (8 + steps) * cb + heads * TABLE_ROWS // LANES]
    table_total = jnp.concatenate(
        [table_rows[i : i + heads] for i in range(0, table_rows.shape[0], heads)], axis=1
    )[:, :buckets].T
    return (
        mixed.reshape(frames.shape),
        frames_grad.reshape(frames.shape),
        query_total,
        key_total,
        value_total,
        output_total,
        up_total,
        down_total.reshape(units, width),
        flat_small[0],
        flat_small[1],
        flat_small[2],
        flat_small[3],
        flat_small[6],
        flat_small[4],
        flat_small[5],
        flat_small[8:].reshape(units),
        flat_small[7],
        table_total,
    )


def solution(mesh):
    batch3 = P("batch", "blk", None)
    in_specs = (batch3, batch3) + (P(),) * 16 + (P("batch", None), P("batch", "blk"), P())
    out_specs = (batch3, batch3) + (P(),) * 16
    return jax.shard_map(
        per_device, mesh=mesh, in_specs=in_specs, out_specs=out_specs, check_vma=False
    )
```
